32 devices in a mesh: dp: 8 (over z, y), sp: 4 (over x, core).
Axes of the slice: x: 2, y: 2, z: 4, core: 2. Of those that a mesh axis runs over, the one named last changes fastest.
Arguments:
- clip_input: float32 [256, 4, 8, 7, 512], P('dp', None, 'sp'), may hold values from -6 to 6
- space_weight: bfloat16 [3, 3, 512, 1152], replicated, may hold values from -0.09375 to 0.09375
- time_weight: bfloat16 [3, 1152, 512], replicated, may hold values from -0.109375 to 0.109375
- gain_mid: float32 [1152], replicated, may hold values from 0.5 to 1.5
- shift_mid: float32 [1152], replicated, may hold values from -1.5 to 1.5
- gain_out: float32 [512], replicated, may hold values from 0.5 to 1.5
- shift_out: float32 [512], replicated, may hold values from -1.5 to 1.5
- class_weight: float32 [512, 400], replicated, may hold values from -0.25 to 0.25
- class_bias: float32 [400], replicated, may hold values from -2.5 to 2.5
- frames: int32 [256], P('dp'), may hold values from 1 to 4, as said below
- rows: int32 [256], P('dp'), may hold values from 1 to 8, as said below
- cols: int32 [256], P('dp'), may hold values from 1 to 7
- logit_grad: float32 [256, 400], P('dp'), may hold values from -6 to 6
Outputs:
- logits: float32 [256, 400], P('dp')
- input_grad: float32 [256, 4, 8, 7, 512], P('dp', None, 'sp')
- space_grad: float32 [3, 3, 512, 1152], replicated
- time_grad: float32 [3, 1152, 512], replicated
- gain_mid_grad: float32 [1152], replicated
- shift_mid_grad: float32 [1152], replicated
- gain_out_grad: float32 [512], replicated
- shift_out_grad: float32 [512], replicated
- class_weight_grad: float32 [512, 400], replicated
- class_bias_grad: float32 [400], replicated
The draws below stay inside these ranges and needn't reach their ends.
Inputs may be any that keep to these rules, and one draw needn't show every extreme that they name: `frames`: each value is 1, 2 or 4; both 1 and 4 occur. In each aligned block of 32 clips one clip has all 8 rows; some clip has 1 row.
All inputs are finite; a program needn't handle non-finite values.
Results may differ from the reference program's by a relative error of at most 0.0065.
Values may be sent and summed in bfloat16 or wider, within the bound.
No kernel may reach another device: no remote copies, remote signals or barrier semaphores. Data moves between devices by JAX's collectives and lax.ppermute only.
A program may use at most 192 MiB of HBM per device.

```python
import jax
import jax.numpy as jnp
from jax import lax

C = 512
M = 1152
CLASSES = 400
FRAMES = 4
HEIGHT = 8
WIDTH = 7
CLIPS_DEV = 32
CLIPS = 256


def draw_frames(key, part):
    key = jax.random.fold_in(key, 11)
    keys = jax.random.split(key, 3)
    levels = jax.random.randint(keys[0], (CLIPS,), 0, 3)
    first_spot = jax.random.randint(keys[1], (), 0, CLIPS)
    second_spot = (first_spot + 1 + jax.random.randint(keys[2], (), 0, CLIPS - 1)) % CLIPS
    places = jnp.arange(CLIPS)
    levels = jnp.where(places == first_spot, 2, levels)
    levels = jnp.where(places == second_spot, 0, levels)
    return jnp.where(levels == 0, 1, jnp.where(levels == 1, 2, 4)).astype(jnp.int32)


def draw_rows(key, part):
    key = jax.random.fold_in(key, 12)
    keys = jax.random.split(key, 2)
    block_count = CLIPS // CLIPS_DEV
    grid = jax.random.randint(keys[0], (block_count, CLIPS_DEV), 1, HEIGHT + 1)
    chosen = jax.random.randint(keys[1], (block_count, 1), 0, CLIPS_DEV)
    places = jnp.arange(CLIPS_DEV)[None, :]
    grid = jnp.where(places == chosen, HEIGHT, grid)
    low_spot = (chosen[0, 0] + 1) % CLIPS_DEV
    first_block = jnp.arange(block_count)[:, None] == 0
    grid = jnp.where(first_block & (places == low_spot), 1, grid)
    return grid.reshape(CLIPS).astype(jnp.int32)


def set_ends(drawn, key, low, top_value):
    index_at = [jax.random.randint(jax.random.fold_in(key, axis), (), 0, length) for axis, length in enumerate(drawn.shape)]
    longest = drawn.shape.index(max(drawn.shape))
    next_to = index_at[:longest] + [(index_at[longest] + 1) % drawn.shape[longest]] + index_at[longest + 1:]
    return drawn.at[tuple(index_at)].set(low).at[tuple(next_to)].set(top_value)


def block_levels(own_key, dims, shards, smallest, top_value):
    level = 1.0
    for dim, blocks in shards:
        heights = jax.random.uniform(jax.random.fold_in(jax.random.fold_in(own_key, 6), dim), (blocks,), jnp.float32, smallest / len(shards), top_value / len(shards))
        level = level * jnp.repeat(jnp.exp(heights), dims[dim] // blocks).reshape((-1,) + (1,) * (len(dims) - 1 - dim))
    return level


def centred(stream_key, shape, deviation, most, pieces=(), dtype=jnp.bfloat16):
    loudness = block_levels(stream_key, shape, pieces, -0.22, 0.18) if pieces else 1.0
    result = jax.random.normal(stream_key, shape, jnp.float32) * deviation * loudness
    return jnp.minimum(jnp.maximum(result, -most), most).astype(dtype)


def setup_inputs(seed: int = 0) -> dict:
    key_of = jax.random.split(jax.random.key(seed), 14)
    clip_input = centred(key_of[0], (CLIPS, FRAMES, HEIGHT, WIDTH, C), 1.0, 6.0, ((0, 8), (2, 4)), jnp.float32)
    space_weight = centred(key_of[1], (3, 3, C, M), (9 * C) ** -0.5, 0.09375)
    time_weight = centred(key_of[2], (3, M, C), (3 * M) ** -0.5, 0.109375)
    gain_mid = jnp.clip(1.0 + 0.1 * jax.random.normal(key_of[3], (M,), jnp.float32), 0.5, 1.5)
    shift_mid = centred(key_of[4], (M,), 0.3, 1.5, (), jnp.float32)
    gain_out = jnp.clip(1.0 + 0.1 * jax.random.normal(key_of[5], (C,), jnp.float32), 0.5, 1.5)
    shift_out = centred(key_of[6], (C,), 0.3, 1.5, (), jnp.float32)
    class_weight = centred(key_of[7], (C, CLASSES), C ** -0.5, 0.25, (), jnp.float32)
    class_bias = centred(key_of[8], (CLASSES,), 0.5, 2.5, (), jnp.float32)
    frames = draw_frames(jax.random.fold_in(key_of[13], 71), 0)
    rows = draw_rows(jax.random.fold_in(key_of[13], 71), 0)
    cols = set_ends(jax.random.randint(key_of[11], (CLIPS,), 1, WIDTH + 1), jax.random.fold_in(key_of[11], 1), 1, WIDTH).astype(jnp.int32)
    logit_grad = centred(key_of[12], (CLIPS, CLASSES), 1.0, 6.0, ((0, 8),), jnp.float32)
    return dict(clip_input=clip_input, space_weight=space_weight, time_weight=time_weight, gain_mid=gain_mid, shift_mid=shift_mid, gain_out=gain_out, shift_out=shift_out, class_weight=class_weight, class_bias=class_bias, frames=frames, rows=rows, cols=cols, logit_grad=logit_grad)


EPSILON = 1e-05
HIGH = lax.Precision.HIGHEST

@jax.custom_vjp
def low(v):
    return lax.optimization_barrier(v.astype(jnp.bfloat16)).astype(jnp.float32)

@jax.custom_vjp
def low_back(v):
    return v

def low_keep(v):
    return (low(v), None)

def low_pass(kept, grad):
    return (grad,)

def back_keep(v):
    return (v, None)

def back_low(kept, grad):
    return (low(grad),)
low.defvjp(low_keep, low_pass)
low_back.defvjp(back_keep, back_low)

def space_conv(values, weight):
    row_count = values.shape[2]
    col_count = values.shape[3]
    padded = jnp.pad(values, ((0, 0), (0, 0), (1, 1), (1, 1), (0, 0)))
    total = None
    for row_off in range(3):
        for col_off in range(3):
            term = jnp.einsum('bthwc,cm->bthwm', padded[:, :, row_off:row_off + row_count, col_off:col_off + col_count, :], weight[row_off, col_off], precision=HIGH)
            total = term if total is None else total + term
    return total

def time_conv(values, weight):
    frame_count = values.shape[1]
    padded = jnp.pad(values, ((0, 0), (1, 1), (0, 0), (0, 0), (0, 0)))
    total = None
    for offset in range(3):
        term = jnp.einsum('bthwm,mc->bthwc', padded[:, offset:offset + frame_count], weight[offset], precision=HIGH)
        total = term if total is None else total + term
    return total

def batch_norm(values, mask, count, gain, shift):
    center = lax.optimization_barrier(jnp.sum(values * mask, axis=(0, 1, 2, 3))) / count
    offset = values - center
    spread = lax.optimization_barrier(jnp.sum(mask * offset * offset, axis=(0, 1, 2, 3))) / count
    return gain * offset * lax.rsqrt(spread + EPSILON) + shift

def reference(clip_input, space_weight, time_weight, gain_mid, shift_mid, gain_out, shift_out, class_weight, class_bias, frames, rows, cols, logit_grad):
    clip_count, frame_count, row_count, col_count, width = clip_input.shape
    frame_ok = jnp.arange(frame_count)[None, :] < frames[:, None]
    row_ok = jnp.arange(row_count)[None, :] < rows[:, None]
    col_ok = jnp.arange(col_count)[None, :] < cols[:, None]
    mask = (frame_ok[:, :, None, None] & row_ok[:, None, :, None] & col_ok[:, None, None, :]).astype(jnp.float32)[..., None]
    count = jnp.sum(mask)
    clip_cells = (frames * rows * cols).astype(jnp.float32)

    def forward(inputs, weight_one, weight_two, gain_one, shift_one, gain_two, shift_two, head_weight, head_bias):
        masked_input = inputs * mask
        input_low = low(masked_input)
        mid_pre = low_back(space_conv(input_low, weight_one))
        mid_act = batch_norm(mid_pre, mask, count, gain_one, shift_one)
        mid_low = low(jax.nn.silu(mid_act) * mask)
        out_pre = low_back(time_conv(mid_low, weight_two))
        out_act = batch_norm(out_pre, mask, count, gain_two, shift_two) + masked_input
        block_out = jax.nn.silu(out_act) * mask
        pooled = lax.optimization_barrier(jnp.sum(block_out, axis=(1, 2, 3))) / clip_cells[:, None]
        return jnp.dot(pooled, head_weight, precision=HIGH) + head_bias
    logits, pullback = jax.vjp(forward, clip_input, space_weight.astype(jnp.float32), time_weight.astype(jnp.float32), gain_mid, shift_mid, gain_out, shift_out, class_weight, class_bias)
    grads = pullback(logit_grad)
    return (logits, grads[0], grads[1], grads[2], grads[3], grads[4], grads[5], grads[6], grads[7], grads[8])
```

```python
import functools

import jax
import jax.numpy as jnp
from jax import lax
from jax.experimental import pallas as pl
from jax.experimental.pallas import tpu as pltpu
from jax.sharding import PartitionSpec as P

EPSILON = 1e-05
HIGH = lax.Precision.HIGHEST
F32 = jnp.float32
BF16 = jnp.bfloat16
S_AT, BLOCKS_AT, CORE_AT, ROW_AT, OFF, LEN, PAD, END_AT = 0, 1, 2, 3, 4, 8, 12, 16

VM = pl.BlockSpec(memory_space=pltpu.VMEM)
SM = pl.BlockSpec(memory_space=pltpu.SMEM)
ANY = pl.BlockSpec(memory_space=pl.ANY)


def params(mib):
    return pltpu.CompilerParams(vmem_limit_bytes=mib << 20)


def nt_dot(a, b):
    return lax.dot_general(a, b, (((1,), (1,)), ((), ())), preferred_element_type=F32)


def tn_dot(a, b):
    return lax.dot_general(a, b, (((0,), (0,)), ((), ())), preferred_element_type=F32)


def dot(a, b):
    return jnp.dot(a, b, preferred_element_type=F32)


def split(value):
    high = value.astype(BF16)
    return high, (value - high.astype(F32)).astype(BF16)


def sigmoid(v):
    return 1.0 / (1.0 + jnp.exp(-v))


def slope(v):
    s = sigmoid(v)
    return s * (1.0 + v * (1.0 - s))


def at16(index):
    return pl.multiple_of(index, 16)


def at128(index):
    return pl.multiple_of(index, 128)


def pick_rows(row_info, shift):
    place, col, cols = row_info[0:1, :], row_info[1:2, :], row_info[2:3, :]
    home = col - shift
    ok = (col < cols) & (home >= 0) & (home < cols)
    spot = jnp.where(ok, place - shift, -1)
    size = row_info.shape[1]
    index = lax.broadcasted_iota(jnp.int32, (size, size), 0)
    return jnp.where(index == spot, 1.0, 0.0).astype(BF16)


def pick_cols(col_info, shift):
    place, col, cols = col_info[:, 0:1], col_info[:, 1:2], col_info[:, 2:3]
    home = col - shift
    ok = (col < cols) & (home >= 0) & (home < cols)
    spot = jnp.where(ok, place - shift, -1)
    size = col_info.shape[0]
    index = lax.broadcasted_iota(jnp.int32, (size, size), 1)
    return jnp.where(index == spot, 1.0, 0.0).astype(BF16)


def each_list(meta, base, frame_count, store):
    for t in range(frame_count):
        for half in range(2):

            @pl.when(half * 128 < meta[PAD + t])
            def _(t=t, half=half):
                store(t, half, at16(base + meta[OFF + t] + half * 128))


def space_kernel(
    meta, row_info, own, part, outer, weight, mid_pre, belong, stats, planes, packed, kernel, pick, sems
):
    frame_count = own.shape[1]
    core = meta[CORE_AT]
    s = meta[S_AT]
    copies = [
        pltpu.make_async_copy(weight, kernel, sems.at[0]),
        pltpu.make_async_copy(own, planes.at[pl.ds(1, 2)], sems.at[1]),
        pltpu.make_async_copy(part.at[core], planes.at[3 - 3 * core], sems.at[2]),
        pltpu.make_async_copy(outer, planes.at[3 * core], sems.at[3]),
    ]
    for copy in copies:
        copy.start()
    info = row_info[...]
    for j in range(3):
        hot = pick_rows(info, j - 1)
        for half in range(2):
            pick[half, j * 128 : (j + 1) * 128, :] = hot[half * 128 : (half + 1) * 128, :]
    size = info.shape[1]
    clip_of = lax.broadcasted_iota(jnp.int32, (size, 128), 0) // 8
    lane = lax.broadcasted_iota(jnp.int32, (size, 128), 1)
    frames_of = jnp.broadcast_to(row_info[3:4, 0:128], (size, 128))
    rows_of = jnp.broadcast_to(row_info[4:5, 0:128], (size, 128))
    for h in range(2):
        for t in range(frame_count):
            inside = (clip_of == lane) & (frames_of > t) & (rows_of > meta[ROW_AT] + h)
            source = jnp.where(inside, 1.0, 0.0).astype(BF16)

            def store(t, half, row, source=source):
                belong[pl.ds(row, 128), :] = dot(pick[half, 128:256, :], source).astype(BF16)

            for half in range(2):

                @pl.when(half * 128 < meta[PAD + t])
                def _(t=t, half=half, store=store, h=h):
                    store(t, half, at16(h * s + meta[OFF + t] + half * 128))

        belong[pl.ds(at16(h * s + meta[END_AT]), 128), :] = jnp.zeros((128, 128), BF16)
    for copy in copies[1:]:
        copy.wait()
    for plane in range(4):

        def store(t, half, row, plane=plane):
            got = dot(pick[half], planes[plane, t]).astype(BF16)
            for j in range(3):
                packed[pl.ds(row, 128), j * 512 : (j + 1) * 512] = got[j * 128 : (j + 1) * 128, :]

        each_list(meta, plane * s, frame_count, store)
        packed[pl.ds(at16(plane * s + meta[END_AT]), 128), :] = jnp.zeros((128, 1536), BF16)
    copies[0].wait()
    blocks = meta[BLOCKS_AT]

    def conv(m, total):
        row = at128(m * 256)
        acc = dot(packed[pl.ds(row, 256), :], kernel[0:1536, :])
        acc += dot(packed[pl.ds(at128(s + row), 256), :], kernel[1536:3072, :])
        acc += dot(packed[pl.ds(at128(2 * s + row), 256), :], kernel[3072:4608, :])
        mid_pre[pl.ds(row, 256), :] = acc
        mask = jnp.sum(belong[pl.ds(row, 256), :].astype(F32), axis=1, keepdims=True)
        count, sums = total
        return count + jnp.sum(mask, axis=0, keepdims=True), sums + jnp.sum(acc * mask, axis=0, keepdims=True)

    count, sums = lax.fori_loop(0, blocks, conv, (jnp.zeros((1, 1), F32), jnp.zeros((1, 1152), F32)))
    center = sums / count

    def spread(m, total):
        row = at128(m * 256)
        mask = jnp.sum(belong[pl.ds(row, 256), :].astype(F32), axis=1, keepdims=True)
        off = (mid_pre[pl.ds(row, 256), :] - center) * mask
        return total + jnp.sum(off * off, axis=0, keepdims=True)

    squares = lax.fori_loop(0, blocks, spread, jnp.zeros((1, 1152), F32))
    stats[0:1, :] = jnp.broadcast_to(count, (1, 1152))
    stats[1:2, :] = sums
    stats[2:3, :] = squares
    stats[3:8, :] = jnp.zeros((5, 1152), F32)


def side_kernel(
    meta, row_info, own, own_low, part, outer, outer_part, turned, residual, planes, packed, pick, sems
):
    frame_count = own.shape[1]
    core = meta[CORE_AT]
    s = meta[S_AT]
    copies = [
        pltpu.make_async_copy(own, planes.at[pl.ds(1 + 2 * core, 2)], sems.at[0]),
        pltpu.make_async_copy(part, planes.at[pl.ds(3 - 2 * core, 2)], sems.at[1]),
        pltpu.make_async_copy(outer, planes.at[5 * core], sems.at[2]),
        pltpu.make_async_copy(outer_part, planes.at[5 - 5 * core], sems.at[3]),
    ]
    for copy in copies:
        copy.start()
    info = row_info[...]
    for j in range(3):
        hot = pick_rows(info, j - 1)
        for half in range(2):
            pick[half, j * 128 : (j + 1) * 128, :] = hot[half * 128 : (half + 1) * 128, :]
    for copy in copies:
        copy.wait()

    def plane_step(plane, carry):
        def store(t, half, row):
            got = dot(pick[half], planes[plane, t]).astype(BF16)
            for j in range(3):
                packed[pl.ds(row, 128), j * 512 : (j + 1) * 512] = got[j * 128 : (j + 1) * 128, :]

        each_list(meta, 0, frame_count, store)
        packed[pl.ds(at16(meta[END_AT]), 128), :] = jnp.zeros((128, 1536), BF16)

        def turn(m, carry):
            row = at128(m * 128)
            block = packed[pl.ds(row, 128), :].astype(F32)
            turned[:, pl.ds(at128(plane * s + row), 128)] = block.T.astype(BF16)
            return carry

        return lax.fori_loop(0, s // 128, turn, carry)

    lax.fori_loop(0, 6, plane_step, 0)
    for h in range(2):

        def store(t, half, row, h=h):
            hot = pick[half, 128:256, :]
            plane = 1 + 2 * core + h
            residual[pl.ds(row, 128), :] = dot(hot, planes[plane, t]) + dot(hot, own_low[h, t])

        each_list(meta, h * s, frame_count, store)
        residual[pl.ds(at16(h * s + meta[END_AT]), 128), :] = jnp.zeros((128, 512), F32)


def shift_lists(meta, frame_count, source, target, width, move):
    s = meta[S_AT]
    for h in range(2):

        def store(t, half, row, h=h):
            other = t + move
            if 0 <= other < frame_count:
                block = source(at16(h * s + meta[OFF + other] + half * 128))
                place = half * 128 + lax.broadcasted_iota(jnp.int32, (128, 1), 0)
                keep = jnp.where(place < meta[LEN + other], 1.0, 0.0).astype(BF16)
                target(row, block * keep)
            else:
                target(row, jnp.zeros((128, width), BF16))

        each_list(meta, h * s, frame_count, store)
        target(at16(h * s + meta[END_AT]), jnp.zeros((128, width), BF16))


def time_kernel(frame_count, meta, mid_pre, belong, coef, weight, mid_low, out_pre, stats, wide):
    blocks = meta[BLOCKS_AT]

    def act(m, carry):
        row = at128(m * 256)
        mask = jnp.sum(belong[pl.ds(row, 256), :].astype(F32), axis=1, keepdims=True)
        normed = (mid_pre[pl.ds(row, 256), :] - coef[0:1, :]) * coef[1:2, :]
        value = coef[2:3, :] * normed + coef[3:4, :]
        low = (value * sigmoid(value) * mask).astype(BF16)
        wide[pl.ds(row, 256), 1152:2304] = low
        mid_low[pl.ds(row, 256), :] = low
        return carry

    lax.fori_loop(0, blocks, act, 0)
    wide[pl.ds(at128(2 * meta[S_AT]), 256), :] = jnp.zeros((256, 3456), BF16)
    for k in (0, 2):

        def source(row):
            return wide[pl.ds(row, 128), 1152:2304]

        def target(row, value, k=k):
            wide[pl.ds(row, 128), k * 1152 : (k + 1) * 1152] = value

        shift_lists(meta, frame_count, source, target, 1152, k - 1)

    def conv(m, total):
        row = at128(m * 256)
        acc = dot(wide[pl.ds(row, 256), :], weight[...])
        out_pre[pl.ds(row, 256), :] = acc
        mask = jnp.sum(belong[pl.ds(row, 256), :].astype(F32), axis=1, keepdims=True)
        count, sums = total
        return count + jnp.sum(mask, axis=0, keepdims=True), sums + jnp.sum(acc * mask, axis=0, keepdims=True)

    count, sums = lax.fori_loop(0, blocks, conv, (jnp.zeros((1, 1), F32), jnp.zeros((1, 512), F32)))
    center = sums / count

    def spread(m, total):
        row = at128(m * 256)
        mask = jnp.sum(belong[pl.ds(row, 256), :].astype(F32), axis=1, keepdims=True)
        off = (out_pre[pl.ds(row, 256), :] - center) * mask
        return total + jnp.sum(off * off, axis=0, keepdims=True)

    squares = lax.fori_loop(0, blocks, spread, jnp.zeros((1, 512), F32))
    stats[0:1, :] = jnp.broadcast_to(count, (1, 512))
    stats[1:2, :] = sums
    stats[2:3, :] = squares
    stats[3:8, :] = jnp.zeros((5, 512), F32)


def act_kernel(meta, out_pre, belong, residual, coef, pooled_grad, act_grad, stats, pooled):
    blocks = meta[BLOCKS_AT]
    high, rest = split(pooled_grad[...])
    pooled[...] = jnp.zeros(pooled.shape, F32)

    def step(m, total):
        row = at128(m * 256)
        hot = belong[pl.ds(row, 256), :]
        normed = (out_pre[pl.ds(row, 256), :] - coef[0:1, :]) * coef[1:2, :]
        value = coef[2:3, :] * normed + coef[3:4, :] + residual[pl.ds(row, 256), :]
        s = sigmoid(value)
        first, second = split(value * s)
        pooled[...] += tn_dot(hot, first) + tn_dot(hot, second)
        grad = (dot(hot, high) + dot(hot, rest)) * (s * (1.0 + value * (1.0 - s)))
        act_grad[pl.ds(row, 256), :] = grad
        shift, gain = total
        return (
            shift + jnp.sum(grad, axis=0, keepdims=True),
            gain + jnp.sum(grad * normed, axis=0, keepdims=True),
        )

    zero = jnp.zeros((1, 512), F32)
    shift, gain = lax.fori_loop(0, blocks, step, (zero, zero))
    stats[0:1, :] = shift
    stats[1:2, :] = gain
    stats[2:8, :] = jnp.zeros((6, 512), F32)


def back_kernel(
    frame_count, meta, act_grad, out_pre, belong, out_coef, weight, mid_pre, mid_coef, wide, mid_act_grad, stats
):
    blocks = meta[BLOCKS_AT]

    def grad(m, carry):
        row = at128(m * 256)
        mask = jnp.sum(belong[pl.ds(row, 256), :].astype(F32), axis=1, keepdims=True)
        normed = (out_pre[pl.ds(row, 256), :] - out_coef[0:1, :]) * out_coef[1:2, :]
        inner = act_grad[pl.ds(row, 256), :] - mask * (out_coef[4:5, :] + normed * out_coef[5:6, :])
        wide[pl.ds(row, 256), 512:1024] = (out_coef[2:3, :] * out_coef[1:2, :] * inner).astype(BF16)
        return carry

    lax.fori_loop(0, blocks, grad, 0)
    wide[pl.ds(at128(2 * meta[S_AT]), 256), :] = jnp.zeros((256, 1536), BF16)
    for k in (0, 2):

        def source(row):
            return wide[pl.ds(row, 128), 512:1024]

        def target(row, value, k=k):
            wide[pl.ds(row, 128), k * 512 : (k + 1) * 512] = value

        shift_lists(meta, frame_count, source, target, 512, 1 - k)

    def conv(m, total):
        row = at128(m * 256)
        block = wide[pl.ds(row, 256), :]
        acc = nt_dot(block[:, 0:512], weight[0])
        acc += nt_dot(block[:, 512:1024], weight[1])
        acc += nt_dot(block[:, 1024:1536], weight[2])
        mask = jnp.sum(belong[pl.ds(row, 256), :].astype(F32), axis=1, keepdims=True)
        normed = (mid_pre[pl.ds(row, 256), :] - mid_coef[0:1, :]) * mid_coef[1:2, :]
        acc = acc * mask * slope(mid_coef[2:3, :] * normed + mid_coef[3:4, :])
        mid_act_grad[pl.ds(row, 256), :] = acc
        shift, gain = total
        return (
            shift + jnp.sum(acc, axis=0, keepdims=True),
            gain + jnp.sum(acc * normed, axis=0, keepdims=True),
        )

    zero = jnp.zeros((1, 1152), F32)
    shift, gain = lax.fori_loop(0, blocks, conv, (zero, zero))
    stats[0:1, :] = shift
    stats[1:2, :] = gain
    stats[2:8, :] = jnp.zeros((6, 1152), F32)


def time_grad_kernel(meta, mid_low, wide, out, total):
    blocks = meta[BLOCKS_AT]
    for k in range(3):
        total[...] = jnp.zeros(total.shape, F32)

        def step(m, carry, k=k):
            row = at128(m * 256)
            total[...] += tn_dot(mid_low[pl.ds(row, 256), :], wide[pl.ds(row, 256), k * 512 : (k + 1) * 512])
            return carry

        lax.fori_loop(0, blocks, step, 0)
        for lane in range(4):
            out[k, lane] = total[:, lane * 128 : (lane + 1) * 128].astype(BF16)


def mid_grad_kernel(meta, mid_act_grad, mid_pre, belong, coef, whole, keep, send):
    core = meta[CORE_AT]

    def step(m, carry):
        row = at128(m * 256)
        mask = jnp.sum(belong[pl.ds(row, 256), :].astype(F32), axis=1, keepdims=True)
        normed = (mid_pre[pl.ds(row, 256), :] - coef[0:1, :]) * coef[1:2, :]
        inner = mid_act_grad[pl.ds(row, 256), :] - mask * (coef[4:5, :] + normed * coef[5:6, :])
        low = (coef[2:3, :] * coef[1:2, :] * inner).astype(BF16)
        whole[pl.ds(row, 256), :] = low

        @pl.when(core == 0)
        def _():
            keep[pl.ds(row, 256), 0:512] = low[:, 0:512]
            send[pl.ds(row, 256), 0:512] = low[:, 512:1024]

        @pl.when(core != 0)
        def _():
            keep[pl.ds(row, 256), 0:512] = low[:, 512:1024]
            send[pl.ds(row, 256), 0:512] = low[:, 0:512]

        keep[pl.ds(row, 256), 512:640] = low[:, 1024:1152]
        send[pl.ds(row, 256), 512:640] = low[:, 1024:1152]
        return carry

    lax.fori_loop(0, meta[BLOCKS_AT], step, 0)


def space_grad_kernel(meta, turned, own, part, out, total):
    core = meta[CORE_AT]
    s = meta[S_AT]
    i = pl.program_id(1)
    total[...] = jnp.zeros(total.shape, F32)

    def step(m, carry):
        row = at128(m * 256)
        first = turned[:, pl.ds(at128((2 * core + i) * s + row), 256)]
        second = turned[:, pl.ds(at128((2 - 2 * core + i) * s + row), 256)]
        total[...] += dot(first, own[pl.ds(row, 256), :]) + dot(second, part[pl.ds(row, 256), :])
        return carry

    lax.fori_loop(0, meta[BLOCKS_AT], step, 0)
    for lane in range(4):
        out[0, lane * 512 : (lane + 1) * 512, :] = total[:, lane * 128 : (lane + 1) * 128].astype(BF16)

    @pl.when(core == 0)
    def _():
        out[0, 2048:2304, :] = total[0:256, 512:640].astype(BF16)

    @pl.when(core != 0)
    def _():
        out[0, 2048:2304, :] = total[256:512, 512:640].astype(BF16)


def input_back_kernel(
    frame_count, meta, col_info, grad, weight, act_grad, dense, edges, wide, spread, high, rest
):
    s = meta[S_AT]
    info = col_info[...]
    for j in range(3):
        spread[:, j * 256 : (j + 1) * 256] = pick_cols(info, j - 1)
    terms = {0: [(0, 0)], 1: [(0, 1), (1, 0)], 2: [(0, 2), (1, 1)], 3: [(1, 2)]}
    for plane in range(4):
        wide[plane, pl.ds(at128(s), 256), :] = jnp.zeros((256, 1536), BF16)

    def conv(m, carry):
        row = at128(m * 128)
        for plane in range(4):
            acc = None
            for h, i in terms[plane]:
                term = nt_dot(grad[pl.ds(at128(h * s + row), 128), :], weight[i * 1536 : (i + 1) * 1536, :])
                acc = term if acc is None else acc + term
            wide[plane, pl.ds(row, 128), :] = acc.astype(BF16)
        return carry

    lax.fori_loop(0, s // 128, conv, 0)

    def cut(m, carry):
        row = at128(m * 256)
        first, second = split(act_grad[pl.ds(row, 256), :])
        high[pl.ds(row, 256), :] = first
        rest[pl.ds(row, 256), :] = second
        return carry

    lax.fori_loop(0, meta[BLOCKS_AT], cut, 0)
    for part in (high, rest):
        part[pl.ds(at128(2 * s), 256), :] = jnp.zeros((256, 512), BF16)
    for plane in range(4):
        for t in range(frame_count):
            row = at16(meta[OFF + t])
            acc = None
            for j in range(3):
                term = dot(spread[:, j * 256 : (j + 1) * 256], wide[plane, pl.ds(row, 256), j * 512 : (j + 1) * 512])
                acc = term if acc is None else acc + term
            if plane == 0:
                edges[0, t] = acc.astype(BF16)
            elif plane == 3:
                edges[1, t] = acc.astype(BF16)
            else:
                row = at16((plane - 1) * s + meta[OFF + t])
                acc += dot(spread[:, 256:512], high[pl.ds(row, 256), :])
                acc += dot(spread[:, 256:512], rest[pl.ds(row, 256), :])
                dense[plane - 1, t] = acc


def join_kernel(meta, own, part, out):
    core = meta[CORE_AT]

    def place(first, second):
        for lane in range(4):
            out[0, :, lane * 128 : (lane + 1) * 128] = first[0, lane * 512 : (lane + 1) * 512, :].astype(F32)
            out[0, :, 512 + lane * 128 : 640 + lane * 128] = second[0, lane * 512 : (lane + 1) * 512, :].astype(F32)
        out[0, 0:256, 1024:1152] = first[0, 2048:2304, :].astype(F32)
        out[0, 256:512, 1024:1152] = second[0, 2048:2304, :].astype(F32)

    @pl.when(core == 0)
    def _():
        place(own, part)

    @pl.when(core != 0)
    def _():
        place(part, own)


def swap(value, axis, bit):
    size = lax.axis_size(axis)
    if size <= bit:
        return None
    return lax.ppermute(value, axis, [(i, i ^ bit) for i in range(size)])


def bits(axis):
    return [(axis, 1 << n) for n in range((lax.axis_size(axis) - 1).bit_length())]


def sum_all(value):
    for axis, bit in bits("sp") + bits("dp"):
        value = value + swap(value, axis, bit)
    return value


def merge_all(stats):
    for axis, bit in bits("sp") + bits("dp"):
        other = swap(stats, axis, bit)
        count = stats[0] + other[0]
        gap = stats[1] / stats[0] - other[1] / other[0]
        squares = stats[2] + other[2] + gap * gap * (stats[0] * other[0] / count)
        stats = jnp.stack([count, stats[1] + other[1], squares])
    return stats


def bit_of(axis, bit):
    return (lax.axis_index(axis) // bit) % 2


def halve(part, order):
    for axis, bit in order:
        n, rows, lanes = part.shape
        part = part.reshape(n, 2, rows // 2, lanes)
        mine = bit_of(axis, bit)
        send = lax.dynamic_index_in_dim(part, 1 - mine, 1, keepdims=False).astype(BF16)
        keep = lax.dynamic_index_in_dim(part, mine, 1, keepdims=False).astype(F32)
        part = keep + swap(send, axis, bit).astype(F32)
    return part.astype(BF16)


def double(part, order):
    for axis, bit in reversed(order):
        other = swap(part, axis, bit)
        mine = bit_of(axis, bit)
        low = jnp.where(mine == 0, part, other)
        high = jnp.where(mine == 0, other, part)
        part = jnp.concatenate([low, high], axis=1)
    return part


def shards(
    clip_input,
    space_weight,
    time_weight,
    gain_mid,
    shift_mid,
    gain_out,
    shift_out,
    class_weight,
    class_bias,
    frames,
    rows,
    cols,
    logit_grad,
):
    clip_count, frame_count, row_count, col_count, width = clip_input.shape
    middle = space_weight.shape[-1]
    classes = class_weight.shape[1]
    cells = clip_count * 8
    most = row_count * frame_count * clip_count * col_count
    sp_count = lax.axis_size("sp")
    core = lax.axis_index("sp") % 2
    row_start = lax.axis_index("sp") * row_count

    before = (frames[None, :] > frames[:, None]) | (
        (frames[None, :] == frames[:, None]) & (jnp.arange(clip_count)[None, :] < jnp.arange(clip_count)[:, None])
    )
    start = jnp.sum(jnp.where(before, cols[None, :], 0), axis=1)
    length = jnp.sum(jnp.where(frames[None, :] > jnp.arange(frame_count)[:, None], cols[None, :], 0), axis=1)
    padded = (length + 15) // 16 * 16
    offset = jnp.cumsum(padded) - padded
    end = jnp.sum(padded)
    plane = (end + 127) // 128 * 128
    meta = jnp.concatenate(
        [jnp.stack([plane, plane // 128, core, row_start]), offset, length, padded, end[None]]
    ).astype(jnp.int32)
    column = jnp.arange(8)[None, :]
    info = jnp.stack(
        [
            start[:, None] + column,
            jnp.broadcast_to(column, (clip_count, 8)),
            jnp.broadcast_to(cols[:, None], (clip_count, 8)),
            jnp.zeros((clip_count, 8), jnp.int32),
        ]
    ).reshape(4, cells)
    by_clip = jnp.zeros((2, cells), jnp.int32).at[:, :clip_count].set(jnp.stack([frames, rows]))
    row_info = jnp.concatenate([info[:3], by_clip, jnp.zeros((3, cells), jnp.int32)]).astype(jnp.int32)
    col_info = jnp.concatenate([info, info], axis=0).T.astype(jnp.int32)

    frame_ok = jnp.arange(frame_count)[None, :] < frames[:, None]
    row_ok = (row_start + jnp.arange(row_count))[None, :] < rows[:, None]
    col_ok = jnp.arange(col_count)[None, :] < cols[:, None]
    mask = (frame_ok[:, :, None, None] & row_ok[:, None, :, None] & col_ok[:, None, None, :])[..., None]
    masked = jnp.where(mask, clip_input, 0.0)
    masked = jnp.pad(masked.transpose(2, 1, 0, 3, 4), ((0, 0), (0, 0), (0, 0), (0, 8 - col_count), (0, 0)))
    masked = masked.reshape(row_count, frame_count, cells, width)
    rounded = lax.reduce_precision(masked, 8, 7)
    own = rounded.astype(BF16)
    own_low = (masked - rounded).astype(BF16)
    part = swap(own, "sp", 1)
    ahead = [(i, i + 1 if i % 2 else i - 1) for i in range(sp_count)]
    outer = lax.ppermute(
        lax.dynamic_index_in_dim(own, core, 0, keepdims=False),
        "sp",
        [(i, j) for i, j in ahead if 0 <= j < sp_count],
    )
    outer_part = swap(outer, "sp", 1)

    weight = space_weight.reshape(9 * width, middle)
    mid_pre, belong, stats = pl.pallas_call(
        space_kernel,
        out_shape=(
            jax.ShapeDtypeStruct((most, middle), F32),
            jax.ShapeDtypeStruct((most + 256, 128), BF16),
            jax.ShapeDtypeStruct((8, middle), F32),
        ),
        in_specs=[SM, VM, ANY, ANY, ANY, ANY],
        out_specs=(VM, VM, VM),
        scratch_shapes=[
            pltpu.VMEM((4, frame_count, cells, width), BF16),
            pltpu.VMEM((2 * most + 256, 3 * width), BF16),
            pltpu.VMEM((9 * width, middle), BF16),
            pltpu.VMEM((2, 384, cells), BF16),
            pltpu.SemaphoreType.DMA((4,)),
        ],
        compiler_params=params(40),
        name="space_conv",
    )(meta, row_info, own, part, outer, weight)

    turned, residual = pl.pallas_call(
        side_kernel,
        out_shape=(
            jax.ShapeDtypeStruct((3 * width, 3 * most), BF16),
            jax.ShapeDtypeStruct((most + 256, width), F32),
        ),
        in_specs=[SM, VM, ANY, VM, ANY, ANY, ANY],
        out_specs=(VM, VM),
        scratch_shapes=[
            pltpu.VMEM((6, frame_count, cells, width), BF16),
            pltpu.VMEM((most // 2 + 256, 3 * width), BF16),
            pltpu.VMEM((2, 384, cells), BF16),
            pltpu.SemaphoreType.DMA((4,)),
        ],
        compiler_params=params(38),
        name="side",
    )(meta, row_info, own, own_low, part, outer, outer_part)

    clip_cells = (frames * rows * cols).astype(F32)
    pooled_grad = jnp.dot(logit_grad, class_weight.T, precision=HIGH) / clip_cells[:, None]
    pooled_grad = jnp.pad(pooled_grad, ((0, 128 - clip_count), (0, 0)))

    merged = merge_all(stats[:3])
    count_all = merged[0, 0]
    mid_coef = jnp.stack(
        [merged[1] / merged[0], lax.rsqrt(merged[2] / merged[0] + EPSILON), gain_mid, shift_mid]
    )
    mid_low, out_pre, stats = pl.pallas_call(
        functools.partial(time_kernel, frame_count),
        out_shape=(
            jax.ShapeDtypeStruct((most, middle), BF16),
            jax.ShapeDtypeStruct((most, width), F32),
            jax.ShapeDtypeStruct((8, width), F32),
        ),
        in_specs=[SM, VM, VM, VM, VM],
        out_specs=(VM, VM, VM),
        scratch_shapes=[pltpu.VMEM((most + 256, 3 * middle), BF16)],
        compiler_params=params(38),
        name="time_conv",
    )(meta, mid_pre, belong, mid_coef, time_weight.reshape(3 * middle, width))

    merged = merge_all(stats[:3])
    out_coef = jnp.stack(
        [merged[1] / merged[0], lax.rsqrt(merged[2] / merged[0] + EPSILON), gain_out, shift_out]
    )
    act_grad, stats, pooled_sum = pl.pallas_call(
        act_kernel,
        out_shape=(
            jax.ShapeDtypeStruct((most, width), F32),
            jax.ShapeDtypeStruct((8, width), F32),
            jax.ShapeDtypeStruct((128, width), F32),
        ),
        in_specs=[SM, VM, VM, VM, VM, VM],
        out_specs=(VM, VM, VM),
        compiler_params=params(16),
        name="act",
    )(meta, out_pre, belong, residual, out_coef, pooled_grad)

    first = (lax.axis_index("sp") == 0).astype(F32)
    bias_part = jnp.pad(jnp.sum(logit_grad, axis=0) * first, (0, width - classes))
    sums = sum_all(jnp.concatenate([stats[:2], bias_part[None]]))
    shift_out_grad, gain_out_grad, class_bias_grad = sums[0], sums[1], sums[2, :classes]
    pooled_own = pooled_sum[:clip_count] / clip_cells[:, None]
    logits = jnp.dot(pooled_own, class_weight, precision=HIGH)
    for axis, bit in bits("sp"):
        logits = logits + swap(logits, axis, bit)
    logits = logits + class_bias
    class_part = jnp.dot(pooled_own.T, logit_grad, precision=HIGH)

    out_coef = jnp.concatenate([out_coef, sums[:2] / count_all])
    wide, mid_act_grad, stats = pl.pallas_call(
        functools.partial(back_kernel, frame_count),
        out_shape=(
            jax.ShapeDtypeStruct((most + 256, 3 * width), BF16),
            jax.ShapeDtypeStruct((most, middle), F32),
            jax.ShapeDtypeStruct((8, middle), F32),
        ),
        in_specs=[SM, VM, VM, VM, VM, VM, VM, VM],
        out_specs=(VM, VM, VM),
        compiler_params=params(39),
        name="time_back",
    )(meta, act_grad, out_pre, belong, out_coef, time_weight, mid_pre, mid_coef)

    time_part = pl.pallas_call(
        time_grad_kernel,
        out_shape=jax.ShapeDtypeStruct((3, 4, middle, 128), BF16),
        in_specs=[SM, VM, VM],
        out_specs=VM,
        scratch_shapes=[pltpu.VMEM((middle, width), F32)],
        compiler_params=params(21),
        name="time_grad",
    )(meta, mid_low, wide)

    sums = sum_all(stats[:2])
    shift_mid_grad, gain_mid_grad = sums[0], sums[1]
    mid_coef = jnp.concatenate([mid_coef, sums / count_all])
    mid_grad, keep, send = pl.pallas_call(
        mid_grad_kernel,
        out_shape=(
            jax.ShapeDtypeStruct((most, middle), BF16),
            jax.ShapeDtypeStruct((most, 640), BF16),
            jax.ShapeDtypeStruct((most, 640), BF16),
        ),
        in_specs=[SM, VM, VM, VM, VM],
        out_specs=(VM, VM, VM),
        compiler_params=params(30),
        name="mid_grad",
    )(meta, mid_act_grad, mid_pre, belong, mid_coef)
    other = swap(send, "sp", 1)

    space_part = pl.pallas_call(
        space_grad_kernel,
        grid_spec=pltpu.PrefetchScalarGridSpec(
            num_scalar_prefetch=1,
            grid=(3, 3),
            in_specs=[
                pl.BlockSpec((width, 3 * most), lambda j, i, meta: (j, 0)),
                pl.BlockSpec((most, 640), lambda j, i, meta: (0, 0)),
                pl.BlockSpec((most, 640), lambda j, i, meta: (0, 0)),
            ],
            out_specs=pl.BlockSpec((1, 2304, 128), lambda j, i, meta: (3 * j + i, 0, 0)),
            scratch_shapes=[pltpu.VMEM((width, 640), F32)],
        ),
        out_shape=jax.ShapeDtypeStruct((9, 2304, 128), BF16),
        compiler_params=params(28),
        name="space_grad",
    )(meta, turned, keep, other)

    dense, edges = pl.pallas_call(
        functools.partial(input_back_kernel, frame_count),
        out_shape=(
            jax.ShapeDtypeStruct((row_count, frame_count, cells, width), F32),
            jax.ShapeDtypeStruct((2, frame_count, cells, width), BF16),
        ),
        in_specs=[SM, VM, VM, VM, VM],
        out_specs=(VM, VM),
        scratch_shapes=[
            pltpu.VMEM((4, most // 2 + 256, 3 * width), BF16),
            pltpu.VMEM((cells, 3 * cells), BF16),
            pltpu.VMEM((most + 256, width), BF16),
            pltpu.VMEM((most + 256, width), BF16),
        ],
        compiler_params=params(48),
        name="input_back",
    )(meta, col_info, mid_grad, weight, act_grad)
    up = lax.ppermute(edges[0], "sp", [(i, i - 1) for i in range(1, sp_count)])
    down = lax.ppermute(edges[1], "sp", [(i, i + 1) for i in range(sp_count - 1)])
    input_grad = dense + jnp.stack([down, up]).astype(F32)
    input_grad = input_grad.reshape(row_count, frame_count, clip_count, 8, width)[:, :, :, :col_count]
    input_grad = jnp.where(mask, input_grad.transpose(2, 1, 0, 3, 4), 0.0)

    x_bits, y_bits, z_bits = bits("sp")[1:], bits("dp")[:1], bits("dp")[1:]
    order_a = x_bits + y_bits + z_bits
    order_b = y_bits + x_bits + z_bits
    order_c = z_bits + x_bits + y_bits
    parts = []
    for low, high, order in ((0, 4, order_a), (4, 8, order_b), (8, 9, order_c)):
        parts.append(double(halve(space_part[low:high], order), order))
    gathered = jnp.concatenate(parts)
    gathered_part = swap(gathered, "sp", 1)
    space_grad = pl.pallas_call(
        join_kernel,
        grid_spec=pltpu.PrefetchScalarGridSpec(
            num_scalar_prefetch=1,
            grid=(9,),
            in_specs=[
                pl.BlockSpec((1, 2304, 128), lambda n, meta: (n % 3 * 3 + n // 3, 0, 0)),
                pl.BlockSpec((1, 2304, 128), lambda n, meta: (n % 3 * 3 + n // 3, 0, 0)),
            ],
            out_specs=pl.BlockSpec((1, width, middle), lambda n, meta: (n, 0, 0)),
        ),
        out_shape=jax.ShapeDtypeStruct((9, width, middle), F32),
        compiler_params=params(24),
        name="join",
    )(meta, gathered, gathered_part).reshape(3, 3, width, middle)

    class_rows = jnp.pad(class_part, ((0, 0), (0, 512 - classes))).astype(BF16)
    class_rows = class_rows.reshape(width, 4, 128).transpose(1, 0, 2).reshape(1, 4 * width, 128)
    small = jnp.concatenate([time_part.reshape(1, 12 * middle, 128), class_rows], axis=1)
    order = bits("sp")[:1] + order_b
    small = double(halve(small, order), order)
    time_grad = small[0, : 12 * middle].reshape(3, 4, middle, 128).transpose(0, 2, 1, 3)
    time_grad = time_grad.reshape(3, middle, width).astype(F32)
    class_weight_grad = small[0, 12 * middle :].reshape(4, width, 128).transpose(1, 0, 2)
    class_weight_grad = class_weight_grad.reshape(width, 512)[:, :classes].astype(F32)
    return (
        logits,
        input_grad,
        space_grad,
        time_grad,
        gain_mid_grad,
        shift_mid_grad,
        gain_out_grad,
        shift_out_grad,
        class_weight_grad,
        class_bias_grad,
    )


def solution(mesh):
    placed = (
        P("dp", None, "sp", None, None),
        P(),
        P(),
        P(),
        P(),
        P(),
        P(),
        P(),
        P(),
        P("dp"),
        P("dp"),
        P("dp"),
        P("dp", None),
    )
    return jax.shard_map(
        shards,
        mesh=mesh,
        in_specs=placed,
        out_specs=(
            P("dp", None),
            P("dp", None, "sp", None, None),
            P(),
            P(),
            P(),
            P(),
            P(),
            P(),
            P(),
            P(),
        ),
        check_vma=False,
    )
```

```python
import functools

import jax
import jax.numpy as jnp
from jax import lax
from jax.experimental import pallas as pl
from jax.experimental.pallas import tpu as pltpu
from jax.sharding import PartitionSpec as P

EPSILON = 1e-05
HIGH = lax.Precision.HIGHEST
F32 = jnp.float32
BF16 = jnp.bfloat16
S_AT, BLOCKS_AT, CORE_AT, ROW_AT, OFF, LEN, PAD, END_AT = 0, 1, 2, 3, 4, 8, 12, 16

PLAN = ("space_b", "t", "space_c", "back", "t", "b", "spread") + ("t", "c", "b") * 7

VM = pl.BlockSpec(memory_space=pltpu.VMEM)
SM = pl.BlockSpec(memory_space=pltpu.SMEM)
ANY = pl.BlockSpec(memory_space=pl.ANY)
HBM = pl.BlockSpec(memory_space=pltpu.HBM)


def in_hbm(value):
    return pltpu.with_memory_space_constraint(value, pltpu.HBM)


def params(mib):
    return pltpu.CompilerParams(vmem_limit_bytes=mib << 20)


def nt_dot(a, b):
    return lax.dot_general(a, b, (((1,), (1,)), ((), ())), preferred_element_type=F32)


def tn_dot(a, b):
    return lax.dot_general(a, b, (((0,), (0,)), ((), ())), preferred_element_type=F32)


def dot(a, b):
    return jnp.dot(a, b, preferred_element_type=F32)


def split(value):
    high = value.astype(BF16)
    return high, (value - high.astype(F32)).astype(BF16)


def sigmoid(v):
    return 1.0 / (1.0 + jnp.exp(-v))


def slope(v):
    s = sigmoid(v)
    return s * (1.0 + v * (1.0 - s))


def at16(index):
    return pl.multiple_of(index, 16)


def at128(index):
    return pl.multiple_of(index, 128)


def pick_rows(row_info, shift):
    place, col, cols = row_info[0:1, :], row_info[1:2, :], row_info[2:3, :]
    home = col - shift
    ok = (col < cols) & (home >= 0) & (home < cols)
    spot = jnp.where(ok, place - shift, -1)
    size = row_info.shape[1]
    index = lax.broadcasted_iota(jnp.int32, (size, size), 0)
    return jnp.where(index == spot, 1.0, 0.0).astype(BF16)


def pick_cols(col_info, shift):
    place, col, cols = col_info[:, 0:1], col_info[:, 1:2], col_info[:, 2:3]
    home = col - shift
    ok = (col < cols) & (home >= 0) & (home < cols)
    spot = jnp.where(ok, place - shift, -1)
    size = col_info.shape[0]
    index = lax.broadcasted_iota(jnp.int32, (size, size), 1)
    return jnp.where(index == spot, 1.0, 0.0).astype(BF16)


def each_list(meta, base, frame_count, store):
    for t in range(frame_count):
        for half in range(2):

            @pl.when(half * 128 < meta[PAD + t])
            def _(t=t, half=half):
                store(t, half, at16(base + meta[OFF + t] + half * 128))


def gather_setup(row_info, pick):
    info = row_info[...]
    for j in range(3):
        hot = pick_rows(info, j - 1)
        for half in range(2):
            pick[half, j * 128 : (j + 1) * 128, :] = hot[half * 128 : (half + 1) * 128, :]


def gather_plane(meta, pick, source, packed, base, frame_count):
    def store(t, half, row):
        got = dot(pick[half], source(t)).astype(BF16)
        for j in range(3):
            packed[pl.ds(row, 128), j * 512 : (j + 1) * 512] = got[j * 128 : (j + 1) * 128, :]

    each_list(meta, base, frame_count, store)
    packed[pl.ds(at16(base + meta[END_AT]), 128), :] = jnp.zeros((128, 1536), BF16)


def copy_out(meta, blocks, source, target, start, sems, action):
    def one(m, carry):
        copy = pltpu.make_async_copy(
            source.at[pl.ds(at128(m * 128), 128)], target.at[pl.ds(at128(start + m * 128), 128)], sems.at[m]
        )
        if action == "start":
            copy.start()
        else:
            copy.wait()
        return carry

    lax.fori_loop(0, blocks, one, 0)


def space_kernel(
    meta, row_info, own, own_low, part, weight_in, mid_pre, belong, residual, stored, packed, pick, weight, sems, load
):
    frame_count = own.shape[1]
    core = meta[CORE_AT]
    s = meta[S_AT]
    blocks = meta[BLOCKS_AT]
    fetch = pltpu.make_async_copy(weight_in, weight, load)
    fetch.start()
    gather_setup(row_info, pick)

    @pl.when(core == 0)
    def _():
        for h in range(2):
            gather_plane(meta, pick, lambda t, h=h: own[h, t], packed, h * s, frame_count)
        for h in range(2):
            gather_plane(meta, pick, lambda t, h=h: part[h, t], packed, (2 + h) * s, frame_count)

    @pl.when(core != 0)
    def _():
        for h in range(2):
            gather_plane(meta, pick, lambda t, h=h: part[h, t], packed, h * s, frame_count)
        for h in range(2):
            gather_plane(meta, pick, lambda t, h=h: own[h, t], packed, (2 + h) * s, frame_count)

    copy_out(meta, 4 * blocks, packed, stored, s, sems, "start")
    size = row_info.shape[1]
    clip_of = lax.broadcasted_iota(jnp.int32, (size, 128), 0) // 8
    lane = lax.broadcasted_iota(jnp.int32, (size, 128), 1)
    frames_of = jnp.broadcast_to(row_info[3:4, 0:128], (size, 128))
    rows_of = jnp.broadcast_to(row_info[4:5, 0:128], (size, 128))
    for h in range(2):

        def store(t, half, row, h=h):
            hot = pick[half, 128:256, :]
            inside = (clip_of == lane) & (frames_of > t) & (rows_of > meta[ROW_AT] + h)
            belong[pl.ds(row, 128), :] = dot(hot, jnp.where(inside, 1.0, 0.0).astype(BF16)).astype(BF16)
            residual[pl.ds(row, 128), :] = dot(hot, own[h, t]) + dot(hot, own_low[h, t])

        each_list(meta, h * s, frame_count, store)
        belong[pl.ds(at16(h * s + meta[END_AT]), 128), :] = jnp.zeros((128, 128), BF16)
        residual[pl.ds(at16(h * s + meta[END_AT]), 128), :] = jnp.zeros((128, 512), F32)
    fetch.wait()
    for h in range(2):

        def conv(m, carry, h=h):
            row = at128(h * s + m * 128)

            def tap(i):
                source = packed[pl.ds(at128((2 * core + h + i - 1) * s + m * 128), 128), :]
                return dot(source, weight[i * 1536 : (i + 1) * 1536, :])

            mid_pre[pl.ds(row, 128), :] = tap(1) + tap(2 - 2 * h)

            @pl.when(core == 1 - h)
            def _():
                mid_pre[pl.ds(row, 128), :] += tap(2 * h)

            return carry

        lax.fori_loop(0, blocks, conv, 0)
    copy_out(meta, 4 * blocks, packed, stored, s, sems, "wait")


def mask_of(belong, row, size=256):
    return jnp.sum(belong[pl.ds(row, size), :].astype(F32), axis=1, keepdims=True)


def norm_of(merged):
    count = merged[0:1, :]
    return merged[1:2, :] / count, lax.rsqrt(merged[2:3, :] / count + EPSILON)


def norm_sums(meta, values, belong, stats):
    width = values.shape[1]

    def sums(m, total):
        row = at128(m * 256)
        mask = mask_of(belong, row)
        return (
            total[0] + jnp.sum(mask, axis=0, keepdims=True),
            total[1] + jnp.sum(values[pl.ds(row, 256), :] * mask, axis=0, keepdims=True),
        )

    count, total = lax.fori_loop(
        0, meta[BLOCKS_AT], sums, (jnp.zeros((1, 1), F32), jnp.zeros((1, width), F32))
    )
    center = total / count

    def spread(m, squares):
        row = at128(m * 256)
        off = (values[pl.ds(row, 256), :] - center) * mask_of(belong, row)
        return squares + jnp.sum(off * off, axis=0, keepdims=True)

    squares = lax.fori_loop(0, meta[BLOCKS_AT], spread, jnp.zeros((1, width), F32))
    stats[0:1, :] = jnp.broadcast_to(count, (1, width))
    stats[1:2, :] = total
    stats[2:3, :] = squares
    stats[3:8, :] = jnp.zeros((5, width), F32)


def space_edge_kernel(
    meta, row_info, mid_in, stored_in, outer, weight_in, belong, mid_pre, stored, stats, pick, plane, weight, sems, load
):
    core = meta[CORE_AT]
    s = meta[S_AT]
    blocks = meta[BLOCKS_AT]
    fetch = pltpu.make_async_copy(
        weight_in.at[pl.ds(pl.multiple_of(core * 3072, 1024), 1536)], weight, load
    )
    fetch.start()
    gather_setup(row_info, pick)
    gather_plane(meta, pick, lambda t: outer[t], plane, 0, outer.shape[0])
    copy_out(meta, blocks, plane, stored, 5 * s * core, sems, "start")
    fetch.wait()

    def conv(m, carry):
        row = at128(core * s + m * 128)
        mid_pre[pl.ds(row, 128), :] += dot(plane[pl.ds(at128(m * 128), 128), :], weight[...])
        return carry

    lax.fori_loop(0, blocks, conv, 0)
    norm_sums(meta, mid_pre, belong, stats)
    copy_out(meta, blocks, plane, stored, 5 * s * core, sems, "wait")


def store_edge_kernel(meta, row_info, stored_in, outer, after, stored, pick, plane, sems):
    core = meta[CORE_AT]
    s = meta[S_AT]
    blocks = meta[BLOCKS_AT]
    gather_setup(row_info, pick)
    gather_plane(meta, pick, lambda t: outer[t], plane, 0, outer.shape[0])
    copy_out(meta, blocks, plane, stored, 5 * s * (1 - core), sems, "start")
    copy_out(meta, blocks, plane, stored, 5 * s * (1 - core), sems, "wait")


def shift_lists(meta, frame_count, source, target, width, move):
    s = meta[S_AT]
    for h in range(2):

        def store(t, half, row, h=h):
            other = t + move
            if 0 <= other < frame_count:
                block = source(at16(h * s + meta[OFF + other] + half * 128))
                place = half * 128 + lax.broadcasted_iota(jnp.int32, (128, 1), 0)
                keep = jnp.where(place < meta[LEN + other], 1.0, 0.0).astype(BF16)
                target(row, block * keep)
            else:
                target(row, jnp.zeros((128, width), BF16))

        each_list(meta, h * s, frame_count, store)
        target(at16(h * s + meta[END_AT]), jnp.zeros((128, width), BF16))


def time_kernel(frame_count, meta, mid_pre, belong, merged, gain, shift, weight, mid_low, out_pre, stats, wide):
    blocks = meta[BLOCKS_AT]
    center, scale = norm_of(merged)

    def act(m, carry):
        row = at128(m * 256)
        mask = mask_of(belong, row)
        normed = (mid_pre[pl.ds(row, 256), :] - center) * scale
        value = gain[...] * normed + shift[...]
        low = (value * sigmoid(value) * mask).astype(BF16)
        wide[pl.ds(row, 256), 1152:2304] = low
        mid_low[pl.ds(row, 256), :] = low
        return carry

    lax.fori_loop(0, blocks, act, 0)
    wide[pl.ds(at128(2 * meta[S_AT]), 256), :] = jnp.zeros((256, 3456), BF16)
    for k in (0, 2):

        def source(row):
            return wide[pl.ds(row, 128), 1152:2304]

        def target(row, value, k=k):
            wide[pl.ds(row, 128), k * 1152 : (k + 1) * 1152] = value

        shift_lists(meta, frame_count, source, target, 1152, k - 1)

    def conv(m, carry):
        row = at128(m * 256)
        out_pre[pl.ds(row, 256), :] = dot(wide[pl.ds(row, 256), :], weight[...])
        return carry

    lax.fori_loop(0, blocks, conv, 0)
    norm_sums(meta, out_pre, belong, stats)


def act_kernel(meta, out_pre, belong, residual, merged, gain_ref, shift_ref, pooled_grad, act_grad, stats, pooled):
    blocks = meta[BLOCKS_AT]
    center, scale = norm_of(merged)
    high, rest = split(pooled_grad[...])
    pooled[...] = jnp.zeros(pooled.shape, F32)

    def step(m, total):
        row = at128(m * 256)
        hot = belong[pl.ds(row, 256), :]
        normed = (out_pre[pl.ds(row, 256), :] - center) * scale
        value = gain_ref[...] * normed + shift_ref[...] + residual[pl.ds(row, 256), :]
        s = sigmoid(value)
        first, second = split(value * s)
        pooled[...] += tn_dot(hot, first) + tn_dot(hot, second)
        grad = (dot(hot, high) + dot(hot, rest)) * (s * (1.0 + value * (1.0 - s)))
        act_grad[pl.ds(row, 256), :] = grad
        shift, gain = total
        return (
            shift + jnp.sum(grad, axis=0, keepdims=True),
            gain + jnp.sum(grad * normed, axis=0, keepdims=True),
        )

    zero = jnp.zeros((1, 512), F32)
    shift, gain = lax.fori_loop(0, blocks, step, (zero, zero))
    stats[0:1, :] = shift
    stats[1:2, :] = gain
    stats[2:8, :] = jnp.zeros((6, 512), F32)


def back_kernel(
    frame_count, meta, act_grad, out_pre, belong, out_merged, out_gain, out_sums, weight, mid_pre, mid_merged,
    mid_gain, mid_shift, wide, mid_act_grad, stats,
):
    blocks = meta[BLOCKS_AT]
    out_center, out_scale = norm_of(out_merged)
    mid_center, mid_scale = norm_of(mid_merged)
    out_shift_part = out_sums[0:1, :] / out_merged[0:1, :]
    out_gain_part = out_sums[1:2, :] / out_merged[0:1, :]

    def grad(m, carry):
        row = at128(m * 256)
        mask = mask_of(belong, row)
        normed = (out_pre[pl.ds(row, 256), :] - out_center) * out_scale
        inner = act_grad[pl.ds(row, 256), :] - mask * (out_shift_part + normed * out_gain_part)
        wide[pl.ds(row, 256), 512:1024] = (out_gain[...] * out_scale * inner).astype(BF16)
        return carry

    lax.fori_loop(0, blocks, grad, 0)
    wide[pl.ds(at128(2 * meta[S_AT]), 256), :] = jnp.zeros((256, 1536), BF16)
    for k in (0, 2):

        def source(row):
            return wide[pl.ds(row, 128), 512:1024]

        def target(row, value, k=k):
            wide[pl.ds(row, 128), k * 512 : (k + 1) * 512] = value

        shift_lists(meta, frame_count, source, target, 512, 1 - k)

    def conv(m, total):
        row = at128(m * 256)
        block = wide[pl.ds(row, 256), :]
        acc = nt_dot(block[:, 0:512], weight[0])
        acc += nt_dot(block[:, 512:1024], weight[1])
        acc += nt_dot(block[:, 1024:1536], weight[2])
        mask = mask_of(belong, row)
        normed = (mid_pre[pl.ds(row, 256), :] - mid_center) * mid_scale
        acc = acc * mask * slope(mid_gain[...] * normed + mid_shift[...])
        mid_act_grad[pl.ds(row, 256), :] = acc
        shift, gain = total
        return (
            shift + jnp.sum(acc, axis=0, keepdims=True),
            gain + jnp.sum(acc * normed, axis=0, keepdims=True),
        )

    zero = jnp.zeros((1, 1152), F32)
    shift, gain = lax.fori_loop(0, blocks, conv, (zero, zero))
    stats[0:1, :] = shift
    stats[1:2, :] = gain
    stats[2:8, :] = jnp.zeros((6, 1152), F32)


def time_grad_kernel(meta, mid_low, wide, pooled, logit_grad, after, keep, send, total):
    core = meta[CORE_AT]
    middle = mid_low.shape[1]
    classes = logit_grad.shape[1]
    half = keep.shape[1]
    for k in range(3):
        rows = slice(k * middle, (k + 1) * middle)
        total[rows, :] = jnp.zeros((middle, 512), F32)

        def step(m, carry, k=k, rows=rows):
            row = at128(m * 256)
            total[rows, :] += tn_dot(mid_low[pl.ds(row, 256), :], wide[pl.ds(row, 256), k * 512 : (k + 1) * 512])
            return carry

        lax.fori_loop(0, meta[BLOCKS_AT], step, 0)
    total[3 * middle : 3 * middle + classes, :] = lax.dot_general(
        logit_grad[...], pooled[...], (((0,), (0,)), ((), ())), precision=HIGH, preferred_element_type=F32
    )
    total[3 * middle + classes :, :] = jnp.zeros((2 * half - 3 * middle - classes, 512), F32)
    for lane in range(4):
        lanes = slice(lane * 128, (lane + 1) * 128)
        keep[lane] = total[pl.ds(at128(core * half), half), lanes]
        send[lane] = total[pl.ds(at128((1 - core) * half), half), lanes].astype(BF16)


def time_join_kernel(meta, own, got, time_grad, class_grad):
    half = own.shape[1]
    rest = time_grad.shape[0] - half

    def place(first, second):
        for lane in range(4):
            lanes = slice(lane * 128, (lane + 1) * 128)
            time_grad[0:half, lanes] = first[lane].astype(F32)
            time_grad[half:, lanes] = second[lane, 0:rest, :].astype(F32)
            class_grad[:, lanes] = second[lane, rest : rest + class_grad.shape[0], :].astype(F32)

    @pl.when(meta[CORE_AT] == 0)
    def _():
        place(own, got)

    @pl.when(meta[CORE_AT] != 0)
    def _():
        place(got, own)


def mid_grad_kernel(meta, mid_act_grad, mid_pre, belong, merged, gain, sums, whole, keep, send):
    core = meta[CORE_AT]
    center, scale = norm_of(merged)
    shift_part = sums[0:1, :] / merged[0:1, :]
    gain_part = sums[1:2, :] / merged[0:1, :]

    def step(m, carry):
        row = at128(m * 256)
        mask = mask_of(belong, row)
        normed = (mid_pre[pl.ds(row, 256), :] - center) * scale
        inner = mid_act_grad[pl.ds(row, 256), :] - mask * (shift_part + normed * gain_part)
        low = (gain[...] * scale * inner).astype(BF16)
        whole[pl.ds(row, 256), :] = low

        @pl.when(core == 0)
        def _():
            keep[pl.ds(row, 256), 0:512] = low[:, 0:512]
            send[pl.ds(row, 256), 0:512] = low[:, 512:1024]

        @pl.when(core != 0)
        def _():
            keep[pl.ds(row, 256), 0:512] = low[:, 512:1024]
            send[pl.ds(row, 256), 0:512] = low[:, 0:512]

        keep[pl.ds(row, 256), 512:640] = low[:, 1024:1152]
        send[pl.ds(row, 256), 512:640] = low[:, 1024:1152]
        return carry

    lax.fori_loop(0, meta[BLOCKS_AT], step, 0)


def space_grad_kernel(first_tap, meta, turns, stored, own, part, after, keep, send, packed, total, sems):
    core = meta[CORE_AT]
    s = meta[S_AT]
    mine = turns[0]
    copy_out(meta, 6 * meta[BLOCKS_AT], stored, packed, 0, sems, "start")
    copy_out(meta, 6 * meta[BLOCKS_AT], stored, packed, 0, sems, "wait")

    def one(tap, carry):
        i, j = lax.div(first_tap + tap, 3), lax.rem(first_tap + tap, 3)
        total[...] = jnp.zeros(total.shape, F32)
        lanes = pl.ds(at128(j * 512), 512)

        def step(m, carry):
            row = at128(m * 256)
            first = packed[pl.ds(at128((2 * core + i) * s + row), 256), lanes]
            second = packed[pl.ds(at128((2 - 2 * core + i) * s + row), 256), lanes]
            total[...] += tn_dot(own[pl.ds(row, 256), :], first) + tn_dot(part[pl.ds(row, 256), :], second)
            return carry

        lax.fori_loop(0, meta[BLOCKS_AT], step, 0)
        for half, out, kind in ((mine, keep, F32), (1 - mine, send, BF16)):
            lane = half * 256
            out[tap, 0:512, :] = total[0:512, pl.ds(at128(lane), 128)].astype(kind)
            out[tap, 512:1024, :] = total[0:512, pl.ds(at128(lane + 128), 128)].astype(kind)
            out[tap, 1024:1152, :] = total[512:640, pl.ds(at128(core * 256 + half * 128), 128)].astype(kind)
        return carry

    lax.fori_loop(0, keep.shape[0], one, 0)


def halve_kernel(stage, turns, keep, got, after, next_keep, next_send):
    half = next_keep.shape[1]
    mine = turns[stage]

    def one(tap, carry):
        low, high = pl.ds(at16(mine * half), half), pl.ds(at16((1 - mine) * half), half)
        next_keep[tap] = keep[tap, low, :] + got[tap, low, :].astype(F32)
        next_send[tap] = (keep[tap, high, :] + got[tap, high, :].astype(F32)).astype(BF16)
        return carry

    lax.fori_loop(0, keep.shape[0], one, 0)


def share_kernel(keep, got, after, out):
    def one(tap, carry):
        out[tap] = (keep[tap] + got[tap].astype(F32)).astype(BF16)
        return carry

    lax.fori_loop(0, keep.shape[0], one, 0)


def double_kernel(stage, turns, own, got, after, out):
    half = own.shape[1]
    mine = turns[stage]

    def one(tap, carry):
        out[tap, pl.ds(at16(mine * half), half), :] = own[tap]
        out[tap, pl.ds(at16((1 - mine) * half), half), :] = got[tap]
        return carry

    lax.fori_loop(0, own.shape[0], one, 0)


def input_back_kernel(meta, grad, weight_in, pooled, class_weight, after, wide, logits, weight, load):
    s = meta[S_AT]
    fetch = pltpu.make_async_copy(weight_in, weight, load)
    fetch.start()
    logits[...] = jnp.dot(pooled[...], class_weight[...], precision=HIGH, preferred_element_type=F32)
    terms = {0: [(0, 0)], 1: [(0, 1), (1, 0)], 2: [(0, 2), (1, 1)], 3: [(1, 2)]}
    for plane in range(4):
        wide[plane, pl.ds(at128(s), 256), :] = jnp.zeros((256, 1536), BF16)
    fetch.wait()

    def conv(m, carry):
        row = at128(m * 128)
        for plane in range(4):
            acc = None
            for h, i in terms[plane]:
                term = nt_dot(grad[pl.ds(at128(h * s + row), 128), :], weight[i * 1536 : (i + 1) * 1536, :])
                acc = term if acc is None else acc + term
            wide[plane, pl.ds(row, 128), :] = acc.astype(BF16)
        return carry

    lax.fori_loop(0, s // 128, conv, 0)


def spread_kernel(frame_count, meta, col_info, wide, act_grad, after, dense, edges, spread, high, rest):
    s = meta[S_AT]
    info = col_info[...]
    for j in range(3):
        spread[:, j * 256 : (j + 1) * 256] = pick_cols(info, j - 1)

    def cut(m, carry):
        row = at128(m * 256)
        first, second = split(act_grad[pl.ds(row, 256), :])
        high[pl.ds(row, 256), :] = first
        rest[pl.ds(row, 256), :] = second
        return carry

    lax.fori_loop(0, meta[BLOCKS_AT], cut, 0)
    for part in (high, rest):
        part[pl.ds(at128(2 * s), 256), :] = jnp.zeros((256, 512), BF16)
    for plane in range(4):
        for t in range(frame_count):
            row = at16(meta[OFF + t])
            acc = None
            for j in range(3):
                term = dot(spread[:, j * 256 : (j + 1) * 256], wide[plane, pl.ds(row, 256), j * 512 : (j + 1) * 512])
                acc = term if acc is None else acc + term
            if plane == 0:
                edges[0, t] = acc.astype(BF16)
            elif plane == 3:
                edges[1, t] = acc.astype(BF16)
            else:
                row = at16((plane - 1) * s + meta[OFF + t])
                acc += dot(spread[:, 256:512], high[pl.ds(row, 256), :])
                acc += dot(spread[:, 256:512], rest[pl.ds(row, 256), :])
                dense[plane - 1, t] = acc


def join_kernel(meta, turns, own, got, part_own, part_got, *rest):
    out = rest[-1]
    core = meta[CORE_AT]
    mine, other = turns[0], turns[turns.shape[0] - 1]
    for piece, half, owner in (
        (own, mine, core),
        (got, 1 - mine, core),
        (part_own, other, 1 - core),
        (part_got, 1 - other, 1 - core),
    ):
        row = half * 256
        middles = pl.ds(at128(owner * 512), 512)
        out[0, pl.ds(at128(row), 128), middles] = piece[0, 0:512, :].astype(F32).T
        out[0, pl.ds(at128(row + 128), 128), middles] = piece[0, 512:1024, :].astype(F32).T
        out[0, pl.ds(at128(owner * 256 + half * 128), 128), 1024:1152] = piece[0, 1024:1152, :].astype(F32).T


def swap(value, axis, bit):
    size = lax.axis_size(axis)
    if size <= bit:
        return None
    return lax.ppermute(value, axis, [(i, i ^ bit) for i in range(size)])


def bits(axis):
    return [(axis, 1 << n) for n in range((lax.axis_size(axis) - 1).bit_length())]


def sum_all(value):
    for axis, bit in bits("sp") + bits("dp"):
        value = value + swap(value, axis, bit)
    return value


def merge_all(stats):
    stats = stats[:3]
    row = lax.broadcasted_iota(jnp.int32, stats.shape, 0)
    for axis, bit in bits("sp") + bits("dp"):
        other = swap(stats, axis, bit)
        gap = stats[1] / stats[0] - other[1] / other[0]
        extra = gap * gap * (stats[0] * other[0] / (stats[0] + other[0]))
        stats = stats + other + jnp.where(row == 2, extra[None], 0.0)
    return stats


def trade(value, order, stage):
    size = lax.axis_size(("dp", "sp"))
    return lax.ppermute(value, ("dp", "sp"), [(i, i ^ order[i % 2][stage]) for i in range(size)])


def halve_step(keep, send, order, turns, stage, after, name):
    got = trade(send, order, stage)
    n, rows, lanes = keep.shape
    if stage + 1 == len(order[0]):
        share = pl.pallas_call(
            share_kernel,
            out_shape=jax.ShapeDtypeStruct(keep.shape, BF16),
            in_specs=[VM, VM, ANY],
            out_specs=VM,
            compiler_params=params(6),
            name=name + "_share",
        )(keep, got, after)
        return share, None
    half = rows // 2
    if half % 16:
        pairs = (keep + got.astype(F32)).reshape(n, 2, half, lanes)
        mine = turns[stage + 1]
        keep = lax.dynamic_index_in_dim(pairs, mine, 1, keepdims=False)
        send = lax.dynamic_index_in_dim(pairs, 1 - mine, 1, keepdims=False).astype(BF16)
        return keep, send
    return pl.pallas_call(
        functools.partial(halve_kernel, stage + 1),
        out_shape=(
            jax.ShapeDtypeStruct((n, half, lanes), F32),
            jax.ShapeDtypeStruct((n, half, lanes), BF16),
        ),
        in_specs=[SM, VM, VM, ANY],
        out_specs=(VM, VM),
        compiler_params=params(10),
        name=name + "_halve%d" % stage,
    )(turns, keep, got, after)


def double_step(own, order, turns, stage, after, name):
    got = trade(own, order, stage)
    n, rows, lanes = own.shape
    if rows % 16:
        mine = turns[stage]
        return jnp.concatenate([jnp.where(mine == 0, own, got), jnp.where(mine == 0, got, own)], axis=1)
    return pl.pallas_call(
        functools.partial(double_kernel, stage),
        out_shape=jax.ShapeDtypeStruct((n, 2 * rows, lanes), BF16),
        in_specs=[SM, VM, VM, ANY],
        out_specs=VM,
        compiler_params=params(8),
        name=name + "_double%d" % stage,
    )(turns, own, got, after)


def shards(
    clip_input,
    space_weight,
    time_weight,
    gain_mid,
    shift_mid,
    gain_out,
    shift_out,
    class_weight,
    class_bias,
    frames,
    rows,
    cols,
    logit_grad,
):
    clip_count, frame_count, row_count, col_count, width = clip_input.shape
    middle = space_weight.shape[-1]
    classes = class_weight.shape[1]
    cells = clip_count * 8
    most = row_count * frame_count * clip_count * col_count
    sp_count = lax.axis_size("sp")
    core = lax.axis_index("sp") % 2
    row_start = lax.axis_index("sp") * row_count

    before = (frames[None, :] > frames[:, None]) | (
        (frames[None, :] == frames[:, None]) & (jnp.arange(clip_count)[None, :] < jnp.arange(clip_count)[:, None])
    )
    start = jnp.sum(jnp.where(before, cols[None, :], 0), axis=1)
    length = jnp.sum(jnp.where(frames[None, :] > jnp.arange(frame_count)[:, None], cols[None, :], 0), axis=1)
    padded = (length + 15) // 16 * 16
    offset = jnp.cumsum(padded) - padded
    end = jnp.sum(padded)
    plane = (end + 127) // 128 * 128
    meta = jnp.concatenate(
        [jnp.stack([plane, plane // 128, core, row_start]), offset, length, padded, end[None]]
    ).astype(jnp.int32)
    column = jnp.arange(8)[None, :]
    info = jnp.stack(
        [
            start[:, None] + column,
            jnp.broadcast_to(column, (clip_count, 8)),
            jnp.broadcast_to(cols[:, None], (clip_count, 8)),
            jnp.zeros((clip_count, 8), jnp.int32),
        ]
    ).reshape(4, cells)
    by_clip = jnp.zeros((2, cells), jnp.int32).at[:, :clip_count].set(jnp.stack([frames, rows]))
    row_info = jnp.concatenate([info[:3], by_clip, jnp.zeros((3, cells), jnp.int32)]).astype(jnp.int32)
    col_info = jnp.concatenate([info, info], axis=0).T.astype(jnp.int32)

    frame_ok = jnp.arange(frame_count)[None, :] < frames[:, None]
    row_ok = (row_start + jnp.arange(row_count))[None, :] < rows[:, None]
    col_ok = jnp.arange(col_count)[None, :] < cols[:, None]
    mask = (frame_ok[:, :, None, None] & row_ok[:, None, :, None] & col_ok[:, None, None, :])[..., None]
    masked = jnp.where(mask, clip_input, 0.0)
    masked = jnp.pad(masked.transpose(2, 1, 0, 3, 4), ((0, 0), (0, 0), (0, 0), (0, 8 - col_count), (0, 0)))
    masked = masked.reshape(row_count, frame_count, cells, width)
    rounded = lax.reduce_precision(masked, 8, 7)
    own = rounded.astype(BF16)
    own_low = (masked - rounded).astype(BF16)
    part = swap(own, "sp", 1)
    ahead = [(i, i + 1 if i % 2 else i - 1) for i in range(sp_count)]
    outer = lax.ppermute(
        lax.dynamic_index_in_dim(own, core, 0, keepdims=False),
        "sp",
        [(i, j) for i, j in ahead if 0 <= j < sp_count],
    )
    outer_part = swap(outer, "sp", 1)

    weight = in_hbm(space_weight.reshape(9 * width, middle))
    stored_shape = pltpu.HBM((3 * most, 3 * width), BF16)
    pick_scratch = pltpu.VMEM((2, 384, cells), BF16)
    plane_scratch = pltpu.VMEM((most // 2 + 256, 3 * width), BF16)
    plane_sems = pltpu.SemaphoreType.DMA((most // 256,))
    mid_pre, belong, residual, stored = pl.pallas_call(
        space_kernel,
        out_shape=(
            pltpu.VMEM((most, middle), F32),
            pltpu.VMEM((most + 256, 128), BF16),
            pltpu.VMEM((most + 256, width), F32),
            stored_shape,
        ),
        in_specs=[SM, VM, VM, VM, VM, HBM],
        out_specs=(VM, VM, VM, HBM),
        scratch_shapes=[
            pltpu.VMEM((2 * most + 256, 3 * width), BF16),
            pick_scratch,
            pltpu.VMEM((9 * width, middle), BF16),
            pltpu.SemaphoreType.DMA((most // 64,)),
            pltpu.SemaphoreType.DMA(()),
        ],
        compiler_params=params(30),
        name="space_conv",
    )(meta, row_info, own, own_low, part, weight)
    mid_pre, stored, stats = pl.pallas_call(
        space_edge_kernel,
        out_shape=(
            pltpu.VMEM((most, middle), F32),
            stored_shape,
            jax.ShapeDtypeStruct((8, middle), F32),
        ),
        in_specs=[SM, VM, VM, HBM, VM, HBM, VM],
        out_specs=(VM, HBM, VM),
        scratch_shapes=[
            pick_scratch,
            plane_scratch,
            pltpu.VMEM((3 * width, middle), BF16),
            plane_sems,
            pltpu.SemaphoreType.DMA(()),
        ],
        input_output_aliases={2: 0, 3: 1},
        compiler_params=params(13),
        name="space_edge",
    )(meta, row_info, mid_pre, in_hbm(stored), outer, weight, belong)
    stored = pl.pallas_call(
        store_edge_kernel,
        out_shape=stored_shape,
        in_specs=[SM, VM, HBM, VM, ANY],
        out_specs=HBM,
        scratch_shapes=[pick_scratch, plane_scratch, plane_sems],
        input_output_aliases={2: 0},
        compiler_params=params(8),
        name="store_edge",
    )(meta, row_info, in_hbm(stored), outer_part, stats)

    clip_cells = (frames * rows * cols).astype(F32)
    pooled_grad = jnp.dot(logit_grad, class_weight.T, precision=HIGH) / clip_cells[:, None]
    pooled_grad = jnp.pad(pooled_grad, ((0, 128 - clip_count), (0, 0)))

    gain_mid, shift_mid = gain_mid[None], shift_mid[None]
    gain_out, shift_out = gain_out[None], shift_out[None]
    mid_merged = merge_all(stats)
    mid_low, out_pre, stats = pl.pallas_call(
        functools.partial(time_kernel, frame_count),
        out_shape=(
            pltpu.VMEM((most, middle), BF16),
            pltpu.VMEM((most, width), F32),
            jax.ShapeDtypeStruct((8, width), F32),
        ),
        in_specs=[SM, VM, VM, VM, VM, VM, VM],
        out_specs=(VM, VM, VM),
        scratch_shapes=[pltpu.VMEM((most + 256, 3 * middle), BF16)],
        compiler_params=params(24),
        name="time_conv",
    )(meta, mid_pre, belong, mid_merged, gain_mid, shift_mid, time_weight.reshape(3 * middle, width))

    out_merged = merge_all(stats)
    act_grad, stats, pooled_sum = pl.pallas_call(
        act_kernel,
        out_shape=(
            pltpu.VMEM((most, width), F32),
            jax.ShapeDtypeStruct((8, width), F32),
            jax.ShapeDtypeStruct((128, width), F32),
        ),
        in_specs=[SM, VM, VM, VM, VM, VM, VM, VM],
        out_specs=(VM, VM, VM),
        compiler_params=params(6),
        name="act",
    )(meta, out_pre, belong, residual, out_merged, gain_out, shift_out, pooled_grad)

    first = (lax.axis_index("sp") == 0).astype(F32)
    bias_part = jnp.pad(jnp.sum(logit_grad, axis=0) * first, (0, width - classes))
    out_sums = sum_all(jnp.concatenate([stats[:2], bias_part[None]]))
    shift_out_grad, gain_out_grad, class_bias_grad = out_sums[0], out_sums[1], out_sums[2, :classes]
    pooled_own = pooled_sum[:clip_count] / clip_cells[:, None]

    wide, mid_act_grad, stats = pl.pallas_call(
        functools.partial(back_kernel, frame_count),
        out_shape=(
            pltpu.VMEM((most + 256, 3 * width), BF16),
            pltpu.VMEM((most, middle), F32),
            jax.ShapeDtypeStruct((8, middle), F32),
        ),
        in_specs=[SM] + [VM] * 11,
        out_specs=(VM, VM, VM),
        compiler_params=params(10),
        name="time_back",
    )(
        meta, act_grad, out_pre, belong, out_merged, gain_out, out_sums, time_weight, mid_pre, mid_merged,
        gain_mid, shift_mid,
    )

    mid_sums = sum_all(stats[:2])
    shift_mid_grad, gain_mid_grad = mid_sums[0], mid_sums[1]
    mid_grad, keep, send = pl.pallas_call(
        mid_grad_kernel,
        out_shape=(
            pltpu.VMEM((most, middle), BF16),
            pltpu.VMEM((most, 640), BF16),
            pltpu.VMEM((most, 640), BF16),
        ),
        in_specs=[SM] + [VM] * 6,
        out_specs=(VM, VM, VM),
        compiler_params=params(8),
        name="mid_grad",
    )(meta, mid_act_grad, mid_pre, belong, mid_merged, gain_mid, mid_sums)
    other = swap(send, "sp", 1)
    small_half = 2048
    small = pl.pallas_call(
        time_grad_kernel,
        out_shape=(
            jax.ShapeDtypeStruct((4, small_half, 128), F32),
            jax.ShapeDtypeStruct((4, small_half, 128), BF16),
        ),
        in_specs=[SM, VM, VM, VM, VM, ANY],
        out_specs=(VM, VM),
        scratch_shapes=[pltpu.VMEM((2 * small_half, width), F32)],
        compiler_params=params(20),
        name="time_grad",
    )(meta, mid_low, wide, pooled_own, logit_grad, send)

    sp_bits, dp_bits = bits("sp")[1:], bits("dp")
    masks = [bit for _, bit in sp_bits], [bit * sp_count for _, bit in dp_bits]
    x, y, z = masks[0], masks[1][:1], masks[1][1:]
    order = x + y + z, y + x + z
    small_order = [1] + x + z + y, [1] + y + z + x
    place = lax.axis_index(("dp", "sp"))

    def turns_of(order, more=()):
        mine = jnp.where(core == 0, jnp.array(order[0]), jnp.array(order[1]))
        other = jnp.where(core == 0, order[1][0], order[0][0])
        return (place & jnp.concatenate([mine, other[None]]) != 0).astype(jnp.int32)

    turns, small_turns = turns_of(order), turns_of(small_order)

    def space_grad_part(first_tap, taps, after):
        return pl.pallas_call(
            functools.partial(space_grad_kernel, first_tap),
            out_shape=(
                jax.ShapeDtypeStruct((taps, 1152, 128), F32),
                jax.ShapeDtypeStruct((taps, 1152, 128), BF16),
            ),
            in_specs=[SM, SM, HBM, VM, VM, ANY],
            out_specs=(VM, VM),
            scratch_shapes=[
                pltpu.VMEM((3 * most, 3 * width), BF16),
                pltpu.VMEM((640, width), F32),
                pltpu.SemaphoreType.DMA((3 * most // 128,)),
            ],
            compiler_params=params(32),
            name="space_grad",
        )(meta, turns, in_hbm(stored), keep, other, after)

    class Chain:
        def __init__(self, name, state, order, turns):
            self.name, self.state, self.order, self.turns = name, state, order, turns
            self.stage, self.down = 0, True

        def step(self, after):
            if self.down:
                self.state = halve_step(*self.state, self.order, self.turns, self.stage, after, self.name)
                self.stage += 1
                if self.state[1] is None:
                    self.state, self.down, self.stage = self.state[0], False, self.stage - 1
            else:
                self.state = double_step(self.state, self.order, self.turns, self.stage, after, self.name)
                self.stage -= 1
            return self.state[0] if self.down else self.state

    chunks = {"b": (0, 5), "c": (5, 4)}
    chains = {"t": Chain("time", small, small_order, small_turns)}
    after = small[1]
    steps = len(x + y + z)
    left = {"t": 2 * steps + 1, "b": 2 * steps - 1, "c": 2 * steps - 1}
    for event in PLAN + ("t", "b", "c") * (2 * steps):
        if event in left and not left[event]:
            continue
        if event in left:
            left[event] -= 1
        if event in ("space_b", "space_c"):
            name = event[-1]
            chains[name] = Chain("taps" + name, space_grad_part(*chunks[name], after), order, turns)
            after = chains[name].state[1]
        elif event == "back":
            wide, logits = pl.pallas_call(
                input_back_kernel,
                out_shape=(
                    jax.ShapeDtypeStruct((4, most // 2 + 256, 3 * width), BF16),
                    jax.ShapeDtypeStruct((clip_count, classes), F32),
                ),
                in_specs=[SM, VM, HBM, VM, VM, ANY],
                out_specs=(VM, VM),
                scratch_shapes=[pltpu.VMEM((9 * width, middle), BF16), pltpu.SemaphoreType.DMA(())],
                compiler_params=params(36),
                name="input_back",
            )(meta, mid_grad, weight, pooled_own, class_weight, after)
            after = logits
        elif event == "spread":
            dense, edges = pl.pallas_call(
                functools.partial(spread_kernel, frame_count),
                out_shape=(
                    jax.ShapeDtypeStruct((row_count, frame_count, cells, width), F32),
                    jax.ShapeDtypeStruct((2, frame_count, cells, width), BF16),
                ),
                in_specs=[SM, VM, VM, VM, ANY],
                out_specs=(VM, VM),
                scratch_shapes=[
                    pltpu.VMEM((cells, 3 * cells), BF16),
                    pltpu.VMEM((most + 256, width), BF16),
                    pltpu.VMEM((most + 256, width), BF16),
                ],
                compiler_params=params(34),
                name="spread",
            )(meta, col_info, wide, act_grad, after)
            after = edges
        else:
            after = chains[event].step(after)

    space_grad = None
    for name in ("b", "c"):
        first_tap, taps = chunks[name]
        own_half = chains[name].state
        got_half = trade(own_half, order, 0)
        pieces = [own_half, got_half, swap(own_half, "sp", 1), swap(got_half, "sp", 1)]
        piece = pl.BlockSpec((1, 1152, 128), lambda n, meta, turns: (n, 0, 0))
        before = [] if space_grad is None else [space_grad]
        space_grad = pl.pallas_call(
            join_kernel,
            grid_spec=pltpu.PrefetchScalarGridSpec(
                num_scalar_prefetch=2,
                grid=(taps,),
                in_specs=[piece] * 4 + [ANY] * len(before),
                out_specs=pl.BlockSpec((1, width, middle), lambda n, meta, turns, tap=first_tap: (n + tap, 0, 0)),
            ),
            out_shape=jax.ShapeDtypeStruct((9, width, middle), F32),
            input_output_aliases={6: 0} if before else {},
            compiler_params=params(12),
            name="join",
        )(meta, turns, *pieces, *before)
    space_grad = space_grad.reshape(3, 3, width, middle)

    up = lax.ppermute(edges[0], "sp", [(i, i - 1) for i in range(1, sp_count)])
    down = lax.ppermute(edges[1], "sp", [(i, i + 1) for i in range(sp_count - 1)])
    input_grad = dense + jnp.stack([down, up]).astype(F32)
    input_grad = input_grad.reshape(row_count, frame_count, clip_count, 8, width)[:, :, :, :col_count]
    input_grad = jnp.where(mask, input_grad.transpose(2, 1, 0, 3, 4), 0.0)
    for axis, bit in bits("sp"):
        logits = logits + swap(logits, axis, bit)
    logits = logits + class_bias

    own_half = chains["t"].state
    time_grad, class_weight_grad = pl.pallas_call(
        time_join_kernel,
        out_shape=(
            jax.ShapeDtypeStruct((3 * middle, width), F32),
            jax.ShapeDtypeStruct((classes, width), F32),
        ),
        in_specs=[SM, VM, VM],
        out_specs=(VM, VM),
        compiler_params=params(16),
        name="time_join",
    )(meta, own_half, trade(own_half, small_order, 0))
    time_grad = time_grad.reshape(3, middle, width)
    class_weight_grad = class_weight_grad.T
    return (
        logits,
        input_grad,
        space_grad,
        time_grad,
        gain_mid_grad,
        shift_mid_grad,
        gain_out_grad,
        shift_out_grad,
        class_weight_grad,
        class_bias_grad,
    )


def solution(mesh):
    placed = (
        P("dp", None, "sp", None, None),
        P(),
        P(),
        P(),
        P(),
        P(),
        P(),
        P(),
        P(),
        P("dp"),
        P("dp"),
        P("dp"),
        P("dp", None),
    )
    return jax.shard_map(
        shards,
        mesh=mesh,
        in_specs=placed,
        out_specs=(
            P("dp", None),
            P("dp", None, "sp", None, None),
            P(),
            P(),
            P(),
            P(),
            P(),
            P(),
            P(),
            P(),
        ),
        check_vma=False,
    )
```

```python
import functools

import jax
import jax.numpy as jnp
from jax import lax
from jax.experimental import pallas as pl
from jax.experimental.pallas import tpu as pltpu
from jax.sharding import PartitionSpec as P

EPSILON = 1e-05
HIGH = lax.Precision.HIGHEST
F32 = jnp.float32
BF16 = jnp.bfloat16
S_AT, BLOCKS_AT, CORE_AT, ROW_AT, OFF, LEN, PAD, END_AT, FIRST_AT, TURN, SMALL_TURN = 0, 1, 2, 3, 4, 8, 12, 16, 17, 18, 33
META = 48

PLAN = ("space_b", "t", "space_c", "t", "back_0", "t", "b", "back_1", "t", "b", "c") + ("t", "b", "c") * 7

VM = pl.BlockSpec(memory_space=pltpu.VMEM)
SM = pl.BlockSpec(memory_space=pltpu.SMEM)
ANY = pl.BlockSpec(memory_space=pl.ANY)
HBM = pl.BlockSpec(memory_space=pltpu.HBM)


def in_hbm(value):
    return pltpu.with_memory_space_constraint(value, pltpu.HBM)


def params(mib):
    return pltpu.CompilerParams(vmem_limit_bytes=mib << 20)


def nt_dot(a, b):
    return lax.dot_general(a, b, (((1,), (1,)), ((), ())), preferred_element_type=F32)


def tn_dot(a, b):
    return lax.dot_general(a, b, (((0,), (0,)), ((), ())), preferred_element_type=F32)


def dot(a, b):
    return jnp.dot(a, b, preferred_element_type=F32)


def split(value):
    high = value.astype(BF16)
    return high, (value - high.astype(F32)).astype(BF16)


def sigmoid(v):
    return 1.0 / (1.0 + jnp.exp(-v))


def slope(v):
    s = sigmoid(v)
    return s * (1.0 + v * (1.0 - s))


def at16(index):
    return pl.multiple_of(index, 16)


def at128(index):
    return pl.multiple_of(index, 128)


def pick_rows(row_info, shift):
    place, col, cols = row_info[0:1, :], row_info[1:2, :], row_info[2:3, :]
    home = col - shift
    ok = (col < cols) & (home >= 0) & (home < cols)
    spot = jnp.where(ok, place - shift, -1)
    size = row_info.shape[1]
    index = lax.broadcasted_iota(jnp.int32, (size, size), 0)
    return jnp.where(index == spot, 1.0, 0.0).astype(BF16)


def pick_cols(col_info, shift):
    place, col, cols = col_info[:, 0:1], col_info[:, 1:2], col_info[:, 2:3]
    home = col - shift
    ok = (col < cols) & (home >= 0) & (home < cols)
    spot = jnp.where(ok, place - shift, -1)
    size = col_info.shape[0]
    index = lax.broadcasted_iota(jnp.int32, (size, size), 1)
    return jnp.where(index == spot, 1.0, 0.0).astype(BF16)


def each_list(meta, base, frame_count, store):
    for t in range(frame_count):
        for half in range(2):

            @pl.when(half * 128 < meta[PAD + t])
            def _(t=t, half=half):
                store(t, half, at16(base + meta[OFF + t] + half * 128))


def setup_kernel(
    sp_count, orders, where, frames, rows, cols, values, meta, row_info, col_info, clip_info, own, own_low, ahead, pad
):
    row_count, frame_count, clip_count, col_count, width = values.shape
    size = clip_count * 8
    core = lax.rem(where[1], 2)
    first_row = where[1] * row_count
    total = jnp.int32(0)
    for t in range(frame_count):
        length = jnp.int32(0)
        for b in range(clip_count):
            length += jnp.where(frames[b] > t, cols[b], 0)
        padded = (length + 15) // 16 * 16
        meta[OFF + t], meta[LEN + t], meta[PAD + t] = total, length, padded
        total += padded
    plane = (total + 127) // 128 * 128
    meta[S_AT], meta[BLOCKS_AT], meta[CORE_AT], meta[ROW_AT] = plane, plane // 128, core, first_row
    meta[END_AT] = total
    meta[FIRST_AT] = jnp.where(where[1] == 0, 1, 0)
    place = where[0] * sp_count + where[1]
    for start, (order, other) in zip((TURN, SMALL_TURN), orders):
        for n, (zero, one) in enumerate(zip(*order)):
            meta[start + n] = jnp.where(place & jnp.where(core == 0, zero, one) != 0, 1, 0)
        meta[start + len(order[0])] = jnp.where(place & jnp.where(core == 0, other[0], other[1]) != 0, 1, 0)

    lane = lax.broadcasted_iota(jnp.int32, (1, size), 1)
    clip, col = lax.shift_right_logical(lane, 3), lane & 7
    zero = jnp.zeros((1, size), jnp.int32)
    of_cell, of_clip = [zero] * 3, [zero] * 3
    for b in range(clip_count):
        for n, source in enumerate((cols, frames, rows)):
            of_cell[n] = jnp.where(clip == b, source[b], of_cell[n])
            of_clip[n] = jnp.where(lane == b, source[b], of_clip[n])
    start = zero
    for b in range(clip_count):
        ahead_of = (frames[b] > of_cell[1]) | ((frames[b] == of_cell[1]) & (clip > b))
        start += jnp.where(ahead_of, cols[b], 0)
    info = [start + col, col, of_cell[0], of_cell[1], of_cell[2], zero, zero, zero]
    for n, line in enumerate(info[:3] + of_clip[1:] + [zero] * 3):
        row_info[n : n + 1, :] = line
    col_info[...] = jnp.concatenate(info, axis=0).astype(F32).T.astype(jnp.int32)
    per_clip = jnp.maximum(of_clip[0] * of_clip[1] * of_clip[2], 1).astype(F32)[:, 0:128]
    clip_info[...] = jnp.concatenate([per_clip] * 8, axis=0).T

    pad[:, col_count:, :] = jnp.zeros((clip_count, 8 - col_count, width), F32)
    cells = col_info[...]
    for h in range(row_count):
        for t in range(frame_count):
            pad[:, 0:col_count, :] = values[h, t]
            inside = (cells[:, 1:2] < cells[:, 2:3]) & (cells[:, 3:4] > t) & (cells[:, 4:5] > first_row + h)
            masked = pad[...].reshape(size, width) * jnp.where(inside, 1.0, 0.0)
            own[h, t], own_low[h, t] = split(masked)

            @pl.when(core == h)
            def _(t=t, masked=masked):
                ahead[t] = masked.astype(BF16)


def gather_setup(row_info, pick):
    info = row_info[...]
    for j in range(3):
        hot = pick_rows(info, j - 1)
        for half in range(2):
            pick[half, j * 128 : (j + 1) * 128, :] = hot[half * 128 : (half + 1) * 128, :]


def gather_plane(meta, pick, source, packed, base, frame_count):
    def store(t, half, row):
        got = dot(pick[half], source(t)).astype(BF16)
        for j in range(3):
            packed[pl.ds(row, 128), j * 512 : (j + 1) * 512] = got[j * 128 : (j + 1) * 128, :]

    each_list(meta, base, frame_count, store)
    packed[pl.ds(at16(base + meta[END_AT]), 128), :] = jnp.zeros((128, 1536), BF16)


def copy_out(blocks, source, begin, target, start, sems, action):
    def one(m, carry):
        copy = pltpu.make_async_copy(
            source.at[pl.ds(at128(begin + m * 128), 128)], target.at[pl.ds(at128(start + m * 128), 128)], sems.at[m]
        )
        if action == "start":
            copy.start()
        else:
            copy.wait()
        return carry

    lax.fori_loop(0, blocks, one, 0)


def space_kernel(
    meta, row_info, own, own_low, part, weight_in, logit_grad, class_weight, clip_info,
    mid_pre, belong, residual, stored, pooled_grad, bias_grad, packed, pick, weight, sems, load,
):
    frame_count = own.shape[1]
    core = meta[CORE_AT]
    s = meta[S_AT]
    blocks = meta[BLOCKS_AT]
    fetch = pltpu.make_async_copy(weight_in, weight, load)
    fetch.start()
    gather_setup(row_info, pick)

    @pl.when(core == 0)
    def _():
        for h in range(2):
            gather_plane(meta, pick, lambda t, h=h: own[h, t], packed, h * s, frame_count)
        for h in range(2):
            gather_plane(meta, pick, lambda t, h=h: part[h, t], packed, (2 + h) * s, frame_count)

    @pl.when(core != 0)
    def _():
        for h in range(2):
            gather_plane(meta, pick, lambda t, h=h: part[h, t], packed, h * s, frame_count)
        for h in range(2):
            gather_plane(meta, pick, lambda t, h=h: own[h, t], packed, (2 + h) * s, frame_count)

    copy_out(4 * blocks, packed, 0, stored, s, sems, "start")
    size = row_info.shape[1]
    clip_of = lax.broadcasted_iota(jnp.int32, (size, 128), 0) // 8
    lane = lax.broadcasted_iota(jnp.int32, (size, 128), 1)
    frames_of = jnp.broadcast_to(row_info[3:4, 0:128], (size, 128))
    rows_of = jnp.broadcast_to(row_info[4:5, 0:128], (size, 128))
    for h in range(2):

        def store(t, half, row, h=h):
            hot = pick[half, 128:256, :]
            inside = (clip_of == lane) & (frames_of > t) & (rows_of > meta[ROW_AT] + h)
            belong[pl.ds(row, 128), :] = dot(hot, jnp.where(inside, 1.0, 0.0).astype(BF16)).astype(BF16)
            residual[pl.ds(row, 128), :] = dot(hot, own[h, t]) + dot(hot, own_low[h, t])

        each_list(meta, h * s, frame_count, store)
        belong[pl.ds(at16(h * s + meta[END_AT]), 128), :] = jnp.zeros((128, 128), BF16)
        residual[pl.ds(at16(h * s + meta[END_AT]), 128), :] = jnp.zeros((128, 512), F32)
    clips, classes = logit_grad.shape
    pooled_grad[...] = jnp.zeros(pooled_grad.shape, F32)
    pooled_grad[0:clips, :] = (
        jnp.dot(logit_grad[...], class_weight[...], precision=HIGH, preferred_element_type=F32)
        / clip_info[0:clips, 0:1]
    )
    bias_grad[...] = jnp.zeros(bias_grad.shape, F32)
    bias_grad[:, 0:classes] = jnp.sum(logit_grad[...], axis=0, keepdims=True) * meta[FIRST_AT].astype(F32)
    fetch.wait()
    for h in range(2):

        def conv(m, carry, h=h):
            row = at128(h * s + m * 128)

            def tap(i):
                source = packed[pl.ds(at128((2 * core + h + i - 1) * s + m * 128), 128), :]
                return dot(source, weight[i * 1536 : (i + 1) * 1536, :])

            mid_pre[pl.ds(row, 128), :] = tap(1) + tap(2 - 2 * h)

            @pl.when(core == 1 - h)
            def _():
                mid_pre[pl.ds(row, 128), :] += tap(2 * h)

            return carry

        lax.fori_loop(0, blocks, conv, 0)
    copy_out(4 * blocks, packed, 0, stored, s, sems, "wait")


def mask_of(belong, row, size=256):
    return jnp.sum(belong[pl.ds(row, size), :].astype(F32), axis=1, keepdims=True)


def norm_of(merged):
    count = merged[0:1, :]
    return merged[1:2, :] / count, lax.rsqrt(merged[2:3, :] / count + EPSILON)


def norm_sums(meta, values, belong, stats):
    width = values.shape[1]

    def sums(m, total):
        row = at128(m * 256)
        mask = mask_of(belong, row)
        return (
            total[0] + jnp.sum(mask, axis=0, keepdims=True),
            total[1] + jnp.sum(values[pl.ds(row, 256), :] * mask, axis=0, keepdims=True),
        )

    count, total = lax.fori_loop(
        0, meta[BLOCKS_AT], sums, (jnp.zeros((1, 1), F32), jnp.zeros((1, width), F32))
    )
    center = total / count

    def spread(m, squares):
        row = at128(m * 256)
        off = (values[pl.ds(row, 256), :] - center) * mask_of(belong, row)
        return squares + jnp.sum(off * off, axis=0, keepdims=True)

    squares = lax.fori_loop(0, meta[BLOCKS_AT], spread, jnp.zeros((1, width), F32))
    stats[0:1, :] = jnp.broadcast_to(count, (1, width))
    stats[1:2, :] = total
    stats[2:3, :] = squares


def space_edge_kernel(
    meta, row_info, mid_in, stored_in, outer, weight_in, belong, mid_pre, stored, stats, pick, plane, weight, sems, load
):
    core = meta[CORE_AT]
    s = meta[S_AT]
    blocks = meta[BLOCKS_AT]
    fetch = pltpu.make_async_copy(
        weight_in.at[pl.ds(pl.multiple_of(core * 3072, 1024), 1536)], weight, load
    )
    fetch.start()
    gather_setup(row_info, pick)
    gather_plane(meta, pick, lambda t: outer[t], plane, 0, outer.shape[0])
    copy_out(blocks, plane, 0, stored, 5 * s * core, sems, "start")
    fetch.wait()

    def conv(m, carry):
        row = at128(core * s + m * 128)
        mid_pre[pl.ds(row, 128), :] += dot(plane[pl.ds(at128(m * 128), 128), :], weight[...])
        return carry

    lax.fori_loop(0, blocks, conv, 0)
    norm_sums(meta, mid_pre, belong, stats)
    copy_out(blocks, plane, 0, stored, 5 * s * core, sems, "wait")


def shift_lists(meta, frame_count, source, target, width, move):
    s = meta[S_AT]
    for h in range(2):

        def store(t, half, row, h=h):
            other = t + move
            if 0 <= other < frame_count:
                block = source(at16(h * s + meta[OFF + other] + half * 128))
                place = half * 128 + lax.broadcasted_iota(jnp.int32, (128, 1), 0)
                keep = jnp.where(place < meta[LEN + other], 1.0, 0.0).astype(BF16)
                target(row, block * keep)
            else:
                target(row, jnp.zeros((128, width), BF16))

        each_list(meta, h * s, frame_count, store)
        target(at16(h * s + meta[END_AT]), jnp.zeros((128, width), BF16))


def time_kernel(frame_count, meta, mid_pre, belong, merged, gain, shift, weight, mid_low, out_pre, stats, wide):
    blocks = meta[BLOCKS_AT]
    center, scale = norm_of(merged)

    def act(m, carry):
        row = at128(m * 256)
        mask = mask_of(belong, row)
        normed = (mid_pre[pl.ds(row, 256), :] - center) * scale
        value = gain[...] * normed + shift[...]
        low = (value * sigmoid(value) * mask).astype(BF16)
        wide[pl.ds(row, 256), 1152:2304] = low
        mid_low[pl.ds(row, 256), :] = low
        return carry

    lax.fori_loop(0, blocks, act, 0)
    wide[pl.ds(at128(2 * meta[S_AT]), 256), :] = jnp.zeros((256, 3456), BF16)
    for k in (0, 2):

        def source(row):
            return wide[pl.ds(row, 128), 1152:2304]

        def target(row, value, k=k):
            wide[pl.ds(row, 128), k * 1152 : (k + 1) * 1152] = value

        shift_lists(meta, frame_count, source, target, 1152, k - 1)

    def conv(m, carry):
        row = at128(m * 256)
        out_pre[pl.ds(row, 256), :] = dot(wide[pl.ds(row, 256), :], weight[...])
        return carry

    lax.fori_loop(0, blocks, conv, 0)
    norm_sums(meta, out_pre, belong, stats)


def act_kernel(
    meta, out_pre, belong, residual, merged, gain_ref, shift_ref, pooled_grad, bias_grad, clip_info,
    act_grad, stats, pooled,
):
    blocks = meta[BLOCKS_AT]
    center, scale = norm_of(merged)
    high, rest = split(pooled_grad[...])
    pooled[...] = jnp.zeros(pooled.shape, F32)

    def step(m, total):
        row = at128(m * 256)
        hot = belong[pl.ds(row, 256), :]
        normed = (out_pre[pl.ds(row, 256), :] - center) * scale
        value = gain_ref[...] * normed + shift_ref[...] + residual[pl.ds(row, 256), :]
        s = sigmoid(value)
        first, second = split(value * s)
        pooled[...] += tn_dot(hot, first) + tn_dot(hot, second)
        grad = (dot(hot, high) + dot(hot, rest)) * (s * (1.0 + value * (1.0 - s)))
        act_grad[pl.ds(row, 256), :] = grad
        shift, gain = total
        return (
            shift + jnp.sum(grad, axis=0, keepdims=True),
            gain + jnp.sum(grad * normed, axis=0, keepdims=True),
        )

    zero = jnp.zeros((1, 512), F32)
    shift, gain = lax.fori_loop(0, blocks, step, (zero, zero))
    stats[0:1, :] = shift
    stats[1:2, :] = gain
    stats[2:3, :] = bias_grad[...]
    pooled[...] = pooled[...] / clip_info[:, 0:1]


def back_kernel(
    frame_count, meta, act_grad, out_pre, belong, out_merged, out_gain, out_sums, weight, mid_pre, mid_merged,
    mid_gain, mid_shift, wide, mid_act_grad, stats,
):
    blocks = meta[BLOCKS_AT]
    out_center, out_scale = norm_of(out_merged)
    mid_center, mid_scale = norm_of(mid_merged)
    out_shift_part = out_sums[0:1, :] / out_merged[0:1, :]
    out_gain_part = out_sums[1:2, :] / out_merged[0:1, :]

    def grad(m, carry):
        row = at128(m * 256)
        mask = mask_of(belong, row)
        normed = (out_pre[pl.ds(row, 256), :] - out_center) * out_scale
        inner = act_grad[pl.ds(row, 256), :] - mask * (out_shift_part + normed * out_gain_part)
        wide[pl.ds(row, 256), 512:1024] = (out_gain[...] * out_scale * inner).astype(BF16)
        return carry

    lax.fori_loop(0, blocks, grad, 0)
    wide[pl.ds(at128(2 * meta[S_AT]), 256), :] = jnp.zeros((256, 1536), BF16)
    for k in (0, 2):

        def source(row):
            return wide[pl.ds(row, 128), 512:1024]

        def target(row, value, k=k):
            wide[pl.ds(row, 128), k * 512 : (k + 1) * 512] = value

        shift_lists(meta, frame_count, source, target, 512, 1 - k)

    def conv(m, total):
        row = at128(m * 256)
        block = wide[pl.ds(row, 256), :]
        acc = nt_dot(block[:, 0:512], weight[0])
        acc += nt_dot(block[:, 512:1024], weight[1])
        acc += nt_dot(block[:, 1024:1536], weight[2])
        mask = mask_of(belong, row)
        normed = (mid_pre[pl.ds(row, 256), :] - mid_center) * mid_scale
        acc = acc * mask * slope(mid_gain[...] * normed + mid_shift[...])
        mid_act_grad[pl.ds(row, 256), :] = acc
        shift, gain = total
        return (
            shift + jnp.sum(acc, axis=0, keepdims=True),
            gain + jnp.sum(acc * normed, axis=0, keepdims=True),
        )

    zero = jnp.zeros((1, 1152), F32)
    shift, gain = lax.fori_loop(0, blocks, conv, (zero, zero))
    stats[0:1, :] = shift
    stats[1:2, :] = gain


def time_grad_kernel(meta, mid_low, wide, pooled, logit_grad, after, keep, send, total):
    core = meta[CORE_AT]
    middle = mid_low.shape[1]
    classes = logit_grad.shape[1]
    half = keep.shape[1]
    for k in range(3):
        rows = slice(k * middle, (k + 1) * middle)
        total[rows, :] = jnp.zeros((middle, 512), F32)

        def step(m, carry, k=k, rows=rows):
            row = at128(m * 256)
            total[rows, :] += tn_dot(mid_low[pl.ds(row, 256), :], wide[pl.ds(row, 256), k * 512 : (k + 1) * 512])
            return carry

        lax.fori_loop(0, meta[BLOCKS_AT], step, 0)
    total[3 * middle : 3 * middle + classes, :] = lax.dot_general(
        logit_grad[...], pooled[0 : logit_grad.shape[0], :], (((0,), (0,)), ((), ())), precision=HIGH, preferred_element_type=F32
    )
    total[3 * middle + classes :, :] = jnp.zeros((2 * half - 3 * middle - classes, 512), F32)
    for lane in range(4):
        lanes = slice(lane * 128, (lane + 1) * 128)
        keep[lane] = total[pl.ds(at128(core * half), half), lanes]
        send[lane] = total[pl.ds(at128((1 - core) * half), half), lanes].astype(BF16)


def time_join_kernel(meta, own, got, time_grad, class_grad):
    half = own.shape[1]
    rest = time_grad.shape[0] - half

    def place(first, second):
        for lane in range(4):
            lanes = slice(lane * 128, (lane + 1) * 128)
            time_grad[0:half, lanes] = first[lane].astype(F32)
            time_grad[half:, lanes] = second[lane, 0:rest, :].astype(F32)
            class_grad[:, lanes] = second[lane, rest : rest + class_grad.shape[0], :].astype(F32)

    @pl.when(meta[CORE_AT] == 0)
    def _():
        place(own, got)

    @pl.when(meta[CORE_AT] != 0)
    def _():
        place(got, own)


def mid_grad_kernel(meta, mid_act_grad, mid_pre, belong, merged, gain, sums, whole, keep, send):
    core = meta[CORE_AT]
    center, scale = norm_of(merged)
    shift_part = sums[0:1, :] / merged[0:1, :]
    gain_part = sums[1:2, :] / merged[0:1, :]

    def step(m, carry):
        row = at128(m * 256)
        mask = mask_of(belong, row)
        normed = (mid_pre[pl.ds(row, 256), :] - center) * scale
        inner = mid_act_grad[pl.ds(row, 256), :] - mask * (shift_part + normed * gain_part)
        low = (gain[...] * scale * inner).astype(BF16)
        whole[pl.ds(row, 256), :] = low

        @pl.when(core == 0)
        def _():
            keep[pl.ds(row, 256), 0:512] = low[:, 0:512]
            send[pl.ds(row, 256), 0:512] = low[:, 512:1024]

        @pl.when(core != 0)
        def _():
            keep[pl.ds(row, 256), 0:512] = low[:, 512:1024]
            send[pl.ds(row, 256), 0:512] = low[:, 0:512]

        keep[pl.ds(row, 256), 512:640] = low[:, 1024:1152]
        send[pl.ds(row, 256), 512:640] = low[:, 1024:1152]
        return carry

    lax.fori_loop(0, meta[BLOCKS_AT], step, 0)


def space_grad_kernel(first_tap, meta, packed, own, part, keep, send, total):
    core = meta[CORE_AT]
    s = meta[S_AT]
    mine = meta[TURN]

    def one(tap, carry):
        i, j = lax.div(first_tap + tap, 3), lax.rem(first_tap + tap, 3)
        lanes = pl.ds(at128(j * 512), 512)

        def both(m):
            row = at128(m * 256)
            first = packed[pl.ds(at128((2 * core + i) * s + row), 256), lanes]
            second = packed[pl.ds(at128((2 - 2 * core + i) * s + row), 256), lanes]
            return tn_dot(own[pl.ds(row, 256), :], first) + tn_dot(part[pl.ds(row, 256), :], second)

        total[...] = both(0)

        def step(m, carry):
            total[...] += both(m)
            return carry

        lax.fori_loop(1, meta[BLOCKS_AT], step, 0)
        for half, out, kind in ((mine, keep, F32), (1 - mine, send, BF16)):
            lane = half * 256
            out[tap, 0:512, :] = total[0:512, pl.ds(at128(lane), 128)].astype(kind)
            out[tap, 512:1024, :] = total[0:512, pl.ds(at128(lane + 128), 128)].astype(kind)
            out[tap, 1024:1152, :] = total[512:640, pl.ds(at128(core * 256 + half * 128), 128)].astype(kind)
        return carry

    lax.fori_loop(0, keep.shape[0], one, 0)


def space_grad_first_kernel(
    first_tap, meta, row_info, stored, outer, own, part, after, keep, send, packed, total, pick, plane, sems
):
    core = meta[CORE_AT]
    s = meta[S_AT]
    blocks = meta[BLOCKS_AT]
    copy_out(5 * blocks, stored, core * s, packed, core * s, sems, "start")
    gather_setup(row_info, pick)
    gather_plane(meta, pick, lambda t: outer[t], plane, 0, outer.shape[0])

    def put(m, carry):
        row = at128(m * 128)
        packed[pl.ds(at128(5 * s * (1 - core) + row), 128), :] = plane[pl.ds(row, 128), :]
        return carry

    lax.fori_loop(0, blocks, put, 0)
    copy_out(5 * blocks, stored, core * s, packed, core * s, sems, "wait")
    space_grad_kernel(first_tap, meta, packed, own, part, keep, send, total)


def halve_kernel(at, meta, keep, got, after, next_keep, next_send):
    half = next_keep.shape[1]
    mine = meta[at]

    def one(tap, carry):
        low, high = pl.ds(at16(mine * half), half), pl.ds(at16((1 - mine) * half), half)
        next_keep[tap] = keep[tap, low, :] + got[tap, low, :].astype(F32)
        next_send[tap] = (keep[tap, high, :] + got[tap, high, :].astype(F32)).astype(BF16)
        return carry

    lax.fori_loop(0, keep.shape[0], one, 0)


def share_kernel(keep, got, after, out):
    def one(tap, carry):
        out[tap] = (keep[tap] + got[tap].astype(F32)).astype(BF16)
        return carry

    lax.fori_loop(0, keep.shape[0], one, 0)


def double_kernel(at, meta, own, got, after, out):
    half = own.shape[1]
    mine = meta[at]

    def one(tap, carry):
        out[tap, pl.ds(at16(mine * half), half), :] = own[tap]
        out[tap, pl.ds(at16((1 - mine) * half), half), :] = got[tap]
        return carry

    lax.fori_loop(0, own.shape[0], one, 0)


def input_back_kernel(
    side, frame_count, meta, col_info, grad, weight_in, act_grad, pooled, class_weight, after,
    dense, edge, logits, weight, wide, spread, high, rest, load,
):
    s = meta[S_AT]
    fetch = pltpu.make_async_copy(weight_in.at[pl.ds(side * 1536, 3072)], weight, load)
    fetch.start()
    if side == 0:
        logits[...] = lax.dot_general(
            pooled[0 : logits.shape[0], :],
            class_weight[...],
            (((1,), (1,)), ((), ())),
            precision=HIGH,
            preferred_element_type=F32,
        )
    else:
        logits[...] = jnp.zeros(logits.shape, F32)
    info = col_info[...]
    for j in range(3):
        spread[:, j * 256 : (j + 1) * 256] = pick_cols(info, j - 1)

    def cut(m, carry):
        row = at128(m * 128)
        first, second = split(act_grad[pl.ds(at128(side * s + row), 128), :])
        high[pl.ds(row, 128), :] = first
        rest[pl.ds(row, 128), :] = second
        return carry

    lax.fori_loop(0, meta[BLOCKS_AT], cut, 0)
    for part in (high, rest):
        part[pl.ds(at128(s), 256), :] = jnp.zeros((256, 512), BF16)
    for plane in range(2):
        wide[plane, pl.ds(at128(s), 256), :] = jnp.zeros((256, 1536), BF16)
    fetch.wait()
    edge_terms, inner_terms = ([(0, 0)], [(0, 1), (1, 0)]) if side == 0 else ([(1, 2)], [(0, 2), (1, 1)])

    def conv(m, carry):
        row = at128(m * 128)
        for plane, terms in enumerate((edge_terms, inner_terms)):
            acc = None
            for h, i in terms:
                source = grad[pl.ds(at128(h * s + row), 128), :]
                term = nt_dot(source, weight[(i - side) * 1536 : (i - side + 1) * 1536, :])
                acc = term if acc is None else acc + term
            wide[plane, pl.ds(row, 128), :] = acc.astype(BF16)
        return carry

    lax.fori_loop(0, meta[BLOCKS_AT], conv, 0)
    for plane in range(2):
        for t in range(frame_count):
            rows = pl.ds(at16(meta[OFF + t]), 256)
            acc = None
            for j in range(3):
                term = dot(spread[:, j * 256 : (j + 1) * 256], wide[plane, rows, j * 512 : (j + 1) * 512])
                acc = term if acc is None else acc + term
            if plane == 0:
                edge[t] = acc.astype(BF16)
            else:
                acc += dot(spread[:, 256:512], high[rows, :]) + dot(spread[:, 256:512], rest[rows, :])
                dense[t] = acc


def join_kernel(steps, meta, own, got, part_own, part_got, *rest):
    out = rest[-1]
    core = meta[CORE_AT]
    mine, other = meta[TURN], meta[TURN + steps]
    for piece, half, owner in (
        (own, mine, core),
        (got, 1 - mine, core),
        (part_own, other, 1 - core),
        (part_got, 1 - other, 1 - core),
    ):
        row = half * 256
        middles = pl.ds(at128(owner * 512), 512)
        out[0, pl.ds(at128(row), 128), middles] = piece[0, 0:512, :].astype(F32).T
        out[0, pl.ds(at128(row + 128), 128), middles] = piece[0, 512:1024, :].astype(F32).T
        out[0, pl.ds(at128(owner * 256 + half * 128), 128), 1024:1152] = piece[0, 1024:1152, :].astype(F32).T


def swap(value, axis, bit):
    size = lax.axis_size(axis)
    if size <= bit:
        return None
    return lax.ppermute(value, axis, [(i, i ^ bit) for i in range(size)])


def bits(axis):
    return [(axis, 1 << n) for n in range((lax.axis_size(axis) - 1).bit_length())]


def sum_all(value):
    for axis, bit in bits("sp") + bits("dp"):
        value = value + swap(value, axis, bit)
    return value


def merge_all(stats):
    stats = stats[:3]
    row = lax.broadcasted_iota(jnp.int32, stats.shape, 0)
    for axis, bit in bits("sp") + bits("dp"):
        other = swap(stats, axis, bit)
        gap = stats[1] / stats[0] - other[1] / other[0]
        extra = gap * gap * (stats[0] * other[0] / (stats[0] + other[0]))
        stats = stats + other + jnp.where(row == 2, extra[None], 0.0)
    return stats


def trade(value, order, stage):
    size = lax.axis_size(("dp", "sp"))
    return lax.ppermute(value, ("dp", "sp"), [(i, i ^ order[i % 2][stage]) for i in range(size)])


def halve_step(keep, send, order, meta, at, stage, after, name):
    got = trade(send, order, stage)
    n, rows, lanes = keep.shape
    if stage + 1 == len(order[0]):
        share = pl.pallas_call(
            share_kernel,
            out_shape=jax.ShapeDtypeStruct(keep.shape, BF16),
            in_specs=[VM, VM, ANY],
            out_specs=VM,
            compiler_params=params(6),
            name=name + "_share",
        )(keep, got, after)
        return share, None
    half = rows // 2
    if half % 16:
        pairs = (keep + got.astype(F32)).reshape(n, 2, half, lanes)
        mine = meta[at + stage + 1]
        keep = lax.dynamic_index_in_dim(pairs, mine, 1, keepdims=False)
        send = lax.dynamic_index_in_dim(pairs, 1 - mine, 1, keepdims=False).astype(BF16)
        return keep, send
    return pl.pallas_call(
        functools.partial(halve_kernel, at + stage + 1),
        out_shape=(
            jax.ShapeDtypeStruct((n, half, lanes), F32),
            jax.ShapeDtypeStruct((n, half, lanes), BF16),
        ),
        in_specs=[SM, VM, VM, ANY],
        out_specs=(VM, VM),
        compiler_params=params(10),
        name=name + "_halve%d" % stage,
    )(meta, keep, got, after)


def double_step(own, order, meta, at, stage, after, name):
    got = trade(own, order, stage)
    n, rows, lanes = own.shape
    if rows % 16:
        mine = meta[at + stage]
        return jnp.concatenate([jnp.where(mine == 0, own, got), jnp.where(mine == 0, got, own)], axis=1)
    return pl.pallas_call(
        functools.partial(double_kernel, at + stage),
        out_shape=jax.ShapeDtypeStruct((n, 2 * rows, lanes), BF16),
        in_specs=[SM, VM, VM, ANY],
        out_specs=VM,
        compiler_params=params(8),
        name=name + "_double%d" % stage,
    )(meta, own, got, after)


def shards(
    clip_input,
    space_weight,
    time_weight,
    gain_mid,
    shift_mid,
    gain_out,
    shift_out,
    class_weight,
    class_bias,
    frames,
    rows,
    cols,
    logit_grad,
):
    clip_count, frame_count, row_count, col_count, width = clip_input.shape
    middle = space_weight.shape[-1]
    classes = class_weight.shape[1]
    cells = clip_count * 8
    most = row_count * frame_count * clip_count * col_count
    sp_count = lax.axis_size("sp")
    x = [bit for _, bit in bits("sp")[1:]]
    y, z = [[bit * sp_count for _, bit in part] for part in (bits("dp")[:1], bits("dp")[1:])]
    order = x + y + z, y + x + z
    small_order = [1] + x + z + y, [1] + y + z + x
    steps = len(order[0])
    orders = (order, (order[1][0], order[0][0])), (small_order, (1, 1))
    place = jnp.stack([lax.axis_index("dp"), lax.axis_index("sp")]).astype(jnp.int32)
    cells_shape = (row_count, frame_count, cells, width)
    meta, row_info, col_info, clip_info, own, own_low, ahead = pl.pallas_call(
        functools.partial(setup_kernel, sp_count, orders),
        out_shape=(
            jax.ShapeDtypeStruct((META,), jnp.int32),
            jax.ShapeDtypeStruct((8, cells), jnp.int32),
            jax.ShapeDtypeStruct((cells, 8), jnp.int32),
            jax.ShapeDtypeStruct((128, 8), F32),
            jax.ShapeDtypeStruct(cells_shape, BF16),
            jax.ShapeDtypeStruct(cells_shape, BF16),
            jax.ShapeDtypeStruct(cells_shape[1:], BF16),
        ),
        in_specs=[SM, SM, SM, SM, VM],
        out_specs=(SM, VM, VM, VM, VM, VM, VM),
        scratch_shapes=[pltpu.VMEM((clip_count, 8, width), F32)],
        compiler_params=params(20),
        name="setup",
    )(place, frames, rows, cols, clip_input.transpose(2, 1, 0, 3, 4))
    class_lines = class_weight.T

    part = swap(own, "sp", 1)
    across = [(i, i + 1 if i % 2 else i - 1) for i in range(sp_count)]
    outer = lax.ppermute(ahead, "sp", [(i, j) for i, j in across if 0 <= j < sp_count])
    outer_part = swap(outer, "sp", 1)

    weight = in_hbm(space_weight.reshape(9 * width, middle))
    stored_shape = pltpu.HBM((3 * most, 3 * width), BF16)
    pick_scratch = pltpu.VMEM((2, 384, cells), BF16)
    plane_scratch = pltpu.VMEM((most // 2 + 256, 3 * width), BF16)
    plane_sems = pltpu.SemaphoreType.DMA((most // 256,))
    mid_pre, belong, residual, stored, pooled_grad, bias_grad = pl.pallas_call(
        space_kernel,
        out_shape=(
            pltpu.VMEM((most, middle), F32),
            pltpu.VMEM((most + 256, 128), BF16),
            pltpu.VMEM((most + 256, width), F32),
            stored_shape,
            pltpu.VMEM((128, width), F32),
            pltpu.VMEM((1, width), F32),
        ),
        in_specs=[SM, VM, VM, VM, VM, HBM, VM, VM, VM],
        out_specs=(VM, VM, VM, HBM, VM, VM),
        scratch_shapes=[
            pltpu.VMEM((2 * most + 256, 3 * width), BF16),
            pick_scratch,
            pltpu.VMEM((9 * width, middle), BF16),
            pltpu.SemaphoreType.DMA((most // 64,)),
            pltpu.SemaphoreType.DMA(()),
        ],
        compiler_params=params(30),
        name="space_conv",
    )(meta, row_info, own, own_low, part, weight, logit_grad, class_lines, clip_info)
    mid_pre, stored, stats = pl.pallas_call(
        space_edge_kernel,
        out_shape=(
            pltpu.VMEM((most, middle), F32),
            stored_shape,
            jax.ShapeDtypeStruct((3, middle), F32),
        ),
        in_specs=[SM, VM, VM, HBM, VM, HBM, VM],
        out_specs=(VM, HBM, VM),
        scratch_shapes=[
            pick_scratch,
            plane_scratch,
            pltpu.VMEM((3 * width, middle), BF16),
            plane_sems,
            pltpu.SemaphoreType.DMA(()),
        ],
        input_output_aliases={2: 0, 3: 1},
        compiler_params=params(13),
        name="space_edge",
    )(meta, row_info, mid_pre, in_hbm(stored), outer, weight, belong)
    gain_mid, shift_mid = gain_mid[None], shift_mid[None]
    gain_out, shift_out = gain_out[None], shift_out[None]
    mid_merged = merge_all(stats)
    mid_low, out_pre, stats = pl.pallas_call(
        functools.partial(time_kernel, frame_count),
        out_shape=(
            pltpu.VMEM((most, middle), BF16),
            pltpu.VMEM((most, width), F32),
            jax.ShapeDtypeStruct((3, width), F32),
        ),
        in_specs=[SM, VM, VM, VM, VM, VM, VM],
        out_specs=(VM, VM, VM),
        scratch_shapes=[pltpu.VMEM((most + 256, 3 * middle), BF16)],
        compiler_params=params(24),
        name="time_conv",
    )(meta, mid_pre, belong, mid_merged, gain_mid, shift_mid, time_weight.reshape(3 * middle, width))

    out_merged = merge_all(stats)
    act_grad, stats, pooled = pl.pallas_call(
        act_kernel,
        out_shape=(
            pltpu.VMEM((most, width), F32),
            jax.ShapeDtypeStruct((3, width), F32),
            jax.ShapeDtypeStruct((128, width), F32),
        ),
        in_specs=[SM] + [VM] * 9,
        out_specs=(VM, VM, VM),
        compiler_params=params(6),
        name="act",
    )(meta, out_pre, belong, residual, out_merged, gain_out, shift_out, pooled_grad, bias_grad, clip_info)

    out_sums = sum_all(stats)
    shift_out_grad, gain_out_grad, class_bias_grad = out_sums[0], out_sums[1], out_sums[2, :classes]
    wide, mid_act_grad, stats = pl.pallas_call(
        functools.partial(back_kernel, frame_count),
        out_shape=(
            pltpu.VMEM((most + 256, 3 * width), BF16),
            pltpu.VMEM((most, middle), F32),
            jax.ShapeDtypeStruct((2, middle), F32),
        ),
        in_specs=[SM] + [VM] * 11,
        out_specs=(VM, VM, VM),
        compiler_params=params(10),
        name="time_back",
    )(
        meta, act_grad, out_pre, belong, out_merged, gain_out, out_sums, time_weight, mid_pre, mid_merged,
        gain_mid, shift_mid,
    )

    mid_sums = sum_all(stats)
    shift_mid_grad, gain_mid_grad = mid_sums[0], mid_sums[1]
    mid_grad, keep, send = pl.pallas_call(
        mid_grad_kernel,
        out_shape=(
            pltpu.VMEM((most, middle), BF16),
            pltpu.VMEM((most, 640), BF16),
            pltpu.VMEM((most, 640), BF16),
        ),
        in_specs=[SM] + [VM] * 6,
        out_specs=(VM, VM, VM),
        compiler_params=params(8),
        name="mid_grad",
    )(meta, mid_act_grad, mid_pre, belong, mid_merged, gain_mid, mid_sums)
    other = swap(send, "sp", 1)
    small_half = 2048
    small = pl.pallas_call(
        time_grad_kernel,
        out_shape=(
            jax.ShapeDtypeStruct((4, small_half, 128), F32),
            jax.ShapeDtypeStruct((4, small_half, 128), BF16),
        ),
        in_specs=[SM, VM, VM, VM, VM, ANY],
        out_specs=(VM, VM),
        scratch_shapes=[pltpu.VMEM((2 * small_half, width), F32)],
        compiler_params=params(20),
        name="time_grad",
    )(meta, mid_low, wide, pooled, logit_grad, send)

    def space_grad_part(first_tap, taps, after):
        shapes = (
            jax.ShapeDtypeStruct((taps, 1152, 128), F32),
            jax.ShapeDtypeStruct((taps, 1152, 128), BF16),
        )
        if first_tap == 0:
            return pl.pallas_call(
                functools.partial(space_grad_first_kernel, first_tap),
                out_shape=shapes + (pltpu.VMEM((3 * most, 3 * width), BF16),),
                in_specs=[SM, VM, HBM, VM, VM, VM, ANY],
                out_specs=(VM, VM, VM),
                scratch_shapes=[
                    pltpu.VMEM((640, width), F32),
                    pick_scratch,
                    plane_scratch,
                    pltpu.SemaphoreType.DMA((5 * most // 256,)),
                ],
                compiler_params=params(14),
                name="space_grad",
            )(meta, row_info, in_hbm(stored), outer_part, keep, other, after)
        return pl.pallas_call(
            functools.partial(space_grad_kernel, first_tap),
            out_shape=shapes,
            in_specs=[SM, VM, VM, VM],
            out_specs=(VM, VM),
            scratch_shapes=[pltpu.VMEM((640, width), F32)],
            compiler_params=params(10),
            name="space_grad",
        )(meta, after, keep, other)

    class Chain:
        def __init__(self, name, state, order, at):
            self.name, self.state, self.order, self.at = name, state, order, at
            self.stage, self.down = 0, True

        def step(self, after):
            if self.down:
                self.state = halve_step(*self.state, self.order, meta, self.at, self.stage, after, self.name)
                self.stage += 1
                if self.state[1] is None:
                    self.state, self.down, self.stage = self.state[0], False, self.stage - 1
            else:
                self.state = double_step(self.state, self.order, meta, self.at, self.stage, after, self.name)
                self.stage -= 1
            return self.state[0] if self.down else self.state

    chunks = {"b": (0, 5), "c": (5, 4)}
    dense, edges, logits = {}, {}, {}
    chains = {"t": Chain("time", small, small_order, SMALL_TURN)}
    after = small[1]
    left = {"t": 2 * steps + 1, "b": 2 * steps - 1, "c": 2 * steps - 1}
    for event in PLAN + ("t", "b", "c") * (2 * steps):
        if event in left and not left[event]:
            continue
        if event in left:
            left[event] -= 1
        if event in ("space_b", "space_c"):
            name = event[-1]
            *state, = space_grad_part(*chunks[name], after if name == "b" else gathered)
            if name == "b":
                gathered = state.pop()
            chains[name] = Chain("taps" + name, state, order, TURN)
            after = state[1]
        elif event in ("back_0", "back_1"):
            side = int(event[-1])
            dense[side], edges[side], logits[side] = pl.pallas_call(
                functools.partial(input_back_kernel, side, frame_count),
                out_shape=(
                    jax.ShapeDtypeStruct((frame_count, cells, width), F32),
                    jax.ShapeDtypeStruct((frame_count, cells, width), BF16),
                    jax.ShapeDtypeStruct((clip_count, classes), F32),
                ),
                in_specs=[SM, VM, VM, HBM, VM, VM, VM, ANY],
                out_specs=(VM, VM, VM),
                scratch_shapes=[
                    pltpu.VMEM((6 * width, middle), BF16),
                    pltpu.VMEM((2, most // 2 + 256, 3 * width), BF16),
                    pltpu.VMEM((cells, 3 * cells), BF16),
                    pltpu.VMEM((most // 2 + 256, width), BF16),
                    pltpu.VMEM((most // 2 + 256, width), BF16),
                    pltpu.SemaphoreType.DMA(()),
                ],
                compiler_params=params(26),
                name="input_back",
            )(meta, col_info, mid_grad, weight, act_grad, pooled, class_lines, after)
            after = edges[side]
        else:
            after = chains[event].step(after)

    space_grad = None
    for name in ("b", "c"):
        first_tap, taps = chunks[name]
        own_half = chains[name].state
        got_half = trade(own_half, order, 0)
        pieces = [own_half, got_half, swap(own_half, "sp", 1), swap(got_half, "sp", 1)]
        piece = pl.BlockSpec((1, 1152, 128), lambda n, meta: (n, 0, 0))
        before = [] if space_grad is None else [space_grad]
        space_grad = pl.pallas_call(
            functools.partial(join_kernel, steps),
            grid_spec=pltpu.PrefetchScalarGridSpec(
                num_scalar_prefetch=1,
                grid=(taps,),
                in_specs=[piece] * 4 + [ANY] * len(before),
                out_specs=pl.BlockSpec((1, width, middle), lambda n, meta, tap=first_tap: (n + tap, 0, 0)),
            ),
            out_shape=jax.ShapeDtypeStruct((9, width, middle), F32),
            input_output_aliases={5: 0} if before else {},
            compiler_params=params(12),
            name="join",
        )(meta, *pieces, *before)
    space_grad = space_grad.reshape(3, 3, width, middle)

    up = lax.ppermute(edges[0], "sp", [(i, i - 1) for i in range(1, sp_count)])
    down = lax.ppermute(edges[1], "sp", [(i, i + 1) for i in range(sp_count - 1)])
    frame_ok = jnp.arange(frame_count)[None, :] < frames[:, None]
    row_ok = (lax.axis_index("sp") * row_count + jnp.arange(row_count))[None, :] < rows[:, None]
    col_ok = jnp.arange(col_count)[None, :] < cols[:, None]
    mask = (frame_ok[:, :, None, None] & row_ok[:, None, :, None] & col_ok[:, None, None, :])[..., None]
    input_grad = jnp.stack([dense[0] + down.astype(F32), dense[1] + up.astype(F32)])
    input_grad = input_grad.reshape(row_count, frame_count, clip_count, 8, width)[:, :, :, :col_count]
    input_grad = jnp.where(mask, input_grad.transpose(2, 1, 0, 3, 4), 0.0)
    logits = logits[0]
    for axis, bit in bits("sp"):
        logits = logits + swap(logits, axis, bit)
    logits = logits + class_bias

    own_half = chains["t"].state
    time_grad, class_weight_grad = pl.pallas_call(
        time_join_kernel,
        out_shape=(
            jax.ShapeDtypeStruct((3 * middle, width), F32),
            jax.ShapeDtypeStruct((classes, width), F32),
        ),
        in_specs=[SM, VM, VM],
        out_specs=(VM, VM),
        compiler_params=params(16),
        name="time_join",
    )(meta, own_half, trade(own_half, small_order, 0))
    time_grad = time_grad.reshape(3, middle, width)
    class_weight_grad = class_weight_grad.T
    return (
        logits,
        input_grad,
        space_grad,
        time_grad,
        gain_mid_grad,
        shift_mid_grad,
        gain_out_grad,
        shift_out_grad,
        class_weight_grad,
        class_bias_grad,
    )


def solution(mesh):
    placed = (
        P("dp", None, "sp", None, None),
        P(),
        P(),
        P(),
        P(),
        P(),
        P(),
        P(),
        P(),
        P("dp"),
        P("dp"),
        P("dp"),
        P("dp", None),
    )
    return jax.shard_map(
        shards,
        mesh=mesh,
        in_specs=placed,
        out_specs=(
            P("dp", None),
            P("dp", None, "sp", None, None),
            P(),
            P(),
            P(),
            P(),
            P(),
            P(),
            P(),
            P(),
        ),
        check_vma=False,
    )
```

```python
import functools

import jax
import jax.numpy as jnp
from jax import lax
from jax.experimental import pallas as pl
from jax.experimental.pallas import tpu as pltpu
from jax.sharding import PartitionSpec as P

EPSILON = 1e-05
HIGH = lax.Precision.HIGHEST
F32 = jnp.float32
BF16 = jnp.bfloat16
S_AT, BLOCKS_AT, CORE_AT, ROW_AT, OFF, LEN, PAD, END_AT, FIRST_AT, TURN, SMALL_TURN = 0, 1, 2, 3, 4, 8, 12, 16, 17, 18, 33
META = 48

PLAN = "Bt0btCbt1bctcbticbtcbctbccpTPqQ"

VM = pl.BlockSpec(memory_space=pltpu.VMEM)
SM = pl.BlockSpec(memory_space=pltpu.SMEM)
ANY = pl.BlockSpec(memory_space=pl.ANY)
HBM = pl.BlockSpec(memory_space=pltpu.HBM)


def in_hbm(value):
    return pltpu.with_memory_space_constraint(value, pltpu.HBM)


STEP = 6


def takes(us):
    return pl.CostEstimate(flops=us * 1_100_000_000, bytes_accessed=us * 3_300_000, transcendentals=0)


def params(mib):
    return pltpu.CompilerParams(vmem_limit_bytes=mib << 20)


def nt_dot(a, b):
    return lax.dot_general(a, b, (((1,), (1,)), ((), ())), preferred_element_type=F32)


def tn_dot(a, b):
    return lax.dot_general(a, b, (((0,), (0,)), ((), ())), preferred_element_type=F32)


def dot(a, b):
    return jnp.dot(a, b, preferred_element_type=F32)


def split(value):
    high = value.astype(BF16)
    return high, (value - high.astype(F32)).astype(BF16)


def sigmoid(v):
    return 1.0 / (1.0 + jnp.exp(-v))


def slope(v):
    s = sigmoid(v)
    return s * (1.0 + v * (1.0 - s))


def at16(index):
    return pl.multiple_of(index, 16)


def at128(index):
    return pl.multiple_of(index, 128)


def pick_rows(row_info, shift):
    place, col, cols = row_info[0:1, :], row_info[1:2, :], row_info[2:3, :]
    home = col - shift
    ok = (col < cols) & (home >= 0) & (home < cols)
    spot = jnp.where(ok, place - shift, -1)
    size = row_info.shape[1]
    index = lax.broadcasted_iota(jnp.int32, (size, size), 0)
    return jnp.where(index == spot, 1.0, 0.0).astype(BF16)


def pick_cols(col_info, shift):
    place, col, cols = col_info[:, 0:1], col_info[:, 1:2], col_info[:, 2:3]
    home = col - shift
    ok = (col < cols) & (home >= 0) & (home < cols)
    spot = jnp.where(ok, place - shift, -1)
    size = col_info.shape[0]
    index = lax.broadcasted_iota(jnp.int32, (size, size), 1)
    return jnp.where(index == spot, 1.0, 0.0).astype(BF16)


def each_list(meta, base, frame_count, store):
    for t in range(frame_count):
        for half in range(2):

            @pl.when(half * 128 < meta[PAD + t])
            def _(t=t, half=half):
                store(t, half, at16(base + meta[OFF + t] + half * 128))


def setup_kernel(
    sp_count, orders, where, frames, rows, cols, values, meta, row_info, col_info, clip_info, own, own_low, ahead, pad
):
    row_count, frame_count, clip_count, col_count, width = values.shape
    size = clip_count * 8
    core = lax.rem(where[1], 2)
    first_row = where[1] * row_count
    total = jnp.int32(0)
    for t in range(frame_count):
        length = jnp.int32(0)
        for b in range(clip_count):
            length += jnp.where(frames[b] > t, cols[b], 0)
        padded = (length + 15) // 16 * 16
        meta[OFF + t], meta[LEN + t], meta[PAD + t] = total, length, padded
        total += padded
    plane = (total + 127) // 128 * 128
    meta[S_AT], meta[BLOCKS_AT], meta[CORE_AT], meta[ROW_AT] = plane, plane // 128, core, first_row
    meta[END_AT] = total
    meta[FIRST_AT] = jnp.where(where[1] == 0, 1, 0)
    place = where[0] * sp_count + where[1]
    for start, (order, other) in zip((TURN, SMALL_TURN), orders):
        for n, (zero, one) in enumerate(zip(*order)):
            meta[start + n] = jnp.where(place & jnp.where(core == 0, zero, one) != 0, 1, 0)
        meta[start + len(order[0])] = jnp.where(place & jnp.where(core == 0, other[0], other[1]) != 0, 1, 0)

    lane = lax.broadcasted_iota(jnp.int32, (1, size), 1)
    clip, col = lax.shift_right_logical(lane, 3), lane & 7
    zero = jnp.zeros((1, size), jnp.int32)
    of_cell, of_clip = [zero] * 3, [zero] * 3
    for b in range(clip_count):
        for n, source in enumerate((cols, frames, rows)):
            of_cell[n] = jnp.where(clip == b, source[b], of_cell[n])
            of_clip[n] = jnp.where(lane == b, source[b], of_clip[n])
    start = zero
    for b in range(clip_count):
        ahead_of = (frames[b] > of_cell[1]) | ((frames[b] == of_cell[1]) & (clip > b))
        start += jnp.where(ahead_of, cols[b], 0)
    info = [start + col, col, of_cell[0], of_cell[1], of_cell[2], zero, zero, zero]
    for n, line in enumerate(info[:3] + of_clip[1:] + [zero] * 3):
        row_info[n : n + 1, :] = line
    col_info[...] = jnp.concatenate(info, axis=0).astype(F32).T.astype(jnp.int32)
    per_clip = jnp.maximum(of_clip[0] * of_clip[1] * of_clip[2], 1).astype(F32)[:, 0:128]
    clip_info[...] = jnp.concatenate([per_clip] * 8, axis=0).T

    pad[:, col_count:, :] = jnp.zeros((clip_count, 8 - col_count, width), F32)
    cells = col_info[...]
    for h in range(row_count):
        for t in range(frame_count):
            pad[:, 0:col_count, :] = values[h, t]
            inside = (cells[:, 1:2] < cells[:, 2:3]) & (cells[:, 3:4] > t) & (cells[:, 4:5] > first_row + h)
            masked = pad[...].reshape(size, width) * jnp.where(inside, 1.0, 0.0)
            own[h, t], own_low[h, t] = split(masked)

            @pl.when(core == h)
            def _(t=t, masked=masked):
                ahead[t] = masked.astype(BF16)


def gather_setup(row_info, pick):
    info = row_info[...]
    for j in range(3):
        hot = pick_rows(info, j - 1)
        for half in range(2):
            pick[half, j * 128 : (j + 1) * 128, :] = hot[half * 128 : (half + 1) * 128, :]


def gather_plane(meta, pick, source, packed, base, frame_count):
    def store(t, half, row):
        got = dot(pick[half], source(t)).astype(BF16)
        for j in range(3):
            packed[pl.ds(row, 128), j * 512 : (j + 1) * 512] = got[j * 128 : (j + 1) * 128, :]

    each_list(meta, base, frame_count, store)
    packed[pl.ds(at16(base + meta[END_AT]), 128), :] = jnp.zeros((128, 1536), BF16)


def copy_out(blocks, source, begin, target, start, sems, action):
    def one(m, carry):
        copy = pltpu.make_async_copy(
            source.at[pl.ds(at128(begin + m * 128), 128)], target.at[pl.ds(at128(start + m * 128), 128)], sems.at[m]
        )
        if action == "start":
            copy.start()
        else:
            copy.wait()
        return carry

    lax.fori_loop(0, blocks, one, 0)


def space_kernel(
    meta, row_info, own, own_low, part, weight_in, logit_grad, class_weight, clip_info,
    mid_pre, belong, residual, stored, pooled_grad, bias_grad, packed, pick, weight, sems, load,
):
    frame_count = own.shape[1]
    core = meta[CORE_AT]
    s = meta[S_AT]
    blocks = meta[BLOCKS_AT]
    fetch = pltpu.make_async_copy(weight_in, weight, load)
    fetch.start()
    gather_setup(row_info, pick)

    @pl.when(core == 0)
    def _():
        for h in range(2):
            gather_plane(meta, pick, lambda t, h=h: own[h, t], packed, h * s, frame_count)
        for h in range(2):
            gather_plane(meta, pick, lambda t, h=h: part[h, t], packed, (2 + h) * s, frame_count)

    @pl.when(core != 0)
    def _():
        for h in range(2):
            gather_plane(meta, pick, lambda t, h=h: part[h, t], packed, h * s, frame_count)
        for h in range(2):
            gather_plane(meta, pick, lambda t, h=h: own[h, t], packed, (2 + h) * s, frame_count)

    copy_out(4 * blocks, packed, 0, stored, s, sems, "start")
    size = row_info.shape[1]
    clip_of = lax.broadcasted_iota(jnp.int32, (size, 128), 0) // 8
    lane = lax.broadcasted_iota(jnp.int32, (size, 128), 1)
    frames_of = jnp.broadcast_to(row_info[3:4, 0:128], (size, 128))
    rows_of = jnp.broadcast_to(row_info[4:5, 0:128], (size, 128))
    for h in range(2):

        def store(t, half, row, h=h):
            hot = pick[half, 128:256, :]
            inside = (clip_of == lane) & (frames_of > t) & (rows_of > meta[ROW_AT] + h)
            belong[pl.ds(row, 128), :] = dot(hot, jnp.where(inside, 1.0, 0.0).astype(BF16)).astype(BF16)
            residual[pl.ds(row, 128), :] = dot(hot, own[h, t]) + dot(hot, own_low[h, t])

        each_list(meta, h * s, frame_count, store)
        belong[pl.ds(at16(h * s + meta[END_AT]), 128), :] = jnp.zeros((128, 128), BF16)
        residual[pl.ds(at16(h * s + meta[END_AT]), 128), :] = jnp.zeros((128, 512), F32)
    clips, classes = logit_grad.shape
    pooled_grad[...] = jnp.zeros(pooled_grad.shape, F32)
    pooled_grad[0:clips, :] = (
        jnp.dot(logit_grad[...], class_weight[...], precision=HIGH, preferred_element_type=F32)
        / clip_info[0:clips, 0:1]
    )
    bias_grad[...] = jnp.zeros(bias_grad.shape, F32)
    bias_grad[:, 0:classes] = jnp.sum(logit_grad[...], axis=0, keepdims=True) * meta[FIRST_AT].astype(F32)
    fetch.wait()
    for h in range(2):

        def conv(m, carry, h=h):
            row = at128(h * s + m * 128)

            def tap(i):
                source = packed[pl.ds(at128((2 * core + h + i - 1) * s + m * 128), 128), :]
                return dot(source, weight[i * 1536 : (i + 1) * 1536, :])

            mid_pre[pl.ds(row, 128), :] = tap(1) + tap(2 - 2 * h)

            @pl.when(core == 1 - h)
            def _():
                mid_pre[pl.ds(row, 128), :] += tap(2 * h)

            return carry

        lax.fori_loop(0, blocks, conv, 0)
    copy_out(4 * blocks, packed, 0, stored, s, sems, "wait")


def mask_of(belong, row, size=256):
    return jnp.sum(belong[pl.ds(row, size), :].astype(F32), axis=1, keepdims=True)


def norm_of(merged):
    count = merged[0:1, :]
    return merged[1:2, :] / count, lax.rsqrt(merged[2:3, :] / count + EPSILON)


def norm_sums(meta, values, belong, stats):
    width = values.shape[1]

    def sums(m, total):
        row = at128(m * 256)
        mask = mask_of(belong, row)
        return (
            total[0] + jnp.sum(mask, axis=0, keepdims=True),
            total[1] + jnp.sum(values[pl.ds(row, 256), :] * mask, axis=0, keepdims=True),
        )

    count, total = lax.fori_loop(
        0, meta[BLOCKS_AT], sums, (jnp.zeros((1, 1), F32), jnp.zeros((1, width), F32))
    )
    center = total / count

    def spread(m, squares):
        row = at128(m * 256)
        off = (values[pl.ds(row, 256), :] - center) * mask_of(belong, row)
        return squares + jnp.sum(off * off, axis=0, keepdims=True)

    squares = lax.fori_loop(0, meta[BLOCKS_AT], spread, jnp.zeros((1, width), F32))
    stats[0:1, :] = jnp.broadcast_to(count, (1, width))
    stats[1:2, :] = total
    stats[2:3, :] = squares


def space_edge_kernel(
    meta, row_info, mid_in, stored_in, outer, weight_in, belong, mid_pre, stored, stats, pick, plane, weight, sems, load
):
    core = meta[CORE_AT]
    s = meta[S_AT]
    blocks = meta[BLOCKS_AT]
    fetch = pltpu.make_async_copy(
        weight_in.at[pl.ds(pl.multiple_of(core * 3072, 1024), 1536)], weight, load
    )
    fetch.start()
    gather_setup(row_info, pick)
    gather_plane(meta, pick, lambda t: outer[t], plane, 0, outer.shape[0])
    copy_out(blocks, plane, 0, stored, 5 * s * core, sems, "start")
    fetch.wait()

    def conv(m, carry):
        row = at128(core * s + m * 128)
        mid_pre[pl.ds(row, 128), :] += dot(plane[pl.ds(at128(m * 128), 128), :], weight[...])
        return carry

    lax.fori_loop(0, blocks, conv, 0)
    norm_sums(meta, mid_pre, belong, stats)
    copy_out(blocks, plane, 0, stored, 5 * s * core, sems, "wait")


def shift_lists(meta, frame_count, source, target, width, move):
    s = meta[S_AT]
    for h in range(2):

        def store(t, half, row, h=h):
            other = t + move
            if 0 <= other < frame_count:
                block = source(at16(h * s + meta[OFF + other] + half * 128))
                place = half * 128 + lax.broadcasted_iota(jnp.int32, (128, 1), 0)
                keep = jnp.where(place < meta[LEN + other], 1.0, 0.0).astype(BF16)
                target(row, block * keep)
            else:
                target(row, jnp.zeros((128, width), BF16))

        each_list(meta, h * s, frame_count, store)
        target(at16(h * s + meta[END_AT]), jnp.zeros((128, width), BF16))


def time_kernel(
    frame_count, meta, mid_pre, belong, merged, gain, shift, weight, after, mid_low, out_pre, stats, wide
):
    blocks = meta[BLOCKS_AT]
    center, scale = norm_of(merged)

    def act(m, carry):
        row = at128(m * 256)
        mask = mask_of(belong, row)
        normed = (mid_pre[pl.ds(row, 256), :] - center) * scale
        value = gain[...] * normed + shift[...]
        low = (value * sigmoid(value) * mask).astype(BF16)
        wide[pl.ds(row, 256), 1152:2304] = low
        mid_low[pl.ds(row, 256), :] = low
        return carry

    lax.fori_loop(0, blocks, act, 0)
    wide[pl.ds(at128(2 * meta[S_AT]), 256), :] = jnp.zeros((256, 3456), BF16)
    for k in (0, 2):

        def source(row):
            return wide[pl.ds(row, 128), 1152:2304]

        def target(row, value, k=k):
            wide[pl.ds(row, 128), k * 1152 : (k + 1) * 1152] = value

        shift_lists(meta, frame_count, source, target, 1152, k - 1)

    def conv(m, carry):
        row = at128(m * 256)
        out_pre[pl.ds(row, 256), :] = dot(wide[pl.ds(row, 256), :], weight[...])
        return carry

    lax.fori_loop(0, blocks, conv, 0)
    norm_sums(meta, out_pre, belong, stats)


def act_kernel(
    meta, out_pre, belong, residual, merged, gain_ref, shift_ref, pooled_grad, bias_grad, clip_info,
    act_grad, stats, pooled,
):
    blocks = meta[BLOCKS_AT]
    center, scale = norm_of(merged)
    high, rest = split(pooled_grad[...])
    pooled[...] = jnp.zeros(pooled.shape, F32)

    def step(m, total):
        row = at128(m * 256)
        hot = belong[pl.ds(row, 256), :]
        normed = (out_pre[pl.ds(row, 256), :] - center) * scale
        value = gain_ref[...] * normed + shift_ref[...] + residual[pl.ds(row, 256), :]
        s = sigmoid(value)
        first, second = split(value * s)
        pooled[...] += tn_dot(hot, first) + tn_dot(hot, second)
        grad = (dot(hot, high) + dot(hot, rest)) * (s * (1.0 + value * (1.0 - s)))
        act_grad[pl.ds(row, 256), :] = grad
        shift, gain = total
        return (
            shift + jnp.sum(grad, axis=0, keepdims=True),
            gain + jnp.sum(grad * normed, axis=0, keepdims=True),
        )

    zero = jnp.zeros((1, 512), F32)
    shift, gain = lax.fori_loop(0, blocks, step, (zero, zero))
    stats[0:1, :] = shift
    stats[1:2, :] = gain
    stats[2:3, :] = bias_grad[...]
    pooled[...] = pooled[...] / clip_info[:, 0:1]


def back_kernel(
    frame_count, meta, act_grad, out_pre, belong, out_merged, out_gain, out_sums, weight, mid_pre, mid_merged,
    mid_gain, mid_shift, wide, mid_act_grad, stats,
):
    blocks = meta[BLOCKS_AT]
    out_center, out_scale = norm_of(out_merged)
    mid_center, mid_scale = norm_of(mid_merged)
    out_shift_part = out_sums[0:1, :] / out_merged[0:1, :]
    out_gain_part = out_sums[1:2, :] / out_merged[0:1, :]

    def grad(m, carry):
        row = at128(m * 256)
        mask = mask_of(belong, row)
        normed = (out_pre[pl.ds(row, 256), :] - out_center) * out_scale
        inner = act_grad[pl.ds(row, 256), :] - mask * (out_shift_part + normed * out_gain_part)
        wide[pl.ds(row, 256), 512:1024] = (out_gain[...] * out_scale * inner).astype(BF16)
        return carry

    lax.fori_loop(0, blocks, grad, 0)
    wide[pl.ds(at128(2 * meta[S_AT]), 256), :] = jnp.zeros((256, 1536), BF16)
    for k in (0, 2):

        def source(row):
            return wide[pl.ds(row, 128), 512:1024]

        def target(row, value, k=k):
            wide[pl.ds(row, 128), k * 512 : (k + 1) * 512] = value

        shift_lists(meta, frame_count, source, target, 512, 1 - k)

    def conv(m, total):
        row = at128(m * 256)
        block = wide[pl.ds(row, 256), :]
        acc = nt_dot(block[:, 0:512], weight[0])
        acc += nt_dot(block[:, 512:1024], weight[1])
        acc += nt_dot(block[:, 1024:1536], weight[2])
        mask = mask_of(belong, row)
        normed = (mid_pre[pl.ds(row, 256), :] - mid_center) * mid_scale
        acc = acc * mask * slope(mid_gain[...] * normed + mid_shift[...])
        mid_act_grad[pl.ds(row, 256), :] = acc
        shift, gain = total
        return (
            shift + jnp.sum(acc, axis=0, keepdims=True),
            gain + jnp.sum(acc * normed, axis=0, keepdims=True),
        )

    zero = jnp.zeros((1, 1152), F32)
    shift, gain = lax.fori_loop(0, blocks, conv, (zero, zero))
    stats[0:1, :] = shift
    stats[1:2, :] = gain


def time_grad_kernel(meta, mid_low, wide, pooled, logit_grad, stats, keep, send, passed, total):
    passed[...] = stats[...]
    core = meta[CORE_AT]
    middle = mid_low.shape[1]
    classes = logit_grad.shape[1]
    half = keep.shape[1]
    for k in range(3):
        rows = slice(k * middle, (k + 1) * middle)
        total[rows, :] = jnp.zeros((middle, 512), F32)

        def step(m, carry, k=k, rows=rows):
            row = at128(m * 256)
            total[rows, :] += tn_dot(mid_low[pl.ds(row, 256), :], wide[pl.ds(row, 256), k * 512 : (k + 1) * 512])
            return carry

        lax.fori_loop(0, meta[BLOCKS_AT], step, 0)
    total[3 * middle : 3 * middle + classes, :] = lax.dot_general(
        logit_grad[...], pooled[0 : logit_grad.shape[0], :], (((0,), (0,)), ((), ())), precision=HIGH, preferred_element_type=F32
    )
    total[3 * middle + classes :, :] = jnp.zeros((2 * half - 3 * middle - classes, 512), F32)
    for lane in range(4):
        lanes = slice(lane * 128, (lane + 1) * 128)
        keep[lane] = total[pl.ds(at128(core * half), half), lanes]
        send[lane] = total[pl.ds(at128((1 - core) * half), half), lanes].astype(BF16)


def time_join_kernel(meta, own, got, after, also, time_grad, class_grad):
    half = own.shape[1]
    rest = time_grad.shape[0] - half

    def place(first, second):
        for lane in range(4):
            lanes = slice(lane * 128, (lane + 1) * 128)
            time_grad[0:half, lanes] = first[lane].astype(F32)
            time_grad[half:, lanes] = second[lane, 0:rest, :].astype(F32)
            class_grad[:, lanes] = second[lane, rest : rest + class_grad.shape[0], :].astype(F32)

    @pl.when(meta[CORE_AT] == 0)
    def _():
        place(own, got)

    @pl.when(meta[CORE_AT] != 0)
    def _():
        place(got, own)


def mid_grad_kernel(meta, mid_act_grad, mid_pre, belong, merged, gain, sums, after, whole, keep, send):
    core = meta[CORE_AT]
    center, scale = norm_of(merged)
    shift_part = sums[0:1, :] / merged[0:1, :]
    gain_part = sums[1:2, :] / merged[0:1, :]

    def step(m, carry):
        row = at128(m * 256)
        mask = mask_of(belong, row)
        normed = (mid_pre[pl.ds(row, 256), :] - center) * scale
        inner = mid_act_grad[pl.ds(row, 256), :] - mask * (shift_part + normed * gain_part)
        low = (gain[...] * scale * inner).astype(BF16)
        whole[pl.ds(row, 256), :] = low

        @pl.when(core == 0)
        def _():
            keep[pl.ds(row, 256), 0:512] = low[:, 0:512]
            send[pl.ds(row, 256), 0:512] = low[:, 512:1024]

        @pl.when(core != 0)
        def _():
            keep[pl.ds(row, 256), 0:512] = low[:, 512:1024]
            send[pl.ds(row, 256), 0:512] = low[:, 0:512]

        keep[pl.ds(row, 256), 512:640] = low[:, 1024:1152]
        send[pl.ds(row, 256), 512:640] = low[:, 1024:1152]
        return carry

    lax.fori_loop(0, meta[BLOCKS_AT], step, 0)


def space_grad_taps(first_tap, meta, packed, own, part, keep, send, total):
    core = meta[CORE_AT]
    s = meta[S_AT]
    mine = meta[TURN]

    def one(tap, carry):
        i, j = lax.div(first_tap + tap, 3), lax.rem(first_tap + tap, 3)
        lanes = pl.ds(at128(j * 512), 512)

        def both(m):
            row = at128(m * 256)
            first = packed[pl.ds(at128((2 * core + i) * s + row), 256), lanes]
            second = packed[pl.ds(at128((2 - 2 * core + i) * s + row), 256), lanes]
            return tn_dot(own[pl.ds(row, 256), :], first) + tn_dot(part[pl.ds(row, 256), :], second)

        total[...] = both(0)

        def step(m, carry):
            total[...] += both(m)
            return carry

        lax.fori_loop(1, meta[BLOCKS_AT], step, 0)
        for half, out, kind in ((mine, keep, F32), (1 - mine, send, BF16)):
            lane = half * 256
            out[tap, 0:512, :] = total[0:512, pl.ds(at128(lane), 128)].astype(kind)
            out[tap, 512:1024, :] = total[0:512, pl.ds(at128(lane + 128), 128)].astype(kind)
            out[tap, 1024:1152, :] = total[512:640, pl.ds(at128(core * 256 + half * 128), 128)].astype(kind)
        return carry

    lax.fori_loop(0, keep.shape[0], one, 0)


def space_grad_kernel(
    first_tap, meta, row_info, stored, outer, own, part, after, also, keep, send, packed, total, pick, plane, sems
):
    core = meta[CORE_AT]
    s = meta[S_AT]
    blocks = meta[BLOCKS_AT]
    copy_out(5 * blocks, stored, core * s, packed, core * s, sems, "start")
    gather_setup(row_info, pick)
    gather_plane(meta, pick, lambda t: outer[t], plane, 0, outer.shape[0])

    def put(m, carry):
        row = at128(m * 128)
        packed[pl.ds(at128(5 * s * (1 - core) + row), 128), :] = plane[pl.ds(row, 128), :]
        return carry

    lax.fori_loop(0, blocks, put, 0)
    copy_out(5 * blocks, stored, core * s, packed, core * s, sems, "wait")
    space_grad_taps(first_tap, meta, packed, own, part, keep, send, total)


def halve_kernel(at, meta, keep, got, after, also, next_keep, next_send):
    half = next_keep.shape[1]
    mine = meta[at]

    def one(tap, carry):
        low, high = pl.ds(at16(mine * half), half), pl.ds(at16((1 - mine) * half), half)
        next_keep[tap] = keep[tap, low, :] + got[tap, low, :].astype(F32)
        next_send[tap] = (keep[tap, high, :] + got[tap, high, :].astype(F32)).astype(BF16)
        return carry

    lax.fori_loop(0, keep.shape[0], one, 0)


def halve_pass_kernel(at, meta, keep, got, value, next_keep, next_send, passed):
    passed[...] = value[...]
    halve_kernel(at, meta, keep, got, None, None, next_keep, next_send)


def share_kernel(keep, got, after, also, out):
    def one(tap, carry):
        out[tap] = (keep[tap] + got[tap].astype(F32)).astype(BF16)
        return carry

    lax.fori_loop(0, keep.shape[0], one, 0)


def double_kernel(at, meta, own, got, after, also, out):
    half = own.shape[1]
    mine = meta[at]

    def one(tap, carry):
        out[tap, pl.ds(at16(mine * half), half), :] = own[tap]
        out[tap, pl.ds(at16((1 - mine) * half), half), :] = got[tap]
        return carry

    lax.fori_loop(0, own.shape[0], one, 0)


def input_back_kernel(
    side, frame_count, meta, col_info, grad, weight_in, act_grad, pooled, class_weight, after, also,
    dense, edge, logits, weight, wide, spread, high, rest, load,
):
    s = meta[S_AT]
    fetch = pltpu.make_async_copy(weight_in.at[pl.ds(side * 1536, 3072)], weight, load)
    fetch.start()
    if side == 0:
        logits[...] = lax.dot_general(
            pooled[0 : logits.shape[0], :],
            class_weight[...],
            (((1,), (1,)), ((), ())),
            precision=HIGH,
            preferred_element_type=F32,
        )
    else:
        logits[...] = jnp.zeros(logits.shape, F32)
    info = col_info[...]
    for j in range(3):
        spread[:, j * 256 : (j + 1) * 256] = pick_cols(info, j - 1)

    def cut(m, carry):
        row = at128(m * 128)
        first, second = split(act_grad[pl.ds(at128(side * s + row), 128), :])
        high[pl.ds(row, 128), :] = first
        rest[pl.ds(row, 128), :] = second
        return carry

    lax.fori_loop(0, meta[BLOCKS_AT], cut, 0)
    for part in (high, rest):
        part[pl.ds(at128(s), 256), :] = jnp.zeros((256, 512), BF16)
    for plane in range(2):
        wide[plane, pl.ds(at128(s), 256), :] = jnp.zeros((256, 1536), BF16)
    fetch.wait()
    edge_terms, inner_terms = ([(0, 0)], [(0, 1), (1, 0)]) if side == 0 else ([(1, 2)], [(0, 2), (1, 1)])

    def conv(m, carry):
        row = at128(m * 128)
        for plane, terms in enumerate((edge_terms, inner_terms)):
            acc = None
            for h, i in terms:
                source = grad[pl.ds(at128(h * s + row), 128), :]
                term = nt_dot(source, weight[(i - side) * 1536 : (i - side + 1) * 1536, :])
                acc = term if acc is None else acc + term
            wide[plane, pl.ds(row, 128), :] = acc.astype(BF16)
        return carry

    lax.fori_loop(0, meta[BLOCKS_AT], conv, 0)
    for plane in range(2):
        for t in range(frame_count):
            rows = pl.ds(at16(meta[OFF + t]), 256)
            acc = None
            for j in range(3):
                term = dot(spread[:, j * 256 : (j + 1) * 256], wide[plane, rows, j * 512 : (j + 1) * 512])
                acc = term if acc is None else acc + term
            if plane == 0:
                edge[t] = acc.astype(BF16)
            else:
                acc += dot(spread[:, 256:512], high[rows, :]) + dot(spread[:, 256:512], rest[rows, :])
                dense[t] = acc


def input_join_kernel(meta, col_info, first, second, down, up, after, also, out, pad):
    frame_count, clip_count, col_count, width = out.shape[1:]
    cells = col_info[...]
    for h, (own, got) in enumerate(((first, down), (second, up))):
        for t in range(frame_count):
            inside = (cells[:, 1:2] < cells[:, 2:3]) & (cells[:, 3:4] > t) & (cells[:, 4:5] > meta[ROW_AT] + h)
            value = jnp.where(inside, own[t] + got[t].astype(F32), 0.0)
            pad[...] = value.reshape(clip_count, 8, width)
            out[h, t] = pad[:, 0:col_count, :]


def join_kernel(steps, meta, own, got, part_own, part_got, after, also, *rest):
    out = rest[-1]
    core = meta[CORE_AT]
    mine, other = meta[TURN], meta[TURN + steps]
    for piece, half, owner in (
        (own, mine, core),
        (got, 1 - mine, core),
        (part_own, other, 1 - core),
        (part_got, 1 - other, 1 - core),
    ):
        row = half * 256
        middles = pl.ds(at128(owner * 512), 512)
        out[0, pl.ds(at128(row), 128), middles] = piece[0, 0:512, :].astype(F32).T
        out[0, pl.ds(at128(row + 128), 128), middles] = piece[0, 512:1024, :].astype(F32).T
        out[0, pl.ds(at128(owner * 256 + half * 128), 128), 1024:1152] = piece[0, 1024:1152, :].astype(F32).T


def swap(value, axis, bit):
    size = lax.axis_size(axis)
    if size <= bit:
        return None
    return lax.ppermute(value, axis, [(i, i ^ bit) for i in range(size)])


def bits(axis):
    return [(axis, 1 << n) for n in range((lax.axis_size(axis) - 1).bit_length())]


def sum_all(value, axes):
    for axis, bit in axes:
        value = value + swap(value, axis, bit)
    return value


def merge_all(stats):
    stats = stats[:3]
    row = lax.broadcasted_iota(jnp.int32, stats.shape, 0)
    for axis, bit in bits("sp") + bits("dp"):
        other = swap(stats, axis, bit)
        gap = stats[1] / stats[0] - other[1] / other[0]
        extra = gap * gap * (stats[0] * other[0] / (stats[0] + other[0]))
        stats = stats + other + jnp.where(row == 2, extra[None], 0.0)
    return stats


def trade(value, order, stage):
    size = lax.axis_size(("dp", "sp"))
    return lax.ppermute(value, ("dp", "sp"), [(i, i ^ order[i % 2][stage]) for i in range(size)])


def halve_step(keep, send, order, meta, at, stage, after, name):
    got = trade(send, order, stage)
    n, rows, lanes = keep.shape
    if stage + 1 == len(order[0]):
        share = pl.pallas_call(
            share_kernel,
            out_shape=jax.ShapeDtypeStruct(keep.shape, BF16),
            in_specs=[VM, VM, ANY, ANY],
            out_specs=VM,
            compiler_params=params(6),
            cost_estimate=takes(STEP),
            name=name + "_share",
        )(keep, got, *after)
        return share, None
    half = rows // 2
    if half % 16:
        pairs = (keep + got.astype(F32)).reshape(n, 2, half, lanes)
        mine = meta[at + stage + 1]
        keep = lax.dynamic_index_in_dim(pairs, mine, 1, keepdims=False)
        send = lax.dynamic_index_in_dim(pairs, 1 - mine, 1, keepdims=False).astype(BF16)
        return keep, send
    return pl.pallas_call(
        functools.partial(halve_kernel, at + stage + 1),
        out_shape=(
            jax.ShapeDtypeStruct((n, half, lanes), F32),
            jax.ShapeDtypeStruct((n, half, lanes), BF16),
        ),
        in_specs=[SM, VM, VM, ANY, ANY],
        out_specs=(VM, VM),
        compiler_params=params(10),
        cost_estimate=takes(STEP),
        name=name + "_halve%d" % stage,
    )(meta, keep, got, *after)


def double_step(own, order, meta, at, stage, after, name):
    got = trade(own, order, stage)
    n, rows, lanes = own.shape
    if rows % 16:
        mine = meta[at + stage]
        return jnp.concatenate([jnp.where(mine == 0, own, got), jnp.where(mine == 0, got, own)], axis=1)
    return pl.pallas_call(
        functools.partial(double_kernel, at + stage),
        out_shape=jax.ShapeDtypeStruct((n, 2 * rows, lanes), BF16),
        in_specs=[SM, VM, VM, ANY, ANY],
        out_specs=VM,
        compiler_params=params(8),
        cost_estimate=takes(STEP),
        name=name + "_double%d" % stage,
    )(meta, own, got, *after)


def shards(
    clip_input,
    space_weight,
    time_weight,
    gain_mid,
    shift_mid,
    gain_out,
    shift_out,
    class_weight,
    class_bias,
    frames,
    rows,
    cols,
    logit_grad,
):
    clip_count, frame_count, row_count, col_count, width = clip_input.shape
    middle = space_weight.shape[-1]
    classes = class_weight.shape[1]
    cells = clip_count * 8
    most = row_count * frame_count * clip_count * col_count
    sp_count = lax.axis_size("sp")
    x = [bit for _, bit in bits("sp")[1:]]
    y, z = [[bit * sp_count for _, bit in part] for part in (bits("dp")[:1], bits("dp")[1:])]
    order = x + y + z, y + x + z
    small_order = [1] + order[0], [1] + order[1]
    steps = len(order[0])
    orders = (order, (order[1][0], order[0][0])), (small_order, (1, 1))
    place = jnp.stack([lax.axis_index("dp"), lax.axis_index("sp")]).astype(jnp.int32)
    cells_shape = (row_count, frame_count, cells, width)
    meta, row_info, col_info, clip_info, own, own_low, ahead = pl.pallas_call(
        functools.partial(setup_kernel, sp_count, orders),
        out_shape=(
            jax.ShapeDtypeStruct((META,), jnp.int32),
            jax.ShapeDtypeStruct((8, cells), jnp.int32),
            jax.ShapeDtypeStruct((cells, 8), jnp.int32),
            jax.ShapeDtypeStruct((128, 8), F32),
            jax.ShapeDtypeStruct(cells_shape, BF16),
            jax.ShapeDtypeStruct(cells_shape, BF16),
            jax.ShapeDtypeStruct(cells_shape[1:], BF16),
        ),
        in_specs=[SM, SM, SM, SM, VM],
        out_specs=(SM, VM, VM, VM, VM, VM, VM),
        scratch_shapes=[pltpu.VMEM((clip_count, 8, width), F32)],
        compiler_params=params(20),
        cost_estimate=takes(3),
        name="setup",
    )(place, frames, rows, cols, clip_input.transpose(2, 1, 0, 3, 4))
    class_lines = class_weight.T

    part = swap(own, "sp", 1)
    across = [(i, i + 1 if i % 2 else i - 1) for i in range(sp_count)]
    outer = lax.ppermute(ahead, "sp", [(i, j) for i, j in across if 0 <= j < sp_count])
    outer_part = swap(outer, "sp", 1)

    weight = in_hbm(space_weight.reshape(9 * width, middle))
    stored_shape = pltpu.HBM((3 * most, 3 * width), BF16)
    pick_scratch = pltpu.VMEM((2, 384, cells), BF16)
    plane_scratch = pltpu.VMEM((most // 2 + 256, 3 * width), BF16)
    plane_sems = pltpu.SemaphoreType.DMA((most // 256,))
    mid_pre, belong, residual, stored, pooled_grad, bias_grad = pl.pallas_call(
        space_kernel,
        out_shape=(
            pltpu.VMEM((most, middle), F32),
            pltpu.VMEM((most + 256, 128), BF16),
            pltpu.VMEM((most + 256, width), F32),
            stored_shape,
            pltpu.VMEM((128, width), F32),
            pltpu.VMEM((1, width), F32),
        ),
        in_specs=[SM, VM, VM, VM, VM, HBM, VM, VM, VM],
        out_specs=(VM, VM, VM, HBM, VM, VM),
        scratch_shapes=[
            pltpu.VMEM((2 * most + 256, 3 * width), BF16),
            pick_scratch,
            pltpu.VMEM((9 * width, middle), BF16),
            pltpu.SemaphoreType.DMA((most // 64,)),
            pltpu.SemaphoreType.DMA(()),
        ],
        compiler_params=params(30),
        cost_estimate=takes(17),
        name="space_conv",
    )(meta, row_info, own, own_low, part, weight, logit_grad, class_lines, clip_info)
    mid_pre, stored, stats = pl.pallas_call(
        space_edge_kernel,
        out_shape=(
            pltpu.VMEM((most, middle), F32),
            stored_shape,
            jax.ShapeDtypeStruct((3, middle), F32),
        ),
        in_specs=[SM, VM, VM, HBM, VM, HBM, VM],
        out_specs=(VM, HBM, VM),
        scratch_shapes=[
            pick_scratch,
            plane_scratch,
            pltpu.VMEM((3 * width, middle), BF16),
            plane_sems,
            pltpu.SemaphoreType.DMA(()),
        ],
        input_output_aliases={2: 0, 3: 1},
        compiler_params=params(13),
        cost_estimate=takes(8),
        name="space_edge",
    )(meta, row_info, mid_pre, in_hbm(stored), outer, weight, belong)
    gain_mid, shift_mid = gain_mid[None], shift_mid[None]
    gain_out, shift_out = gain_out[None], shift_out[None]
    mid_merged = merge_all(stats)
    mid_low, out_pre, stats = pl.pallas_call(
        functools.partial(time_kernel, frame_count),
        out_shape=(
            pltpu.VMEM((most, middle), BF16),
            pltpu.VMEM((most, width), F32),
            jax.ShapeDtypeStruct((3, width), F32),
        ),
        in_specs=[SM, VM, VM, VM, VM, VM, VM, ANY],
        out_specs=(VM, VM, VM),
        scratch_shapes=[pltpu.VMEM((most + 256, 3 * middle), BF16)],
        compiler_params=params(24),
        cost_estimate=takes(8),
        name="time_conv",
    )(meta, mid_pre, belong, mid_merged, gain_mid, shift_mid, time_weight.reshape(3 * middle, width), outer_part)

    out_merged = merge_all(stats)
    act_grad, stats, pooled = pl.pallas_call(
        act_kernel,
        out_shape=(
            pltpu.VMEM((most, width), F32),
            jax.ShapeDtypeStruct((3, width), F32),
            jax.ShapeDtypeStruct((128, width), F32),
        ),
        in_specs=[SM] + [VM] * 9,
        out_specs=(VM, VM, VM),
        compiler_params=params(6),
        cost_estimate=takes(3),
        name="act",
    )(meta, out_pre, belong, residual, out_merged, gain_out, shift_out, pooled_grad, bias_grad, clip_info)

    out_sums = sum_all(stats, bits("sp") + bits("dp"))
    shift_out_grad, gain_out_grad, class_bias_grad = out_sums[0], out_sums[1], out_sums[2, :classes]
    wide, mid_act_grad, stats = pl.pallas_call(
        functools.partial(back_kernel, frame_count),
        out_shape=(
            pltpu.VMEM((most + 256, 3 * width), BF16),
            pltpu.VMEM((most, middle), F32),
            jax.ShapeDtypeStruct((2, middle), F32),
        ),
        in_specs=[SM] + [VM] * 11,
        out_specs=(VM, VM, VM),
        compiler_params=params(10),
        cost_estimate=takes(6),
        name="time_back",
    )(
        meta, act_grad, out_pre, belong, out_merged, gain_out, out_sums, time_weight, mid_pre, mid_merged,
        gain_mid, shift_mid,
    )

    small_half = 2048
    *small, stats = pl.pallas_call(
        time_grad_kernel,
        out_shape=(
            jax.ShapeDtypeStruct((4, small_half, 128), F32),
            jax.ShapeDtypeStruct((4, small_half, 128), BF16),
            jax.ShapeDtypeStruct((2, middle), F32),
        ),
        in_specs=[SM] + [VM] * 5,
        out_specs=(VM, VM, VM),
        scratch_shapes=[pltpu.VMEM((2 * small_half, width), F32)],
        compiler_params=params(13),
        cost_estimate=takes(8),
        name="time_grad",
    )(meta, mid_low, wide, pooled, logit_grad, stats)

    got = trade(small[1], small_order, 0)
    axes = bits("sp") + bits("dp")
    mid_sums = sum_all(stats, axes[:2])
    *small, mid_sums = pl.pallas_call(
        functools.partial(halve_pass_kernel, SMALL_TURN + 1),
        out_shape=(
            jax.ShapeDtypeStruct((4, small_half // 2, 128), F32),
            jax.ShapeDtypeStruct((4, small_half // 2, 128), BF16),
            jax.ShapeDtypeStruct((2, middle), F32),
        ),
        in_specs=[SM, VM, VM, VM],
        out_specs=(VM, VM, VM),
        compiler_params=params(8),
        cost_estimate=takes(1),
        name="time_halve",
    )(meta, small[0], got, mid_sums)
    mid_sums = sum_all(mid_sums, axes[2:])

    class Chain:
        def __init__(self, name, state, order, at):
            self.name, self.state, self.order, self.at = name, state, order, at
            self.stage, self.down = 0, True

        def step(self, after):
            if self.down:
                self.state = halve_step(*self.state, self.order, meta, self.at, self.stage, after, self.name)
                self.stage += 1
                if self.state[1] is None:
                    self.state, self.down, self.stage = self.state[0], False, self.stage - 1
            else:
                self.state = double_step(self.state, self.order, meta, self.at, self.stage, after, self.name)
                self.stage -= 1
            return self.state[0] if self.down else self.state

    chains = {"t": Chain("time", small, small_order, SMALL_TURN)}
    chains["t"].stage = 1
    after = chains["t"].step((mid_sums, mid_sums))
    shift_mid_grad, gain_mid_grad = mid_sums[0], mid_sums[1]
    mid_grad, keep, send = pl.pallas_call(
        mid_grad_kernel,
        out_shape=(
            pltpu.VMEM((most, middle), BF16),
            pltpu.VMEM((most, 640), BF16),
            pltpu.VMEM((most, 640), BF16),
        ),
        in_specs=[SM] + [VM] * 6 + [ANY],
        out_specs=(VM, VM, VM),
        compiler_params=params(6),
        cost_estimate=takes(2),
        name="mid_grad",
    )(meta, mid_act_grad, mid_pre, belong, mid_merged, gain_mid, mid_sums, after)
    other = swap(send, "sp", 1)
    def space_grad_part(first_tap, taps, after):
        return pl.pallas_call(
            functools.partial(space_grad_kernel, first_tap),
            out_shape=(
                jax.ShapeDtypeStruct((taps, 1152, 128), F32),
                jax.ShapeDtypeStruct((taps, 1152, 128), BF16),
            ),
            in_specs=[SM, VM, HBM, VM, VM, VM, ANY, ANY],
            out_specs=(VM, VM),
            scratch_shapes=[
                pltpu.VMEM((3 * most, 3 * width), BF16),
                pltpu.VMEM((640, width), F32),
                pick_scratch,
                plane_scratch,
                pltpu.SemaphoreType.DMA((5 * most // 256,)),
            ],
            compiler_params=params(30),
            cost_estimate=takes(11),
            name="space_grad",
        )(meta, row_info, in_hbm(stored), outer_part, keep, other, *after)

    chunks = {"b": (0, 5), "c": (5, 4)}
    dense, edges, logits = {}, {}, {}
    left = {"t": 2 * steps - 1, "b": 2 * steps - 1, "c": 2 * steps - 1}
    space_grad = None
    last = {}
    after = send, send

    def step(name):
        left[name] -= 1
        token = chains[name].step(after)
        return token, token

    for event in PLAN:
        if event in "tbc":
            if left[event]:
                after = step(event)
        elif event in "BC":
            name = event.lower()
            keep_part, send_part = space_grad_part(*chunks[name], after)
            chains[name] = Chain("taps" + name, (keep_part, send_part), order, TURN)
            after = send_part, send_part
        elif event in "01":
            side = int(event)
            dense[side], edges[side], logits[side] = pl.pallas_call(
                functools.partial(input_back_kernel, side, frame_count),
                out_shape=(
                    jax.ShapeDtypeStruct((frame_count, cells, width), F32),
                    jax.ShapeDtypeStruct((frame_count, cells, width), BF16),
                    jax.ShapeDtypeStruct((clip_count, classes), F32),
                ),
                in_specs=[SM, VM, VM, HBM, VM, VM, VM, ANY, ANY],
                out_specs=(VM, VM, VM),
                scratch_shapes=[
                    pltpu.VMEM((6 * width, middle), BF16),
                    pltpu.VMEM((2, most // 2 + 256, 3 * width), BF16),
                    pltpu.VMEM((cells, 3 * cells), BF16),
                    pltpu.VMEM((most // 2 + 256, width), BF16),
                    pltpu.VMEM((most // 2 + 256, width), BF16),
                    pltpu.SemaphoreType.DMA(()),
                ],
                compiler_params=params(26),
                cost_estimate=takes(17),
                name="input_back",
            )(meta, col_info, mid_grad, weight, act_grad, pooled, class_lines, *after)
            if side == 0:
                scores = logits[0]
                for axis, bit in bits("sp"):
                    scores = scores + swap(scores, axis, bit)
                up = lax.ppermute(edges[0], "sp", [(i, i - 1) for i in range(1, sp_count)])
            else:
                down = lax.ppermute(edges[1], "sp", [(i, i + 1) for i in range(sp_count - 1)])
            after = edges[side], edges[side]
        elif event == "i":
            input_grad = pl.pallas_call(
                input_join_kernel,
                out_shape=jax.ShapeDtypeStruct((row_count, frame_count, clip_count, col_count, width), F32),
                in_specs=[SM, VM, VM, VM, VM, VM, ANY, ANY],
                out_specs=VM,
                scratch_shapes=[pltpu.VMEM((clip_count, 8, width), F32)],
                compiler_params=params(18),
                cost_estimate=takes(2),
                name="input_join",
            )(meta, col_info, dense[0], dense[1], down, up, after[0], scores)
            after = input_grad, input_grad
        elif event == "T":
            while left["t"]:
                after = step("t")
            own_half = chains["t"].state
            time_grad, class_weight_grad = pl.pallas_call(
                time_join_kernel,
                out_shape=(
                    jax.ShapeDtypeStruct((3 * middle, width), F32),
                    jax.ShapeDtypeStruct((classes, width), F32),
                ),
                in_specs=[SM, VM, VM, ANY, ANY],
                out_specs=(VM, VM),
                compiler_params=params(16),
                cost_estimate=takes(5),
                name="time_join",
            )(meta, own_half, trade(own_half, small_order, 0), *after)
            after = class_weight_grad, class_weight_grad
        elif event in "pq":
            name = "b" if event == "p" else "c"
            while left[name]:
                after = step(name)
            own_half = chains[name].state
            got_half = trade(own_half, order, 0)
            last[name] = [own_half, got_half, swap(own_half, "sp", 1), swap(got_half, "sp", 1)]
            after = after[0], got_half
        else:
            name = "b" if event == "P" else "c"
            first_tap, taps = chunks[name]
            piece = pl.BlockSpec((1, 1152, 128), lambda n, meta: (n, 0, 0))
            before = [] if space_grad is None else [space_grad]
            space_grad = pl.pallas_call(
                functools.partial(join_kernel, steps),
                grid_spec=pltpu.PrefetchScalarGridSpec(
                    num_scalar_prefetch=1,
                    grid=(taps,),
                    in_specs=[piece] * 4 + [ANY] * (2 + len(before)),
                    out_specs=pl.BlockSpec((1, width, middle), lambda n, meta, tap=first_tap: (n + tap, 0, 0)),
                ),
                out_shape=jax.ShapeDtypeStruct((9, width, middle), F32),
                input_output_aliases={7: 0} if before else {},
                compiler_params=params(12),
                cost_estimate=takes(6),
                name="join",
            )(meta, *last[name], *after, *before)
            after = after[0], space_grad
    space_grad = space_grad.reshape(3, 3, width, middle)
    input_grad = input_grad.transpose(2, 1, 0, 3, 4)
    time_grad = time_grad.reshape(3, middle, width)
    class_weight_grad = class_weight_grad.T
    logits = scores + class_bias
    return (
        logits,
        input_grad,
        space_grad,
        time_grad,
        gain_mid_grad,
        shift_mid_grad,
        gain_out_grad,
        shift_out_grad,
        class_weight_grad,
        class_bias_grad,
    )


def solution(mesh):
    placed = (
        P("dp", None, "sp", None, None),
        P(),
        P(),
        P(),
        P(),
        P(),
        P(),
        P(),
        P(),
        P("dp"),
        P("dp"),
        P("dp"),
        P("dp", None),
    )
    return jax.shard_map(
        shards,
        mesh=mesh,
        in_specs=placed,
        out_specs=(
            P("dp", None),
            P("dp", None, "sp", None, None),
            P(),
            P(),
            P(),
            P(),
            P(),
            P(),
            P(),
            P(),
        ),
        check_vma=False,
    )
```

```python
import functools

import jax
import jax.numpy as jnp
from jax import lax
from jax.experimental import pallas as pl
from jax.experimental.pallas import tpu as pltpu
from jax.sharding import PartitionSpec as P

EPSILON = 1e-05
HIGH = lax.Precision.HIGHEST
F32 = jnp.float32
BF16 = jnp.bfloat16
S_AT, CORE_AT, ROW_AT, OFF, LEN, PAD, END_AT, FIRST_AT, TURN, SMALL_TURN = 0, 1, 2, 4, 8, 12, 16, 17, 18, 33
META = 48

PLAN = "Bt0btCbt1bctcbticbtcbctbccpTPqQ"

VM = pl.BlockSpec(memory_space=pltpu.VMEM)
SM = pl.BlockSpec(memory_space=pltpu.SMEM)
ANY = pl.BlockSpec(memory_space=pl.ANY)
HBM = pl.BlockSpec(memory_space=pltpu.HBM)


def in_hbm(value):
    return pltpu.with_memory_space_constraint(value, pltpu.HBM)


STEP = 6


def takes(us):
    return pl.CostEstimate(flops=us * 1_100_000_000, bytes_accessed=us * 3_300_000, transcendentals=0)


def params(mib):
    return pltpu.CompilerParams(vmem_limit_bytes=mib << 20)


def nt_dot(a, b):
    return lax.dot_general(a, b, (((1,), (1,)), ((), ())), preferred_element_type=F32)


def tn_dot(a, b):
    return lax.dot_general(a, b, (((0,), (0,)), ((), ())), preferred_element_type=F32)


def dot(a, b):
    return jnp.dot(a, b, preferred_element_type=F32)


def split(value):
    high = value.astype(BF16)
    return high, (value - high.astype(F32)).astype(BF16)


def sigmoid(v):
    return 1.0 / (1.0 + jnp.exp(-v))


def slope(v):
    s = sigmoid(v)
    return s * (1.0 + v * (1.0 - s))


def at16(index):
    return pl.multiple_of(index, 16)


def at64(index):
    return pl.multiple_of(index, 64)


def at128(index):
    return pl.multiple_of(index, 128)


def sweep(rows, size, body):
    count = lax.div(rows, size)

    def one(m, carry):
        body(pl.multiple_of(m * size, size), size)
        return carry

    lax.fori_loop(0, count, one, 0)

    @pl.when(rows > count * size)
    def _():
        body(pl.multiple_of(count * size, size), size // 2)


def pick_rows(row_info, shift):
    place, col, cols = row_info[0:1, :], row_info[1:2, :], row_info[2:3, :]
    home = col - shift
    ok = (col < cols) & (home >= 0) & (home < cols)
    spot = jnp.where(ok, place - shift, -1)
    size = row_info.shape[1]
    index = lax.broadcasted_iota(jnp.int32, (size, size), 0)
    return jnp.where(index == spot, 1.0, 0.0).astype(BF16)


def pick_cols(col_info, shift):
    place, col, cols = col_info[:, 0:1], col_info[:, 1:2], col_info[:, 2:3]
    home = col - shift
    ok = (col < cols) & (home >= 0) & (home < cols)
    spot = jnp.where(ok, place - shift, -1)
    size = col_info.shape[0]
    index = lax.broadcasted_iota(jnp.int32, (size, size), 1)
    return jnp.where(index == spot, 1.0, 0.0).astype(BF16)


def each_list(meta, base, frame_count, store):
    for t in range(frame_count):
        for half in range(2):

            @pl.when(half * 128 < meta[PAD + t])
            def _(t=t, half=half):
                store(t, half, at16(base + meta[OFF + t] + half * 128))


def setup_kernel(
    sp_count, orders, where, frames, rows, cols, values, meta, row_info, col_info, clip_info, own, own_low, ahead, pad
):
    row_count, frame_count, clip_count, col_count, width = values.shape
    size = clip_count * 8
    core = lax.rem(where[1], 2)
    first_row = where[1] * row_count
    total = jnp.int32(0)
    for t in range(frame_count):
        length = jnp.int32(0)
        for b in range(clip_count):
            length += jnp.where(frames[b] > t, cols[b], 0)
        padded = (length + 15) // 16 * 16
        meta[OFF + t], meta[LEN + t], meta[PAD + t] = total, length, padded
        total += padded
    meta[S_AT], meta[CORE_AT], meta[ROW_AT] = (total + 63) // 64 * 64, core, first_row
    meta[END_AT] = total
    meta[FIRST_AT] = jnp.where(where[1] == 0, 1, 0)
    place = where[0] * sp_count + where[1]
    for start, (order, other) in zip((TURN, SMALL_TURN), orders):
        for n, (zero, one) in enumerate(zip(*order)):
            meta[start + n] = jnp.where(place & jnp.where(core == 0, zero, one) != 0, 1, 0)
        meta[start + len(order[0])] = jnp.where(place & jnp.where(core == 0, other[0], other[1]) != 0, 1, 0)

    lane = lax.broadcasted_iota(jnp.int32, (1, size), 1)
    clip, col = lax.shift_right_logical(lane, 3), lane & 7
    zero = jnp.zeros((1, size), jnp.int32)
    of_cell, of_clip = [zero] * 3, [zero] * 3
    for b in range(clip_count):
        for n, source in enumerate((cols, frames, rows)):
            of_cell[n] = jnp.where(clip == b, source[b], of_cell[n])
            of_clip[n] = jnp.where(lane == b, source[b], of_clip[n])
    start = zero
    for b in range(clip_count):
        ahead_of = (frames[b] > of_cell[1]) | ((frames[b] == of_cell[1]) & (clip > b))
        start += jnp.where(ahead_of, cols[b], 0)
    info = [start + col, col, of_cell[0], of_cell[1], of_cell[2], zero, zero, zero]
    for n, line in enumerate(info[:3] + of_clip[1:] + [zero] * 3):
        row_info[n : n + 1, :] = line
    col_info[...] = jnp.concatenate(info, axis=0).astype(F32).T.astype(jnp.int32)
    per_clip = jnp.maximum(of_clip[0] * of_clip[1] * of_clip[2], 1).astype(F32)[:, 0:128]
    clip_info[...] = jnp.concatenate([per_clip] * 8, axis=0).T

    pad[:, col_count:, :] = jnp.zeros((clip_count, 8 - col_count, width), F32)
    cells = col_info[...]
    for h in range(row_count):
        for t in range(frame_count):
            pad[:, 0:col_count, :] = values[h, t]
            inside = (cells[:, 1:2] < cells[:, 2:3]) & (cells[:, 3:4] > t) & (cells[:, 4:5] > first_row + h)
            masked = pad[...].reshape(size, width) * jnp.where(inside, 1.0, 0.0)
            own[h, t], own_low[h, t] = split(masked)

            @pl.when(core == h)
            def _(t=t, masked=masked):
                ahead[t] = masked.astype(BF16)


def gather_setup(row_info, pick):
    info = row_info[...]
    for j in range(3):
        hot = pick_rows(info, j - 1)
        for half in range(2):
            pick[half, j * 128 : (j + 1) * 128, :] = hot[half * 128 : (half + 1) * 128, :]


def gather_plane(meta, pick, source, packed, base, frame_count):
    def store(t, half, row):
        got = dot(pick[half], source(t)).astype(BF16)
        for j in range(3):
            packed[pl.ds(row, 128), j * 512 : (j + 1) * 512] = got[j * 128 : (j + 1) * 128, :]

    each_list(meta, base, frame_count, store)
    packed[pl.ds(at16(base + meta[END_AT]), 128), :] = jnp.zeros((128, 1536), BF16)


def copy_out(rows, source, begin, target, start, sems, action):
    def one(m, carry):
        copy = pltpu.make_async_copy(
            source.at[pl.ds(at64(begin + m * 64), 64)], target.at[pl.ds(at64(start + m * 64), 64)], sems.at[m]
        )
        if action == "start":
            copy.start()
        else:
            copy.wait()
        return carry

    lax.fori_loop(0, lax.div(rows, 64), one, 0)


def space_kernel(
    meta, row_info, own, own_low, part, weight_in, logit_grad, class_weight, clip_info,
    mid_pre, belong, residual, stored, pooled_grad, bias_grad, packed, pick, weight, sems, load,
):
    frame_count = own.shape[1]
    core = meta[CORE_AT]
    s = meta[S_AT]
    fetch = pltpu.make_async_copy(weight_in, weight, load)
    fetch.start()
    gather_setup(row_info, pick)

    @pl.when(core == 0)
    def _():
        for h in range(2):
            gather_plane(meta, pick, lambda t, h=h: own[h, t], packed, h * s, frame_count)
        for h in range(2):
            gather_plane(meta, pick, lambda t, h=h: part[h, t], packed, (2 + h) * s, frame_count)

    @pl.when(core != 0)
    def _():
        for h in range(2):
            gather_plane(meta, pick, lambda t, h=h: part[h, t], packed, h * s, frame_count)
        for h in range(2):
            gather_plane(meta, pick, lambda t, h=h: own[h, t], packed, (2 + h) * s, frame_count)

    copy_out(4 * s, packed, 0, stored, s, sems, "start")
    size = row_info.shape[1]
    clip_of = lax.broadcasted_iota(jnp.int32, (size, 128), 0) // 8
    lane = lax.broadcasted_iota(jnp.int32, (size, 128), 1)
    frames_of = jnp.broadcast_to(row_info[3:4, 0:128], (size, 128))
    rows_of = jnp.broadcast_to(row_info[4:5, 0:128], (size, 128))
    for h in range(2):

        def store(t, half, row, h=h):
            hot = pick[half, 128:256, :]
            inside = (clip_of == lane) & (frames_of > t) & (rows_of > meta[ROW_AT] + h)
            belong[pl.ds(row, 128), :] = dot(hot, jnp.where(inside, 1.0, 0.0).astype(BF16)).astype(BF16)
            residual[pl.ds(row, 128), :] = dot(hot, own[h, t]) + dot(hot, own_low[h, t])

        each_list(meta, h * s, frame_count, store)
        belong[pl.ds(at16(h * s + meta[END_AT]), 128), :] = jnp.zeros((128, 128), BF16)
        residual[pl.ds(at16(h * s + meta[END_AT]), 128), :] = jnp.zeros((128, 512), F32)
    clips, classes = logit_grad.shape
    pooled_grad[...] = jnp.zeros(pooled_grad.shape, F32)
    pooled_grad[0:clips, :] = (
        jnp.dot(logit_grad[...], class_weight[...], precision=HIGH, preferred_element_type=F32)
        / clip_info[0:clips, 0:1]
    )
    bias_grad[...] = jnp.zeros(bias_grad.shape, F32)
    bias_grad[:, 0:classes] = jnp.sum(logit_grad[...], axis=0, keepdims=True) * meta[FIRST_AT].astype(F32)
    fetch.wait()
    for h in range(2):

        def conv(row, size, h=h):
            rows = pl.ds(at64(h * s + row), size)

            def tap(i):
                source = packed[pl.ds(at64((2 * core + h + i - 1) * s + row), size), :]
                return dot(source, weight[i * 1536 : (i + 1) * 1536, :])

            mid_pre[rows, :] = tap(1) + tap(2 - 2 * h)

            @pl.when(core == 1 - h)
            def _():
                mid_pre[rows, :] += tap(2 * h)

        sweep(s, 128, conv)
    copy_out(4 * s, packed, 0, stored, s, sems, "wait")


def mask_of(belong, row, size):
    return jnp.sum(belong[pl.ds(row, size), :].astype(F32), axis=1, keepdims=True)


def norm_of(merged):
    count = merged[0:1, :]
    return merged[1:2, :] / count, lax.rsqrt(merged[2:3, :] / count + EPSILON)


def norm_sums(meta, values, belong, stats):
    mask = mask_of(belong, 0, 128)
    pivot = jnp.sum(values[0:128, :] * mask, axis=0, keepdims=True) / jnp.maximum(jnp.sum(mask), 1.0)
    stats[...] = jnp.zeros(stats.shape, F32)

    def sums(row, size):
        mask = mask_of(belong, row, size)
        off = (values[pl.ds(row, size), :] - pivot) * mask
        stats[0:1, :] += jnp.sum(mask, axis=0, keepdims=True)
        stats[1:2, :] += jnp.sum(off, axis=0, keepdims=True)
        stats[2:3, :] += jnp.sum(off * off, axis=0, keepdims=True)

    sweep(2 * meta[S_AT], 256, sums)
    count, total = stats[0:1, :], stats[1:2, :]
    stats[2:3, :] = jnp.maximum(stats[2:3, :] - total * total / count, 0.0)
    stats[1:2, :] = total + count * pivot


def space_edge_kernel(
    meta, row_info, mid_in, stored_in, outer, weight_in, belong, mid_pre, stored, stats, pick, plane, weight, sems, load
):
    core = meta[CORE_AT]
    s = meta[S_AT]
    fetch = pltpu.make_async_copy(
        weight_in.at[pl.ds(pl.multiple_of(core * 3072, 1024), 1536)], weight, load
    )
    fetch.start()
    gather_setup(row_info, pick)
    gather_plane(meta, pick, lambda t: outer[t], plane, 0, outer.shape[0])
    copy_out(s, plane, 0, stored, 5 * s * core, sems, "start")
    fetch.wait()

    def conv(row, size):
        mid_pre[pl.ds(at64(core * s + row), size), :] += dot(plane[pl.ds(row, size), :], weight[...])

    sweep(s, 128, conv)
    norm_sums(meta, mid_pre, belong, stats)
    copy_out(s, plane, 0, stored, 5 * s * core, sems, "wait")


def shift_lists(meta, frame_count, source, target, width, move):
    s = meta[S_AT]
    for h in range(2):

        def store(t, half, row, h=h):
            other = t + move
            if 0 <= other < frame_count:
                block = source(at16(h * s + meta[OFF + other] + half * 128))
                place = half * 128 + lax.broadcasted_iota(jnp.int32, (128, 1), 0)
                keep = jnp.where(place < meta[LEN + other], 1.0, 0.0).astype(BF16)
                target(row, block * keep)
            else:
                target(row, jnp.zeros((128, width), BF16))

        each_list(meta, h * s, frame_count, store)
        target(at16(h * s + meta[END_AT]), jnp.zeros((128, width), BF16))


def time_kernel(
    frame_count, meta, mid_pre, belong, merged, gain, shift, weight, after, mid_low, out_pre, stats, wide
):
    rows = 2 * meta[S_AT]
    center, scale = norm_of(merged)

    def act(row, size):
        block = pl.ds(row, size)
        value = gain[...] * ((mid_pre[block, :] - center) * scale) + shift[...]
        low = (value * sigmoid(value) * mask_of(belong, row, size)).astype(BF16)
        wide[block, 1152:2304] = low
        mid_low[block, :] = low

    sweep(rows, 256, act)
    wide[pl.ds(at128(rows), 256), :] = jnp.zeros((256, 3456), BF16)
    for k in (0, 2):

        def source(row):
            return wide[pl.ds(row, 128), 1152:2304]

        def target(row, value, k=k):
            wide[pl.ds(row, 128), k * 1152 : (k + 1) * 1152] = value

        shift_lists(meta, frame_count, source, target, 1152, k - 1)

    def conv(row, size):
        out_pre[pl.ds(row, size), :] = dot(wide[pl.ds(row, size), :], weight[...])

    sweep(rows, 256, conv)
    norm_sums(meta, out_pre, belong, stats)


def act_kernel(
    meta, out_pre, belong, residual, merged, gain_ref, shift_ref, pooled_grad, bias_grad, clip_info,
    act_grad, stats, pooled,
):
    center, scale = norm_of(merged)
    high, rest = split(pooled_grad[...])
    pooled[...] = jnp.zeros(pooled.shape, F32)
    stats[...] = jnp.zeros(stats.shape, F32)

    def step(row, size):
        block = pl.ds(row, size)
        hot = belong[block, :]
        normed = (out_pre[block, :] - center) * scale
        value = gain_ref[...] * normed + shift_ref[...] + residual[block, :]
        s = sigmoid(value)
        first, second = split(value * s)
        pooled[...] += tn_dot(hot, first) + tn_dot(hot, second)
        grad = (dot(hot, high) + dot(hot, rest)) * (s * (1.0 + value * (1.0 - s)))
        act_grad[block, :] = grad
        stats[0:1, :] += jnp.sum(grad, axis=0, keepdims=True)
        stats[1:2, :] += jnp.sum(grad * normed, axis=0, keepdims=True)

    sweep(2 * meta[S_AT], 256, step)
    stats[2:3, :] = bias_grad[...]
    pooled[...] = pooled[...] / clip_info[:, 0:1]


def back_kernel(
    frame_count, meta, act_grad, out_pre, belong, out_merged, out_gain, out_sums, weight, mid_pre, mid_merged,
    mid_gain, mid_shift, wide, mid_act_grad, stats,
):
    rows = 2 * meta[S_AT]
    out_center, out_scale = norm_of(out_merged)
    mid_center, mid_scale = norm_of(mid_merged)
    out_shift_part = out_sums[0:1, :] / out_merged[0:1, :]
    out_gain_part = out_sums[1:2, :] / out_merged[0:1, :]
    stats[...] = jnp.zeros(stats.shape, F32)

    def grad(row, size):
        block = pl.ds(row, size)
        normed = (out_pre[block, :] - out_center) * out_scale
        inner = act_grad[block, :] - mask_of(belong, row, size) * (out_shift_part + normed * out_gain_part)
        wide[block, 512:1024] = (out_gain[...] * out_scale * inner).astype(BF16)

    sweep(rows, 256, grad)
    wide[pl.ds(at128(rows), 256), :] = jnp.zeros((256, 1536), BF16)
    for k in (0, 2):

        def source(row):
            return wide[pl.ds(row, 128), 512:1024]

        def target(row, value, k=k):
            wide[pl.ds(row, 128), k * 512 : (k + 1) * 512] = value

        shift_lists(meta, frame_count, source, target, 512, 1 - k)

    def conv(row, size):
        block = pl.ds(row, size)
        acc = nt_dot(wide[block, 0:512], weight[0])
        acc += nt_dot(wide[block, 512:1024], weight[1])
        acc += nt_dot(wide[block, 1024:1536], weight[2])
        normed = (mid_pre[block, :] - mid_center) * mid_scale
        acc = acc * mask_of(belong, row, size) * slope(mid_gain[...] * normed + mid_shift[...])
        mid_act_grad[block, :] = acc
        stats[0:1, :] += jnp.sum(acc, axis=0, keepdims=True)
        stats[1:2, :] += jnp.sum(acc * normed, axis=0, keepdims=True)

    sweep(rows, 256, conv)


def time_grad_kernel(meta, mid_low, wide, pooled, logit_grad, stats, keep, send, passed, total):
    passed[...] = stats[...]
    core = meta[CORE_AT]
    middle = mid_low.shape[1]
    classes = logit_grad.shape[1]
    half = keep.shape[1]
    for k in range(3):
        rows = slice(k * middle, (k + 1) * middle)
        total[rows, :] = jnp.zeros((middle, 512), F32)

        def step(row, size, k=k, rows=rows):
            block = pl.ds(row, size)
            total[rows, :] += tn_dot(mid_low[block, :], wide[block, k * 512 : (k + 1) * 512])

        sweep(2 * meta[S_AT], 256, step)
    total[3 * middle : 3 * middle + classes, :] = lax.dot_general(
        logit_grad[...], pooled[0 : logit_grad.shape[0], :], (((0,), (0,)), ((), ())), precision=HIGH, preferred_element_type=F32
    )
    total[3 * middle + classes :, :] = jnp.zeros((2 * half - 3 * middle - classes, 512), F32)
    for lane in range(4):
        lanes = slice(lane * 128, (lane + 1) * 128)
        keep[lane] = total[pl.ds(at128(core * half), half), lanes]
        send[lane] = total[pl.ds(at128((1 - core) * half), half), lanes].astype(BF16)


def relay_kernel(got, *rest):
    rest[-1][...] = got[...]


def time_join_kernel(meta, own, got, after, also, time_grad, class_grad, token):
    token[...] = jnp.zeros(token.shape, F32)
    half = own.shape[1]
    rest = time_grad.shape[0] - half

    def place(first, second):
        for lane in range(4):
            lanes = slice(lane * 128, (lane + 1) * 128)
            time_grad[0:half, lanes] = first[lane].astype(F32)
            time_grad[half:, lanes] = second[lane, 0:rest, :].astype(F32)
            class_grad[:, lanes] = second[lane, rest : rest + class_grad.shape[0], :].astype(F32)

    @pl.when(meta[CORE_AT] == 0)
    def _():
        place(own, got)

    @pl.when(meta[CORE_AT] != 0)
    def _():
        place(got, own)


def mid_grad_kernel(meta, mid_act_grad, mid_pre, belong, merged, gain, sums, after, whole, keep, send):
    core = meta[CORE_AT]
    center, scale = norm_of(merged)
    shift_part = sums[0:1, :] / merged[0:1, :]
    gain_part = sums[1:2, :] / merged[0:1, :]

    def step(row, size):
        block = pl.ds(row, size)
        normed = (mid_pre[block, :] - center) * scale
        inner = mid_act_grad[block, :] - mask_of(belong, row, size) * (shift_part + normed * gain_part)
        low = (gain[...] * scale * inner).astype(BF16)
        whole[block, :] = low

        @pl.when(core == 0)
        def _():
            keep[block, 0:512] = low[:, 0:512]
            send[block, 0:512] = low[:, 512:1024]

        @pl.when(core != 0)
        def _():
            keep[block, 0:512] = low[:, 512:1024]
            send[block, 0:512] = low[:, 0:512]

        keep[block, 512:640] = low[:, 1024:1152]
        send[block, 512:640] = low[:, 1024:1152]

    sweep(2 * meta[S_AT], 256, step)


def space_grad_taps(first_tap, meta, packed, own, part, keep, send, total):
    core = meta[CORE_AT]
    s = meta[S_AT]
    mine = meta[TURN]

    def one(tap, carry):
        i, j = lax.div(first_tap + tap, 3), lax.rem(first_tap + tap, 3)
        lanes = pl.ds(at128(j * 512), 512)

        total[...] = jnp.zeros(total.shape, F32)

        def step(row, size):
            first = packed[pl.ds(at64((2 * core + i) * s + row), size), lanes]
            second = packed[pl.ds(at64((2 - 2 * core + i) * s + row), size), lanes]
            total[...] += tn_dot(own[pl.ds(row, size), :], first) + tn_dot(part[pl.ds(row, size), :], second)

        sweep(2 * s, 256, step)
        for half, out, kind in ((mine, keep, F32), (1 - mine, send, BF16)):
            lane = half * 256
            out[tap, 0:512, :] = total[0:512, pl.ds(at128(lane), 128)].astype(kind)
            out[tap, 512:1024, :] = total[0:512, pl.ds(at128(lane + 128), 128)].astype(kind)
            out[tap, 1024:1152, :] = total[512:640, pl.ds(at128(core * 256 + half * 128), 128)].astype(kind)
        return carry

    lax.fori_loop(0, keep.shape[0], one, 0)


def space_rows(meta, row_info, stored, outer, packed, pick, plane, sems):
    core = meta[CORE_AT]
    s = meta[S_AT]
    copy_out(5 * s, stored, core * s, packed, core * s, sems, "start")
    gather_setup(row_info, pick)
    gather_plane(meta, pick, lambda t: outer[t], plane, 0, outer.shape[0])

    def put(row, size):
        packed[pl.ds(at64(5 * s * (1 - core) + row), size), :] = plane[pl.ds(row, size), :]

    sweep(s, 128, put)
    copy_out(5 * s, stored, core * s, packed, core * s, sems, "wait")


def space_rows_kernel(meta, row_info, stored, outer, after, packed, pick, plane, sems):
    space_rows(meta, row_info, stored, outer, packed, pick, plane, sems)


def space_grad_kernel(
    first_tap, meta, row_info, stored, outer, own, part, after, also, keep, send, packed, total, pick, plane, sems
):
    space_rows(meta, row_info, stored, outer, packed, pick, plane, sems)
    space_grad_taps(first_tap, meta, packed, own, part, keep, send, total)


def space_grad_first_kernel(first_tap, meta, packed, own, part, after, also, keep, send, total):
    space_grad_taps(first_tap, meta, packed, own, part, keep, send, total)


def halve_kernel(at, meta, keep, got, after, also, next_keep, next_send):
    half = next_keep.shape[1]
    mine = meta[at]

    def one(tap, carry):
        low, high = pl.ds(at16(mine * half), half), pl.ds(at16((1 - mine) * half), half)
        next_keep[tap] = keep[tap, low, :] + got[tap, low, :].astype(F32)
        next_send[tap] = (keep[tap, high, :] + got[tap, high, :].astype(F32)).astype(BF16)
        return carry

    lax.fori_loop(0, keep.shape[0], one, 0)


def halve_pass_kernel(at, meta, keep, got, value, next_keep, next_send, passed):
    passed[...] = value[...]
    halve_kernel(at, meta, keep, got, None, None, next_keep, next_send)


def share_kernel(keep, got, after, also, out):
    def one(tap, carry):
        out[tap] = (keep[tap] + got[tap].astype(F32)).astype(BF16)
        return carry

    lax.fori_loop(0, keep.shape[0], one, 0)


def double_kernel(at, meta, own, got, after, also, out):
    half = own.shape[1]
    mine = meta[at]

    def one(tap, carry):
        out[tap, pl.ds(at16(mine * half), half), :] = own[tap]
        out[tap, pl.ds(at16((1 - mine) * half), half), :] = got[tap]
        return carry

    lax.fori_loop(0, own.shape[0], one, 0)


def input_back_kernel(
    side, frame_count, meta, col_info, grad, weight_in, act_grad, pooled, class_weight, after, also,
    dense, edge, logits, weight, wide, spread, high, rest, load,
):
    s = meta[S_AT]
    fetch = pltpu.make_async_copy(weight_in.at[pl.ds(side * 1536, 3072)], weight, load)
    fetch.start()
    if side == 0:
        logits[...] = lax.dot_general(
            pooled[0 : logits.shape[0], :],
            class_weight[...],
            (((1,), (1,)), ((), ())),
            precision=HIGH,
            preferred_element_type=F32,
        )
    else:
        logits[...] = jnp.zeros(logits.shape, F32)
    info = col_info[...]
    for j in range(3):
        spread[:, j * 256 : (j + 1) * 256] = pick_cols(info, j - 1)

    def cut(row, size):
        first, second = split(act_grad[pl.ds(at64(side * s + row), size), :])
        high[pl.ds(row, size), :] = first
        rest[pl.ds(row, size), :] = second

    sweep(s, 128, cut)
    for part in (high, rest):
        part[pl.ds(at64(s), 256), :] = jnp.zeros((256, 512), BF16)
    for plane in range(2):
        wide[plane, pl.ds(at64(s), 256), :] = jnp.zeros((256, 1536), BF16)
    fetch.wait()
    outer_weight, inner_weight = weight[0:1536, :], weight[1536:3072, :]
    if side:
        outer_weight, inner_weight = inner_weight, outer_weight

    def conv(row, size):
        near, far = grad[pl.ds(at64(side * s + row), size), :], grad[pl.ds(at64((1 - side) * s + row), size), :]
        both = nt_dot(jnp.concatenate([near, far], axis=0), outer_weight)
        wide[0, pl.ds(row, size), :] = both[0:size, :].astype(BF16)
        wide[1, pl.ds(row, size), :] = (both[size:, :] + nt_dot(near, inner_weight)).astype(BF16)

    sweep(s, 128, conv)
    for t in range(frame_count):

        def scatter(size, t=t):
            rows = pl.ds(at16(meta[OFF + t]), size)
            edge_acc = inner = None
            for j in range(3):
                hot = spread[:, j * 256 : j * 256 + size]
                first = dot(hot, wide[0, rows, j * 512 : (j + 1) * 512])
                second = dot(hot, wide[1, rows, j * 512 : (j + 1) * 512])
                edge_acc = first if j == 0 else edge_acc + first
                inner = second if j == 0 else inner + second
            hot = spread[:, 256 : 256 + size]
            edge[t] = edge_acc.astype(BF16)
            dense[t] = inner + dot(hot, high[rows, :]) + dot(hot, rest[rows, :])

        @pl.when(meta[LEN + t] > 128)
        def _(scatter=scatter):
            scatter(256)

        @pl.when(meta[LEN + t] <= 128)
        def _(scatter=scatter):
            scatter(128)


def input_join_kernel(meta, col_info, first, second, down, up, after, also, out, token, pad):
    frame_count, clip_count, col_count, width = out.shape[1:]
    token[...] = jnp.zeros(token.shape, F32)
    cells = col_info[...]
    for h, (own, got) in enumerate(((first, down), (second, up))):
        for t in range(frame_count):
            inside = (cells[:, 1:2] < cells[:, 2:3]) & (cells[:, 3:4] > t) & (cells[:, 4:5] > meta[ROW_AT] + h)
            value = jnp.where(inside, own[t] + got[t].astype(F32), 0.0)
            pad[...] = value.reshape(clip_count, 8, width)
            out[h, t] = pad[:, 0:col_count, :]


def join_kernel(steps, meta, own, got, part_own, part_got, after, also, *rest):
    out, token = rest[-2:]
    token[...] = jnp.zeros(token.shape, F32)
    core = meta[CORE_AT]
    mine, other = meta[TURN], meta[TURN + steps]
    for piece, half, owner in (
        (own, mine, core),
        (got, 1 - mine, core),
        (part_own, other, 1 - core),
        (part_got, 1 - other, 1 - core),
    ):
        row = half * 256
        middles = pl.ds(at128(owner * 512), 512)
        out[0, pl.ds(at128(row), 128), middles] = piece[0, 0:512, :].astype(F32).T
        out[0, pl.ds(at128(row + 128), 128), middles] = piece[0, 512:1024, :].astype(F32).T
        out[0, pl.ds(at128(owner * 256 + half * 128), 128), 1024:1152] = piece[0, 1024:1152, :].astype(F32).T


def swap(value, axis, bit):
    size = lax.axis_size(axis)
    if size <= bit:
        return None
    return lax.ppermute(value, axis, [(i, i ^ bit) for i in range(size)])


def bits(axis):
    return [(axis, 1 << n) for n in range((lax.axis_size(axis) - 1).bit_length())]


def sum_all(value, axes):
    for axis, bit in axes:
        value = value + swap(value, axis, bit)
    return value


def merge_all(stats):
    stats = stats[:3]
    row = lax.broadcasted_iota(jnp.int32, stats.shape, 0)
    for axis, bit in bits("sp") + bits("dp"):
        other = swap(stats, axis, bit)
        gap = stats[1] / stats[0] - other[1] / other[0]
        extra = gap * gap * (stats[0] * other[0] / (stats[0] + other[0]))
        stats = stats + other + jnp.where(row == 2, extra[None], 0.0)
    return stats


def trade(value, order, stage):
    size = lax.axis_size(("dp", "sp"))
    return lax.ppermute(value, ("dp", "sp"), [(i, i ^ order[i % 2][stage]) for i in range(size)])


def halve_step(keep, send, order, meta, at, stage, after, name):
    got = trade(send, order, stage)
    n, rows, lanes = keep.shape
    if stage + 1 == len(order[0]):
        share = pl.pallas_call(
            share_kernel,
            out_shape=jax.ShapeDtypeStruct(keep.shape, BF16),
            in_specs=[VM, VM, ANY, ANY],
            out_specs=VM,
            compiler_params=params(6),
            cost_estimate=takes(STEP),
            name=name + "_share",
        )(keep, got, *after)
        return share, None
    half = rows // 2
    if half % 16:
        pairs = (keep + got.astype(F32)).reshape(n, 2, half, lanes)
        mine = meta[at + stage + 1]
        keep = lax.dynamic_index_in_dim(pairs, mine, 1, keepdims=False)
        send = lax.dynamic_index_in_dim(pairs, 1 - mine, 1, keepdims=False).astype(BF16)
        return keep, send
    return pl.pallas_call(
        functools.partial(halve_kernel, at + stage + 1),
        out_shape=(
            jax.ShapeDtypeStruct((n, half, lanes), F32),
            jax.ShapeDtypeStruct((n, half, lanes), BF16),
        ),
        in_specs=[SM, VM, VM, ANY, ANY],
        out_specs=(VM, VM),
        compiler_params=params(10),
        cost_estimate=takes(STEP),
        name=name + "_halve%d" % stage,
    )(meta, keep, got, *after)


def double_step(own, order, meta, at, stage, after, name):
    got = trade(own, order, stage)
    n, rows, lanes = own.shape
    if rows % 16:
        mine = meta[at + stage]
        return jnp.concatenate([jnp.where(mine == 0, own, got), jnp.where(mine == 0, got, own)], axis=1)
    return pl.pallas_call(
        functools.partial(double_kernel, at + stage),
        out_shape=jax.ShapeDtypeStruct((n, 2 * rows, lanes), BF16),
        in_specs=[SM, VM, VM, ANY, ANY],
        out_specs=VM,
        compiler_params=params(8),
        cost_estimate=takes(STEP),
        name=name + "_double%d" % stage,
    )(meta, own, got, *after)


def shards(
    clip_input,
    space_weight,
    time_weight,
    gain_mid,
    shift_mid,
    gain_out,
    shift_out,
    class_weight,
    class_bias,
    frames,
    rows,
    cols,
    logit_grad,
):
    clip_count, frame_count, row_count, col_count, width = clip_input.shape
    middle = space_weight.shape[-1]
    classes = class_weight.shape[1]
    cells = clip_count * 8
    most = row_count * frame_count * clip_count * col_count
    sp_count = lax.axis_size("sp")
    x = [bit for _, bit in bits("sp")[1:]]
    y, z = [[bit * sp_count for _, bit in part] for part in (bits("dp")[:1], bits("dp")[1:])]
    order = x + y + z, y + x + z
    small_order = [1] + order[0], [1] + order[1]
    steps = len(order[0])
    orders = (order, (order[1][0], order[0][0])), (small_order, (1, 1))
    place = jnp.stack([lax.axis_index("dp"), lax.axis_index("sp")]).astype(jnp.int32)
    cells_shape = (row_count, frame_count, cells, width)
    meta, row_info, col_info, clip_info, own, own_low, ahead = pl.pallas_call(
        functools.partial(setup_kernel, sp_count, orders),
        out_shape=(
            jax.ShapeDtypeStruct((META,), jnp.int32),
            jax.ShapeDtypeStruct((8, cells), jnp.int32),
            jax.ShapeDtypeStruct((cells, 8), jnp.int32),
            jax.ShapeDtypeStruct((128, 8), F32),
            jax.ShapeDtypeStruct(cells_shape, BF16),
            jax.ShapeDtypeStruct(cells_shape, BF16),
            jax.ShapeDtypeStruct(cells_shape[1:], BF16),
        ),
        in_specs=[SM, SM, SM, SM, VM],
        out_specs=(SM, VM, VM, VM, VM, VM, VM),
        scratch_shapes=[pltpu.VMEM((clip_count, 8, width), F32)],
        compiler_params=params(20),
        cost_estimate=takes(3),
        name="setup",
    )(place, frames, rows, cols, clip_input.transpose(2, 1, 0, 3, 4))
    class_lines = class_weight.T

    part = swap(own, "sp", 1)
    across = [(i, i + 1 if i % 2 else i - 1) for i in range(sp_count)]
    outer = lax.ppermute(ahead, "sp", [(i, j) for i, j in across if 0 <= j < sp_count])
    outer_part = swap(outer, "sp", 1)

    weight = in_hbm(space_weight.reshape(9 * width, middle))
    stored_shape = pltpu.HBM((3 * most, 3 * width), BF16)
    pick_scratch = pltpu.VMEM((2, 384, cells), BF16)
    plane_scratch = pltpu.VMEM((most // 2 + 256, 3 * width), BF16)
    plane_sems = pltpu.SemaphoreType.DMA((most // 128,))
    mid_pre, belong, residual, stored, pooled_grad, bias_grad = pl.pallas_call(
        space_kernel,
        out_shape=(
            pltpu.VMEM((most, middle), F32),
            pltpu.VMEM((most + 256, 128), BF16),
            pltpu.VMEM((most + 256, width), F32),
            stored_shape,
            pltpu.VMEM((128, width), F32),
            pltpu.VMEM((1, width), F32),
        ),
        in_specs=[SM, VM, VM, VM, VM, HBM, VM, VM, VM],
        out_specs=(VM, VM, VM, HBM, VM, VM),
        scratch_shapes=[
            pltpu.VMEM((2 * most + 256, 3 * width), BF16),
            pick_scratch,
            pltpu.VMEM((9 * width, middle), BF16),
            pltpu.SemaphoreType.DMA((most // 32,)),
            pltpu.SemaphoreType.DMA(()),
        ],
        compiler_params=params(30),
        cost_estimate=takes(17),
        name="space_conv",
    )(meta, row_info, own, own_low, part, weight, logit_grad, class_lines, clip_info)
    mid_pre, stored, stats = pl.pallas_call(
        space_edge_kernel,
        out_shape=(
            pltpu.VMEM((most, middle), F32),
            stored_shape,
            jax.ShapeDtypeStruct((3, middle), F32),
        ),
        in_specs=[SM, VM, VM, HBM, VM, HBM, VM],
        out_specs=(VM, HBM, VM),
        scratch_shapes=[
            pick_scratch,
            plane_scratch,
            pltpu.VMEM((3 * width, middle), BF16),
            plane_sems,
            pltpu.SemaphoreType.DMA(()),
        ],
        input_output_aliases={2: 0, 3: 1},
        compiler_params=params(13),
        cost_estimate=takes(8),
        name="space_edge",
    )(meta, row_info, mid_pre, in_hbm(stored), outer, weight, belong)
    gain_mid, shift_mid = gain_mid[None], shift_mid[None]
    gain_out, shift_out = gain_out[None], shift_out[None]
    mid_merged = merge_all(stats)
    mid_low, out_pre, stats = pl.pallas_call(
        functools.partial(time_kernel, frame_count),
        out_shape=(
            pltpu.VMEM((most, middle), BF16),
            pltpu.VMEM((most, width), F32),
            jax.ShapeDtypeStruct((3, width), F32),
        ),
        in_specs=[SM, VM, VM, VM, VM, VM, VM, ANY],
        out_specs=(VM, VM, VM),
        scratch_shapes=[pltpu.VMEM((most + 256, 3 * middle), BF16)],
        compiler_params=params(24),
        cost_estimate=takes(8),
        name="time_conv",
    )(meta, mid_pre, belong, mid_merged, gain_mid, shift_mid, time_weight.reshape(3 * middle, width), outer_part)

    out_merged = merge_all(stats)
    act_grad, stats, pooled = pl.pallas_call(
        act_kernel,
        out_shape=(
            pltpu.VMEM((most, width), F32),
            jax.ShapeDtypeStruct((3, width), F32),
            jax.ShapeDtypeStruct((128, width), F32),
        ),
        in_specs=[SM] + [VM] * 9,
        out_specs=(VM, VM, VM),
        compiler_params=params(6),
        cost_estimate=takes(3),
        name="act",
    )(meta, out_pre, belong, residual, out_merged, gain_out, shift_out, pooled_grad, bias_grad, clip_info)

    out_sums = sum_all(stats, bits("sp") + bits("dp"))
    shift_out_grad, gain_out_grad, class_bias_grad = out_sums[0], out_sums[1], out_sums[2, :classes]
    wide, mid_act_grad, stats = pl.pallas_call(
        functools.partial(back_kernel, frame_count),
        out_shape=(
            pltpu.VMEM((most + 256, 3 * width), BF16),
            pltpu.VMEM((most, middle), F32),
            jax.ShapeDtypeStruct((2, middle), F32),
        ),
        in_specs=[SM] + [VM] * 11,
        out_specs=(VM, VM, VM),
        compiler_params=params(10),
        cost_estimate=takes(6),
        name="time_back",
    )(
        meta, act_grad, out_pre, belong, out_merged, gain_out, out_sums, time_weight, mid_pre, mid_merged,
        gain_mid, shift_mid,
    )

    small_half = 2048
    *small, stats = pl.pallas_call(
        time_grad_kernel,
        out_shape=(
            jax.ShapeDtypeStruct((4, small_half, 128), F32),
            jax.ShapeDtypeStruct((4, small_half, 128), BF16),
            jax.ShapeDtypeStruct((2, middle), F32),
        ),
        in_specs=[SM] + [VM] * 5,
        out_specs=(VM, VM, VM),
        scratch_shapes=[pltpu.VMEM((2 * small_half, width), F32)],
        compiler_params=params(13),
        cost_estimate=takes(8),
        name="time_grad",
    )(meta, mid_low, wide, pooled, logit_grad, stats)

    got = trade(small[1], small_order, 0)
    axes = bits("sp") + bits("dp")
    mid_sums = sum_all(stats, axes[:2])
    *small, mid_sums = pl.pallas_call(
        functools.partial(halve_pass_kernel, SMALL_TURN + 1),
        out_shape=(
            jax.ShapeDtypeStruct((4, small_half // 2, 128), F32),
            jax.ShapeDtypeStruct((4, small_half // 2, 128), BF16),
            jax.ShapeDtypeStruct((2, middle), F32),
        ),
        in_specs=[SM, VM, VM, VM],
        out_specs=(VM, VM, VM),
        compiler_params=params(8),
        cost_estimate=takes(1),
        name="time_halve",
    )(meta, small[0], got, mid_sums)
    mid_sums = sum_all(mid_sums, axes[2:])

    class Chain:
        def __init__(self, name, state, order, at):
            self.name, self.state, self.order, self.at = name, state, order, at
            self.stage, self.down = 0, True

        def step(self, after):
            if self.down:
                self.state = halve_step(*self.state, self.order, meta, self.at, self.stage, after, self.name)
                self.stage += 1
                if self.state[1] is None:
                    self.state, self.down, self.stage = self.state[0], False, self.stage - 1
            else:
                self.state = double_step(self.state, self.order, meta, self.at, self.stage, after, self.name)
                self.stage -= 1
            return self.state[0] if self.down else self.state

    chains = {"t": Chain("time", small, small_order, SMALL_TURN)}
    chains["t"].stage = 1
    after = chains["t"].step((mid_sums, mid_sums))
    shift_mid_grad, gain_mid_grad = mid_sums[0], mid_sums[1]
    mid_grad, keep, send = pl.pallas_call(
        mid_grad_kernel,
        out_shape=(
            pltpu.VMEM((most, middle), BF16),
            pltpu.VMEM((most, 640), BF16),
            pltpu.VMEM((most, 640), BF16),
        ),
        in_specs=[SM] + [VM] * 6 + [ANY],
        out_specs=(VM, VM, VM),
        compiler_params=params(6),
        cost_estimate=takes(2),
        name="mid_grad",
    )(meta, mid_act_grad, mid_pre, belong, mid_merged, gain_mid, mid_sums, after)
    other = swap(send, "sp", 1)
    row_scratch = [pick_scratch, plane_scratch, pltpu.SemaphoreType.DMA((5 * most // 128,))]
    gathered = pl.pallas_call(
        space_rows_kernel,
        out_shape=pltpu.VMEM((3 * most, 3 * width), BF16),
        in_specs=[SM, VM, HBM, VM, ANY],
        out_specs=VM,
        scratch_shapes=row_scratch,
        compiler_params=params(10),
        cost_estimate=takes(4),
        name="space_rows",
    )(meta, row_info, in_hbm(stored), outer_part, send)

    def space_grad_part(first_tap, taps, after):
        shapes = (
            jax.ShapeDtypeStruct((taps, 1152, 128), F32),
            jax.ShapeDtypeStruct((taps, 1152, 128), BF16),
        )
        if first_tap == 0:
            return pl.pallas_call(
                functools.partial(space_grad_first_kernel, first_tap),
                out_shape=shapes,
                in_specs=[SM, VM, VM, VM, ANY, ANY],
                out_specs=(VM, VM),
                scratch_shapes=[pltpu.VMEM((640, width), F32)],
                compiler_params=params(10),
                cost_estimate=takes(9),
                name="space_grad",
            )(meta, gathered, keep, other, *after)
        return pl.pallas_call(
            functools.partial(space_grad_kernel, first_tap),
            out_shape=shapes,
            in_specs=[SM, VM, HBM, VM, VM, VM, ANY, ANY],
            out_specs=(VM, VM),
            scratch_shapes=[
                pltpu.VMEM((3 * most, 3 * width), BF16),
                pltpu.VMEM((640, width), F32),
                *row_scratch,
            ],
            compiler_params=params(30),
            cost_estimate=takes(11),
            name="space_grad",
        )(meta, row_info, in_hbm(stored), outer_part, keep, other, *after)

    chunks = {"b": (0, 4), "c": (4, 5)}
    dense, edges, logits = {}, {}, {}
    left = {"t": 2 * steps - 1, "b": 2 * steps - 1, "c": 2 * steps - 1}
    space_grad = None
    token_shape = jax.ShapeDtypeStruct((8, 128), F32)
    last = {}
    after = send, send

    def step(name):
        left[name] -= 1
        token = chains[name].step(after)
        return token, token

    for event in PLAN:
        if event in "tbc":
            if left[event]:
                after = step(event)
        elif event in "BC":
            name = event.lower()
            keep_part, send_part = space_grad_part(*chunks[name], after)
            chains[name] = Chain("taps" + name, (keep_part, send_part), order, TURN)
            after = send_part, send_part
        elif event in "01":
            side = int(event)
            dense[side], edges[side], logits[side] = pl.pallas_call(
                functools.partial(input_back_kernel, side, frame_count),
                out_shape=(
                    jax.ShapeDtypeStruct((frame_count, cells, width), F32),
                    jax.ShapeDtypeStruct((frame_count, cells, width), BF16),
                    jax.ShapeDtypeStruct((clip_count, classes), F32),
                ),
                in_specs=[SM, VM, VM, HBM, VM, VM, VM, ANY, ANY],
                out_specs=(VM, VM, VM),
                scratch_shapes=[
                    pltpu.VMEM((6 * width, middle), BF16),
                    pltpu.VMEM((2, most // 2 + 256, 3 * width), BF16),
                    pltpu.VMEM((cells, 3 * cells), BF16),
                    pltpu.VMEM((most // 2 + 256, width), BF16),
                    pltpu.VMEM((most // 2 + 256, width), BF16),
                    pltpu.SemaphoreType.DMA(()),
                ],
                compiler_params=params(26),
                cost_estimate=takes(17),
                name="input_back",
            )(meta, col_info, mid_grad, weight, act_grad, pooled, class_lines, *after)
            if side == 0:
                scores = logits[0]
                for axis, bit in bits("sp"):
                    scores = scores + swap(scores, axis, bit)
                up = lax.ppermute(edges[0], "sp", [(i, i - 1) for i in range(1, sp_count)])
            else:
                down = lax.ppermute(edges[1], "sp", [(i, i + 1) for i in range(sp_count - 1)])
            after = edges[side], edges[side]
        elif event == "i":
            input_grad, token = pl.pallas_call(
                input_join_kernel,
                out_shape=(
                    jax.ShapeDtypeStruct((row_count, frame_count, clip_count, col_count, width), F32),
                    token_shape,
                ),
                in_specs=[SM, VM, VM, VM, VM, VM, ANY, ANY],
                out_specs=(VM, VM),
                scratch_shapes=[pltpu.VMEM((clip_count, 8, width), F32)],
                compiler_params=params(18),
                cost_estimate=takes(2),
                name="input_join",
            )(meta, col_info, dense[0], dense[1], down, up, after[0], scores)
            after = token, token
        elif event == "T":
            while left["t"]:
                after = step("t")
            own_half = chains["t"].state
            time_grad, class_weight_grad, token = pl.pallas_call(
                time_join_kernel,
                out_shape=(
                    jax.ShapeDtypeStruct((3 * middle, width), F32),
                    jax.ShapeDtypeStruct((classes, width), F32),
                    token_shape,
                ),
                in_specs=[SM, VM, VM, ANY, ANY],
                out_specs=(VM, VM, VM),
                compiler_params=params(16),
                cost_estimate=takes(5),
                name="time_join",
            )(meta, own_half, trade(own_half, small_order, 0), *after)
            after = token, token
        elif event in "pq":
            name = "b" if event == "p" else "c"
            while left[name]:
                after = step(name)
            own_half = chains[name].state
            got_half = trade(own_half, order, 0)
            relay = got_half
            if event == "q":
                relay = pl.pallas_call(
                    relay_kernel,
                    out_shape=jax.ShapeDtypeStruct(got_half.shape, BF16),
                    in_specs=[VM, ANY, ANY],
                    out_specs=VM,
                    compiler_params=params(4),
                    cost_estimate=takes(1),
                    name="relay",
                )(got_half, *after)
            last[name] = [own_half, got_half, swap(own_half, "sp", 1), swap(relay, "sp", 1)]
            after = after[0], got_half
        else:
            name = "b" if event == "P" else "c"
            first_tap, taps = chunks[name]
            piece = pl.BlockSpec((1, 1152, 128), lambda n, meta: (n, 0, 0))
            before = [] if space_grad is None else [space_grad]
            space_grad, token = pl.pallas_call(
                functools.partial(join_kernel, steps),
                grid_spec=pltpu.PrefetchScalarGridSpec(
                    num_scalar_prefetch=1,
                    grid=(taps,),
                    in_specs=[piece] * 4 + [ANY] * (2 + len(before)),
                    out_specs=(
                        pl.BlockSpec((1, width, middle), lambda n, meta, tap=first_tap: (n + tap, 0, 0)),
                        pl.BlockSpec((8, 128), lambda n, meta: (0, 0)),
                    ),
                ),
                out_shape=(jax.ShapeDtypeStruct((9, width, middle), F32), token_shape),
                input_output_aliases={7: 0} if before else {},
                compiler_params=params(12),
                cost_estimate=takes(6),
                name="join",
            )(meta, *last[name], *after, *before)
            after = token, token
    space_grad = space_grad.reshape(3, 3, width, middle)
    input_grad = input_grad.transpose(2, 1, 0, 3, 4)
    time_grad = time_grad.reshape(3, middle, width)
    class_weight_grad = class_weight_grad.T
    logits = scores + class_bias
    return (
        logits,
        input_grad,
        space_grad,
        time_grad,
        gain_mid_grad,
        shift_mid_grad,
        gain_out_grad,
        shift_out_grad,
        class_weight_grad,
        class_bias_grad,
    )


def solution(mesh):
    placed = (
        P("dp", None, "sp", None, None),
        P(),
        P(),
        P(),
        P(),
        P(),
        P(),
        P(),
        P(),
        P("dp"),
        P("dp"),
        P("dp"),
        P("dp", None),
    )
    return jax.shard_map(
        shards,
        mesh=mesh,
        in_specs=placed,
        out_specs=(
            P("dp", None),
            P("dp", None, "sp", None, None),
            P(),
            P(),
            P(),
            P(),
            P(),
            P(),
            P(),
            P(),
        ),
        check_vma=False,
    )
```

```python
import functools

import jax
import jax.numpy as jnp
from jax import lax
from jax.experimental import pallas as pl
from jax.experimental.pallas import tpu as pltpu
from jax.sharding import PartitionSpec as P

EPSILON = 1e-05
HIGH = lax.Precision.HIGHEST
F32 = jnp.float32
BF16 = jnp.bfloat16
S_AT, CORE_AT, ROW_AT, OFF, LEN, PAD, END_AT, FIRST_AT, TURN, SMALL_TURN = 0, 1, 2, 4, 8, 12, 16, 17, 18, 33
META = 48

PLAN = "Bt0btCbt1bctcbticbtcbctbccpTPqQ"

VM = pl.BlockSpec(memory_space=pltpu.VMEM)
SM = pl.BlockSpec(memory_space=pltpu.SMEM)
ANY = pl.BlockSpec(memory_space=pl.ANY)
HBM = pl.BlockSpec(memory_space=pltpu.HBM)


def in_hbm(value):
    return pltpu.with_memory_space_constraint(value, pltpu.HBM)


STEP = 6


def takes(us):
    return pl.CostEstimate(flops=us * 1_100_000_000, bytes_accessed=us * 3_300_000, transcendentals=0)


def params(mib):
    return pltpu.CompilerParams(vmem_limit_bytes=mib << 20)


def nt_dot(a, b):
    return lax.dot_general(a, b, (((1,), (1,)), ((), ())), preferred_element_type=F32)


def tn_dot(a, b):
    return lax.dot_general(a, b, (((0,), (0,)), ((), ())), preferred_element_type=F32)


def dot(a, b):
    return jnp.dot(a, b, preferred_element_type=F32)


def split(value):
    high = value.astype(BF16)
    return high, (value - high.astype(F32)).astype(BF16)


def sigmoid(v):
    return 1.0 / (1.0 + jnp.exp(-v))


def slope(v):
    s = sigmoid(v)
    return s * (1.0 + v * (1.0 - s))


def at16(index):
    return pl.multiple_of(index, 16)


def at64(index):
    return pl.multiple_of(index, 64)


def at128(index):
    return pl.multiple_of(index, 128)


def sweep(rows, size, body):
    count = lax.div(rows, size)

    def one(m, carry):
        body(pl.multiple_of(m * size, size), size)
        return carry

    lax.fori_loop(0, count, one, 0)

    @pl.when(rows > count * size)
    def _():
        body(pl.multiple_of(count * size, size), size // 2)


def pick_rows(row_info, shift):
    place, col, cols = row_info[0:1, :], row_info[1:2, :], row_info[2:3, :]
    home = col - shift
    ok = (col < cols) & (home >= 0) & (home < cols)
    spot = jnp.where(ok, place - shift, -1)
    size = row_info.shape[1]
    index = lax.broadcasted_iota(jnp.int32, (size, size), 0)
    return jnp.where(index == spot, 1.0, 0.0).astype(BF16)


def pick_cols(col_info, shift):
    place, col, cols = col_info[:, 0:1], col_info[:, 1:2], col_info[:, 2:3]
    home = col - shift
    ok = (col < cols) & (home >= 0) & (home < cols)
    spot = jnp.where(ok, place - shift, -1)
    size = col_info.shape[0]
    index = lax.broadcasted_iota(jnp.int32, (size, size), 1)
    return jnp.where(index == spot, 1.0, 0.0).astype(BF16)


def each_list(meta, base, frame_count, store):
    for t in range(frame_count):
        for half in range(2):

            @pl.when(half * 128 < meta[PAD + t])
            def _(t=t, half=half):
                store(t, half, at16(base + meta[OFF + t] + half * 128))


def setup_kernel(
    sp_count, orders, where, frames, rows, cols, values, meta, row_info, col_info, clip_info, own, own_low, ahead, pad
):
    row_count, frame_count, clip_count, col_count, width = values.shape
    size = clip_count * 8
    core = lax.rem(where[1], 2)
    first_row = where[1] * row_count
    total = jnp.int32(0)
    for t in range(frame_count):
        length = jnp.int32(0)
        for b in range(clip_count):
            length += jnp.where(frames[b] > t, cols[b], 0)
        padded = (length + 15) // 16 * 16
        meta[OFF + t], meta[LEN + t], meta[PAD + t] = total, length, padded
        total += padded
    meta[S_AT], meta[CORE_AT], meta[ROW_AT] = (total + 63) // 64 * 64, core, first_row
    meta[END_AT] = total
    meta[FIRST_AT] = jnp.where(where[1] == 0, 1, 0)
    place = where[0] * sp_count + where[1]
    for start, (order, other) in zip((TURN, SMALL_TURN), orders):
        for n, (zero, one) in enumerate(zip(*order)):
            meta[start + n] = jnp.where(place & jnp.where(core == 0, zero, one) != 0, 1, 0)
        meta[start + len(order[0])] = jnp.where(place & jnp.where(core == 0, other[0], other[1]) != 0, 1, 0)

    lane = lax.broadcasted_iota(jnp.int32, (1, size), 1)
    clip, col = lax.shift_right_logical(lane, 3), lane & 7
    zero = jnp.zeros((1, size), jnp.int32)
    of_cell, of_clip = [zero] * 3, [zero] * 3
    for b in range(clip_count):
        for n, source in enumerate((cols, frames, rows)):
            of_cell[n] = jnp.where(clip == b, source[b], of_cell[n])
            of_clip[n] = jnp.where(lane == b, source[b], of_clip[n])
    start = zero
    for b in range(clip_count):
        ahead_of = (frames[b] > of_cell[1]) | ((frames[b] == of_cell[1]) & (clip > b))
        start += jnp.where(ahead_of, cols[b], 0)
    info = [start + col, col, of_cell[0], of_cell[1], of_cell[2], zero, zero, zero]
    for n, line in enumerate(info[:3] + of_clip[1:] + [zero] * 3):
        row_info[n : n + 1, :] = line
    col_info[...] = jnp.concatenate(info, axis=0).astype(F32).T.astype(jnp.int32)
    per_clip = jnp.maximum(of_clip[0] * of_clip[1] * of_clip[2], 1).astype(F32)[:, 0:128]
    clip_info[...] = jnp.concatenate([per_clip] * 8, axis=0).T

    pad[:, col_count:, :] = jnp.zeros((clip_count, 8 - col_count, width), F32)
    cells = col_info[...]
    for h in range(row_count):
        for t in range(frame_count):
            pad[:, 0:col_count, :] = values[h, t]
            inside = (cells[:, 1:2] < cells[:, 2:3]) & (cells[:, 3:4] > t) & (cells[:, 4:5] > first_row + h)
            masked = pad[...].reshape(size, width) * jnp.where(inside, 1.0, 0.0)
            own[h, t], own_low[h, t] = split(masked)

            @pl.when(core == h)
            def _(t=t, masked=masked):
                ahead[t] = masked.astype(BF16)


def gather_setup(row_info, pick):
    info = row_info[...]
    for j in range(3):
        hot = pick_rows(info, j - 1)
        for half in range(2):
            pick[half, j * 128 : (j + 1) * 128, :] = hot[half * 128 : (half + 1) * 128, :]


def gather_plane(meta, pick, source, packed, base, frame_count):
    def store(t, half, row):
        got = dot(pick[half], source(t)).astype(BF16)
        for j in range(3):
            packed[pl.ds(row, 128), j * 512 : (j + 1) * 512] = got[j * 128 : (j + 1) * 128, :]

    each_list(meta, base, frame_count, store)
    packed[pl.ds(at16(base + meta[END_AT]), 128), :] = jnp.zeros((128, 1536), BF16)


def copy_out(rows, source, begin, target, start, sems, action):
    def one(m, carry):
        copy = pltpu.make_async_copy(
            source.at[pl.ds(at64(begin + m * 64), 64)], target.at[pl.ds(at64(start + m * 64), 64)], sems.at[m]
        )
        if action == "start":
            copy.start()
        else:
            copy.wait()
        return carry

    lax.fori_loop(0, lax.div(rows, 64), one, 0)


def space_kernel(
    meta, row_info, own, own_low, weight_in, logit_grad, class_weight, clip_info,
    mid_pre, belong, residual, stored, pooled_grad, bias_grad, packed, pick, weight, sems, load,
):
    frame_count = own.shape[1]
    core = meta[CORE_AT]
    s = meta[S_AT]
    fetch = pltpu.make_async_copy(weight_in, weight, load)
    fetch.start()
    gather_setup(row_info, pick)

    for h in range(2):
        gather_plane(meta, pick, lambda t, h=h: own[h, t], packed, h * s, frame_count)
    copy_out(2 * s, packed, 0, stored, (1 + 2 * core) * s, sems, "start")
    size = row_info.shape[1]
    clip_of = lax.broadcasted_iota(jnp.int32, (size, 128), 0) // 8
    lane = lax.broadcasted_iota(jnp.int32, (size, 128), 1)
    frames_of = jnp.broadcast_to(row_info[3:4, 0:128], (size, 128))
    rows_of = jnp.broadcast_to(row_info[4:5, 0:128], (size, 128))
    for h in range(2):

        def store(t, half, row, h=h):
            hot = pick[half, 128:256, :]
            inside = (clip_of == lane) & (frames_of > t) & (rows_of > meta[ROW_AT] + h)
            belong[pl.ds(row, 128), :] = dot(hot, jnp.where(inside, 1.0, 0.0).astype(BF16)).astype(BF16)
            residual[pl.ds(row, 128), :] = dot(hot, own[h, t]) + dot(hot, own_low[h, t])

        each_list(meta, h * s, frame_count, store)
        belong[pl.ds(at16(h * s + meta[END_AT]), 128), :] = jnp.zeros((128, 128), BF16)
        residual[pl.ds(at16(h * s + meta[END_AT]), 128), :] = jnp.zeros((128, 512), F32)
    clips, classes = logit_grad.shape
    pooled_grad[...] = jnp.zeros(pooled_grad.shape, F32)
    pooled_grad[0:clips, :] = (
        jnp.dot(logit_grad[...], class_weight[...], precision=HIGH, preferred_element_type=F32)
        / clip_info[0:clips, 0:1]
    )
    bias_grad[...] = jnp.zeros(bias_grad.shape, F32)
    bias_grad[:, 0:classes] = jnp.sum(logit_grad[...], axis=0, keepdims=True) * meta[FIRST_AT].astype(F32)
    fetch.wait()
    for h in range(2):

        def conv(row, size, h=h):
            rows = pl.ds(at64(h * s + row), size)

            acc = None
            for plane in range(2):
                i = plane - h + 1
                term = dot(packed[pl.ds(at64(plane * s + row), size), :], weight[i * 1536 : (i + 1) * 1536, :])
                acc = term if acc is None else acc + term
            mid_pre[rows, :] = acc

        sweep(s, 128, conv)
    copy_out(2 * s, packed, 0, stored, (1 + 2 * core) * s, sems, "wait")


def mask_of(belong, row, size):
    return jnp.sum(belong[pl.ds(row, size), :].astype(F32), axis=1, keepdims=True)


def norm_of(merged):
    count = merged[0:1, :]
    return merged[1:2, :] / count, lax.rsqrt(merged[2:3, :] / count + EPSILON)


def norm_sums(meta, values, belong, stats):
    mask = mask_of(belong, 0, 128)
    pivot = jnp.sum(values[0:128, :] * mask, axis=0, keepdims=True) / jnp.maximum(jnp.sum(mask), 1.0)
    stats[...] = jnp.zeros(stats.shape, F32)

    def sums(row, size):
        mask = mask_of(belong, row, size)
        off = (values[pl.ds(row, size), :] - pivot) * mask
        stats[0:1, :] += jnp.sum(mask, axis=0, keepdims=True)
        stats[1:2, :] += jnp.sum(off, axis=0, keepdims=True)
        stats[2:3, :] += jnp.sum(off * off, axis=0, keepdims=True)

    sweep(2 * meta[S_AT], 256, sums)
    count, total = stats[0:1, :], stats[1:2, :]
    stats[2:3, :] = jnp.maximum(stats[2:3, :] - total * total / count, 0.0)
    stats[1:2, :] = total + count * pivot


def space_edge_kernel(
    meta, row_info, mid_in, stored_in, part, outer, weight_in, belong, mid_pre, stored, stats,
    pick, planes, weight, sems, load,
):
    core = meta[CORE_AT]
    s = meta[S_AT]
    frame_count = outer.shape[0]
    fetches = [
        pltpu.make_async_copy(weight_in.at[pl.ds(n * 3072, 1536)], weight.at[pl.ds(n * 1536, 1536)], load.at[n])
        for n in range(2)
    ]
    for fetch in fetches:
        fetch.start()
    gather_setup(row_info, pick)
    gather_plane(meta, pick, lambda t: part[core, t], planes.at[0], 0, frame_count)
    gather_plane(meta, pick, lambda t: outer[t], planes.at[1], 0, frame_count)
    near, far = (3 - core) * s, 5 * core * s
    copy_out(s, planes.at[0], 0, stored, near, sems.at[0], "start")
    copy_out(s, planes.at[1], 0, stored, far, sems.at[1], "start")
    for fetch in fetches:
        fetch.wait()

    def conv(row, size):
        for n, row_of, lines in ((0, 1 - core, 1 - core), (1, core, core)):
            block = pl.ds(at64(row_of * s + row), size)
            taps = weight[pl.ds(pl.multiple_of(lines * 1536, 512), 1536), :]
            mid_pre[block, :] += dot(planes[n, pl.ds(row, size), :], taps)

    sweep(s, 128, conv)
    norm_sums(meta, mid_pre, belong, stats)
    copy_out(s, planes.at[0], 0, stored, near, sems.at[0], "wait")
    copy_out(s, planes.at[1], 0, stored, far, sems.at[1], "wait")


def shift_lists(meta, frame_count, source, target, width, move):
    s = meta[S_AT]
    for h in range(2):

        def store(t, half, row, h=h):
            other = t + move
            if 0 <= other < frame_count:
                block = source(at16(h * s + meta[OFF + other] + half * 128))
                place = half * 128 + lax.broadcasted_iota(jnp.int32, (128, 1), 0)
                keep = jnp.where(place < meta[LEN + other], 1.0, 0.0).astype(BF16)
                target(row, block * keep)
            else:
                target(row, jnp.zeros((128, width), BF16))

        each_list(meta, h * s, frame_count, store)
        target(at16(h * s + meta[END_AT]), jnp.zeros((128, width), BF16))


def time_kernel(
    frame_count, meta, mid_pre, belong, merged, gain, shift, weight, after, mid_low, out_pre, stats, wide
):
    rows = 2 * meta[S_AT]
    center, scale = norm_of(merged)

    def act(row, size):
        block = pl.ds(row, size)
        value = gain[...] * ((mid_pre[block, :] - center) * scale) + shift[...]
        low = (value * sigmoid(value) * mask_of(belong, row, size)).astype(BF16)
        wide[block, 1152:2304] = low
        mid_low[block, :] = low

    sweep(rows, 256, act)
    wide[pl.ds(at128(rows), 256), :] = jnp.zeros((256, 3456), BF16)
    for k in (0, 2):

        def source(row):
            return wide[pl.ds(row, 128), 1152:2304]

        def target(row, value, k=k):
            wide[pl.ds(row, 128), k * 1152 : (k + 1) * 1152] = value

        shift_lists(meta, frame_count, source, target, 1152, k - 1)

    def conv(row, size):
        out_pre[pl.ds(row, size), :] = dot(wide[pl.ds(row, size), :], weight[...])

    sweep(rows, 256, conv)
    norm_sums(meta, out_pre, belong, stats)


def act_kernel(
    meta, out_pre, belong, residual, merged, gain_ref, shift_ref, pooled_grad, bias_grad, clip_info,
    act_grad, stats, pooled,
):
    center, scale = norm_of(merged)
    high, rest = split(pooled_grad[...])
    pooled[...] = jnp.zeros(pooled.shape, F32)
    stats[...] = jnp.zeros(stats.shape, F32)

    def step(row, size):
        block = pl.ds(row, size)
        hot = belong[block, :]
        normed = (out_pre[block, :] - center) * scale
        value = gain_ref[...] * normed + shift_ref[...] + residual[block, :]
        s = sigmoid(value)
        first, second = split(value * s)
        pooled[...] += tn_dot(hot, first) + tn_dot(hot, second)
        grad = (dot(hot, high) + dot(hot, rest)) * (s * (1.0 + value * (1.0 - s)))
        act_grad[block, :] = grad
        stats[0:1, :] += jnp.sum(grad, axis=0, keepdims=True)
        stats[1:2, :] += jnp.sum(grad * normed, axis=0, keepdims=True)

    sweep(2 * meta[S_AT], 256, step)
    stats[2:3, :] = bias_grad[...]
    pooled[...] = pooled[...] / clip_info[:, 0:1]


def back_kernel(
    frame_count, meta, act_grad, out_pre, belong, out_merged, out_gain, out_sums, weight, mid_pre, mid_merged,
    mid_gain, mid_shift, wide, mid_act_grad, stats,
):
    rows = 2 * meta[S_AT]
    out_center, out_scale = norm_of(out_merged)
    mid_center, mid_scale = norm_of(mid_merged)
    out_shift_part = out_sums[0:1, :] / out_merged[0:1, :]
    out_gain_part = out_sums[1:2, :] / out_merged[0:1, :]
    stats[...] = jnp.zeros(stats.shape, F32)

    def grad(row, size):
        block = pl.ds(row, size)
        normed = (out_pre[block, :] - out_center) * out_scale
        inner = act_grad[block, :] - mask_of(belong, row, size) * (out_shift_part + normed * out_gain_part)
        wide[block, 512:1024] = (out_gain[...] * out_scale * inner).astype(BF16)

    sweep(rows, 256, grad)
    wide[pl.ds(at128(rows), 256), :] = jnp.zeros((256, 1536), BF16)
    for k in (0, 2):

        def source(row):
            return wide[pl.ds(row, 128), 512:1024]

        def target(row, value, k=k):
            wide[pl.ds(row, 128), k * 512 : (k + 1) * 512] = value

        shift_lists(meta, frame_count, source, target, 512, 1 - k)

    def conv(row, size):
        block = pl.ds(row, size)
        acc = nt_dot(wide[block, 0:512], weight[0])
        acc += nt_dot(wide[block, 512:1024], weight[1])
        acc += nt_dot(wide[block, 1024:1536], weight[2])
        normed = (mid_pre[block, :] - mid_center) * mid_scale
        acc = acc * mask_of(belong, row, size) * slope(mid_gain[...] * normed + mid_shift[...])
        mid_act_grad[block, :] = acc
        stats[0:1, :] += jnp.sum(acc, axis=0, keepdims=True)
        stats[1:2, :] += jnp.sum(acc * normed, axis=0, keepdims=True)

    sweep(rows, 256, conv)


def typical_act(gain, shift):
    spread = 3.0**0.5 * gain
    value = 0.0
    for share, at in ((1.0, shift - spread), (4.0, shift), (1.0, shift + spread)):
        value += share / 6.0 * at * sigmoid(at)
    return jnp.concatenate([value] * 8, axis=0).T[:, 0:1]


def time_grad_kernel(
    meta, mid_low, wide, belong, gain, shift, pooled, logit_grad, stats, keep, send, passed, total, by_clip
):
    rows = 2 * meta[S_AT]
    by_clip[...] = jnp.zeros(by_clip.shape, F32)

    def sums(row, size):
        by_clip[...] += tn_dot(belong[pl.ds(row, size), :], wide[pl.ds(row, size), :])

    sweep(rows, 256, sums)
    grad_sums = jnp.sum(by_clip[...], axis=0, keepdims=True)
    passed[0:2, :] = stats[...]
    passed[2:3, :] = grad_sums[:, 0:1152]
    passed[3:4, :] = jnp.zeros((1, 1152), F32)
    passed[3:4, 0:384] = grad_sums[:, 1152:1536]
    typical = typical_act(gain[...], shift[...])
    core = meta[CORE_AT]
    middle = mid_low.shape[1]
    classes = logit_grad.shape[1]
    half = keep.shape[1]
    for k in range(3):
        lines = slice(k * middle, (k + 1) * middle)
        total[lines, :] = -typical * grad_sums[:, k * 512 : (k + 1) * 512]

        def step(row, size, k=k, lines=lines):
            block = pl.ds(row, size)
            total[lines, :] += tn_dot(mid_low[block, :], wide[block, k * 512 : (k + 1) * 512])

        sweep(rows, 256, step)
    total[3 * middle : 3 * middle + classes, :] = lax.dot_general(
        logit_grad[...], pooled[0 : logit_grad.shape[0], :], (((0,), (0,)), ((), ())), precision=HIGH, preferred_element_type=F32
    )
    total[3 * middle + classes :, :] = jnp.zeros((2 * half - 3 * middle - classes, 512), F32)
    for lane in range(4):
        lanes = slice(lane * 128, (lane + 1) * 128)
        keep[lane] = total[pl.ds(at128(core * half), half), lanes]
        send[lane] = total[pl.ds(at128((1 - core) * half), half), lanes].astype(BF16)


def relay_kernel(got, *rest):
    rest[-1][...] = got[...]


def time_join_kernel(meta, own, got, gain, shift, sums, after, also, time_grad, class_grad, token):
    token[...] = jnp.zeros(token.shape, F32)
    half = own.shape[1]
    rest = time_grad.shape[0] - half

    def place(first, second):
        for lane in range(4):
            lanes = slice(lane * 128, (lane + 1) * 128)
            time_grad[0:half, lanes] = first[lane].astype(F32)
            time_grad[half:, lanes] = second[lane, 0:rest, :].astype(F32)
            class_grad[:, lanes] = second[lane, rest : rest + class_grad.shape[0], :].astype(F32)

    @pl.when(meta[CORE_AT] == 0)
    def _():
        place(own, got)

    @pl.when(meta[CORE_AT] != 0)
    def _():
        place(got, own)

    typical = typical_act(gain[...], shift[...])
    middle = gain.shape[1]
    grad_sums = jnp.concatenate([sums[2:3, :], sums[3:4, 0:384]], axis=1)
    for k in range(3):
        time_grad[k * middle : (k + 1) * middle, :] += typical * grad_sums[:, k * 512 : (k + 1) * 512]


def mid_grad_kernel(meta, mid_act_grad, mid_pre, belong, merged, gain, sums, after, whole, keep, send):
    core = meta[CORE_AT]
    center, scale = norm_of(merged)
    shift_part = sums[0:1, :] / merged[0:1, :]
    gain_part = sums[1:2, :] / merged[0:1, :]

    def step(row, size):
        block = pl.ds(row, size)
        normed = (mid_pre[block, :] - center) * scale
        inner = mid_act_grad[block, :] - mask_of(belong, row, size) * (shift_part + normed * gain_part)
        low = (gain[...] * scale * inner).astype(BF16)
        whole[block, :] = low

        @pl.when(core == 0)
        def _():
            keep[block, 0:512] = low[:, 0:512]
            send[block, 0:512] = low[:, 512:1024]

        @pl.when(core != 0)
        def _():
            keep[block, 0:512] = low[:, 512:1024]
            send[block, 0:512] = low[:, 0:512]

        keep[block, 512:640] = low[:, 1024:1152]
        send[block, 512:640] = low[:, 1024:1152]

    sweep(2 * meta[S_AT], 256, step)


def space_grad_taps(first_tap, meta, packed, own, part, keep, send, total):
    core = meta[CORE_AT]
    s = meta[S_AT]
    mine = meta[TURN]

    def one(tap, carry):
        i, j = lax.div(first_tap + tap, 3), lax.rem(first_tap + tap, 3)
        lanes = pl.ds(at128(j * 512), 512)

        total[...] = jnp.zeros(total.shape, F32)

        def step(row, size):
            first = packed[pl.ds(at64((2 * core + i) * s + row), size), lanes]
            second = packed[pl.ds(at64((2 - 2 * core + i) * s + row), size), lanes]
            total[...] += tn_dot(own[pl.ds(row, size), :], first) + tn_dot(part[pl.ds(row, size), :], second)

        sweep(2 * s, 256, step)
        for half, out, kind in ((mine, keep, F32), (1 - mine, send, BF16)):
            lane = half * 256
            out[tap, 0:512, :] = total[0:512, pl.ds(at128(lane), 128)].astype(kind)
            out[tap, 512:1024, :] = total[0:512, pl.ds(at128(lane + 128), 128)].astype(kind)
            out[tap, 1024:1152, :] = total[512:640, pl.ds(at128(core * 256 + half * 128), 128)].astype(kind)
        return carry

    lax.fori_loop(0, keep.shape[0], one, 0)


def space_rows(meta, row_info, stored, part, outer, packed, pick, plane, sems):
    core = meta[CORE_AT]
    s = meta[S_AT]
    copy_out(4 * s, stored, 2 * core * s, packed, 2 * core * s, sems, "start")
    gather_setup(row_info, pick)
    for source, place in ((lambda t: part[1 - core, t], 4 - 3 * core), (lambda t: outer[t], 5 - 5 * core)):
        gather_plane(meta, pick, source, plane, 0, outer.shape[0])

        def put(row, size, place=place):
            packed[pl.ds(at64(place * s + row), size), :] = plane[pl.ds(row, size), :]

        sweep(s, 128, put)
    copy_out(4 * s, stored, 2 * core * s, packed, 2 * core * s, sems, "wait")


def space_rows_kernel(meta, row_info, stored, part, outer, after, packed, pick, plane, sems):
    space_rows(meta, row_info, stored, part, outer, packed, pick, plane, sems)


def space_grad_kernel(
    first_tap, meta, row_info, stored, near, outer, own, part, after, also, keep, send, packed, total, pick, plane, sems
):
    space_rows(meta, row_info, stored, near, outer, packed, pick, plane, sems)
    space_grad_taps(first_tap, meta, packed, own, part, keep, send, total)


def space_grad_first_kernel(first_tap, meta, packed, own, part, after, also, keep, send, total):
    space_grad_taps(first_tap, meta, packed, own, part, keep, send, total)


def halve_kernel(at, meta, keep, got, after, also, next_keep, next_send):
    half = next_keep.shape[1]
    mine = meta[at]

    def one(tap, carry):
        low, high = pl.ds(at16(mine * half), half), pl.ds(at16((1 - mine) * half), half)
        next_keep[tap] = keep[tap, low, :] + got[tap, low, :].astype(F32)
        next_send[tap] = (keep[tap, high, :] + got[tap, high, :].astype(F32)).astype(BF16)
        return carry

    lax.fori_loop(0, keep.shape[0], one, 0)


def halve_pass_kernel(at, meta, keep, got, value, next_keep, next_send, passed):
    passed[...] = value[...]
    halve_kernel(at, meta, keep, got, None, None, next_keep, next_send)


def share_kernel(keep, got, after, also, out):
    def one(tap, carry):
        out[tap] = (keep[tap] + got[tap].astype(F32)).astype(BF16)
        return carry

    lax.fori_loop(0, keep.shape[0], one, 0)


def double_kernel(at, meta, own, got, after, also, out):
    half = own.shape[1]
    mine = meta[at]

    def one(tap, carry):
        out[tap, pl.ds(at16(mine * half), half), :] = own[tap]
        out[tap, pl.ds(at16((1 - mine) * half), half), :] = got[tap]
        return carry

    lax.fori_loop(0, own.shape[0], one, 0)


def input_back_kernel(
    side, frame_count, meta, col_info, grad, weight_in, act_grad, pooled, class_weight, after, also,
    dense, edge, logits, weight, wide, spread, high, rest, load,
):
    s = meta[S_AT]
    fetch = pltpu.make_async_copy(weight_in.at[pl.ds(side * 1536, 3072)], weight, load)
    fetch.start()
    if side == 0:
        logits[...] = lax.dot_general(
            pooled[0 : logits.shape[0], :],
            class_weight[...],
            (((1,), (1,)), ((), ())),
            precision=HIGH,
            preferred_element_type=F32,
        )
    else:
        logits[...] = jnp.zeros(logits.shape, F32)
    info = col_info[...]
    for j in range(3):
        spread[:, j * 256 : (j + 1) * 256] = pick_cols(info, j - 1)

    def cut(row, size):
        first, second = split(act_grad[pl.ds(at64(side * s + row), size), :])
        high[pl.ds(row, size), :] = first
        rest[pl.ds(row, size), :] = second

    sweep(s, 128, cut)
    for part in (high, rest):
        part[pl.ds(at64(s), 256), :] = jnp.zeros((256, 512), BF16)
    for plane in range(2):
        wide[plane, pl.ds(at64(s), 256), :] = jnp.zeros((256, 1536), BF16)
    fetch.wait()
    outer_weight, inner_weight = weight[0:1536, :], weight[1536:3072, :]
    if side:
        outer_weight, inner_weight = inner_weight, outer_weight

    def conv(row, size):
        near, far = grad[pl.ds(at64(side * s + row), size), :], grad[pl.ds(at64((1 - side) * s + row), size), :]
        both = nt_dot(jnp.concatenate([near, far], axis=0), outer_weight)
        wide[0, pl.ds(row, size), :] = both[0:size, :].astype(BF16)
        wide[1, pl.ds(row, size), :] = (both[size:, :] + nt_dot(near, inner_weight)).astype(BF16)

    sweep(s, 128, conv)
    for t in range(frame_count):

        def scatter(size, t=t):
            rows = pl.ds(at16(meta[OFF + t]), size)
            edge_acc = inner = None
            for j in range(3):
                hot = spread[:, j * 256 : j * 256 + size]
                first = dot(hot, wide[0, rows, j * 512 : (j + 1) * 512])
                second = dot(hot, wide[1, rows, j * 512 : (j + 1) * 512])
                edge_acc = first if j == 0 else edge_acc + first
                inner = second if j == 0 else inner + second
            hot = spread[:, 256 : 256 + size]
            edge[t] = edge_acc.astype(BF16)
            dense[t] = inner + dot(hot, high[rows, :]) + dot(hot, rest[rows, :])

        @pl.when(meta[LEN + t] > 128)
        def _(scatter=scatter):
            scatter(256)

        @pl.when(meta[LEN + t] <= 128)
        def _(scatter=scatter):
            scatter(128)


def input_join_kernel(meta, col_info, first, second, down, up, after, also, out, token, pad):
    frame_count, clip_count, col_count, width = out.shape[1:]
    token[...] = jnp.zeros(token.shape, F32)
    cells = col_info[...]
    for h, (own, got) in enumerate(((first, down), (second, up))):
        for t in range(frame_count):
            inside = (cells[:, 1:2] < cells[:, 2:3]) & (cells[:, 3:4] > t) & (cells[:, 4:5] > meta[ROW_AT] + h)
            value = jnp.where(inside, own[t] + got[t].astype(F32), 0.0)
            pad[...] = value.reshape(clip_count, 8, width)
            out[h, t] = pad[:, 0:col_count, :]


def join_kernel(steps, meta, own, got, part_own, part_got, after, also, *rest):
    out, token = rest[-2:]
    token[...] = jnp.zeros(token.shape, F32)
    core = meta[CORE_AT]
    mine, other = meta[TURN], meta[TURN + steps]
    for piece, half, owner in (
        (own, mine, core),
        (got, 1 - mine, core),
        (part_own, other, 1 - core),
        (part_got, 1 - other, 1 - core),
    ):
        row = half * 256
        middles = pl.ds(at128(owner * 512), 512)
        out[0, pl.ds(at128(row), 128), middles] = piece[0, 0:512, :].astype(F32).T
        out[0, pl.ds(at128(row + 128), 128), middles] = piece[0, 512:1024, :].astype(F32).T
        out[0, pl.ds(at128(owner * 256 + half * 128), 128), 1024:1152] = piece[0, 1024:1152, :].astype(F32).T


def swap(value, axis, bit):
    size = lax.axis_size(axis)
    if size <= bit:
        return None
    return lax.ppermute(value, axis, [(i, i ^ bit) for i in range(size)])


def bits(axis):
    return [(axis, 1 << n) for n in range((lax.axis_size(axis) - 1).bit_length())]


def sum_all(value, axes):
    for axis, bit in axes:
        value = value + swap(value, axis, bit)
    return value


def merge_all(stats):
    stats = stats[:3]
    row = lax.broadcasted_iota(jnp.int32, stats.shape, 0)
    for axis, bit in bits("sp") + bits("dp"):
        other = swap(stats, axis, bit)
        gap = stats[1] / stats[0] - other[1] / other[0]
        extra = gap * gap * (stats[0] * other[0] / (stats[0] + other[0]))
        stats = stats + other + jnp.where(row == 2, extra[None], 0.0)
    return stats


def trade(value, order, stage):
    size = lax.axis_size(("dp", "sp"))
    return lax.ppermute(value, ("dp", "sp"), [(i, i ^ order[i % 2][stage]) for i in range(size)])


def halve_step(keep, send, order, meta, at, stage, after, name):
    got = trade(send, order, stage)
    n, rows, lanes = keep.shape
    if stage + 1 == len(order[0]):
        share = pl.pallas_call(
            share_kernel,
            out_shape=jax.ShapeDtypeStruct(keep.shape, BF16),
            in_specs=[VM, VM, ANY, ANY],
            out_specs=VM,
            compiler_params=params(6),
            cost_estimate=takes(STEP),
            name=name + "_share",
        )(keep, got, *after)
        return share, None
    half = rows // 2
    if half % 16:
        pairs = (keep + got.astype(F32)).reshape(n, 2, half, lanes)
        mine = meta[at + stage + 1]
        keep = lax.dynamic_index_in_dim(pairs, mine, 1, keepdims=False)
        send = lax.dynamic_index_in_dim(pairs, 1 - mine, 1, keepdims=False).astype(BF16)
        return keep, send
    return pl.pallas_call(
        functools.partial(halve_kernel, at + stage + 1),
        out_shape=(
            jax.ShapeDtypeStruct((n, half, lanes), F32),
            jax.ShapeDtypeStruct((n, half, lanes), BF16),
        ),
        in_specs=[SM, VM, VM, ANY, ANY],
        out_specs=(VM, VM),
        compiler_params=params(10),
        cost_estimate=takes(STEP),
        name=name + "_halve%d" % stage,
    )(meta, keep, got, *after)


def double_step(own, order, meta, at, stage, after, name):
    got = trade(own, order, stage)
    n, rows, lanes = own.shape
    if rows % 16:
        mine = meta[at + stage]
        return jnp.concatenate([jnp.where(mine == 0, own, got), jnp.where(mine == 0, got, own)], axis=1)
    return pl.pallas_call(
        functools.partial(double_kernel, at + stage),
        out_shape=jax.ShapeDtypeStruct((n, 2 * rows, lanes), BF16),
        in_specs=[SM, VM, VM, ANY, ANY],
        out_specs=VM,
        compiler_params=params(8),
        cost_estimate=takes(STEP),
        name=name + "_double%d" % stage,
    )(meta, own, got, *after)


def shards(
    clip_input,
    space_weight,
    time_weight,
    gain_mid,
    shift_mid,
    gain_out,
    shift_out,
    class_weight,
    class_bias,
    frames,
    rows,
    cols,
    logit_grad,
):
    clip_count, frame_count, row_count, col_count, width = clip_input.shape
    middle = space_weight.shape[-1]
    classes = class_weight.shape[1]
    cells = clip_count * 8
    most = row_count * frame_count * clip_count * col_count
    sp_count = lax.axis_size("sp")
    x = [bit for _, bit in bits("sp")[1:]]
    y, z = [[bit * sp_count for _, bit in part] for part in (bits("dp")[:1], bits("dp")[1:])]
    order = x + y + z, y + x + z
    small_order = [1] + order[0], [1] + order[1]
    steps = len(order[0])
    orders = (order, (order[1][0], order[0][0])), (small_order, (1, 1))
    place = jnp.stack([lax.axis_index("dp"), lax.axis_index("sp")]).astype(jnp.int32)
    cells_shape = (row_count, frame_count, cells, width)
    meta, row_info, col_info, clip_info, own, own_low, ahead = pl.pallas_call(
        functools.partial(setup_kernel, sp_count, orders),
        out_shape=(
            jax.ShapeDtypeStruct((META,), jnp.int32),
            jax.ShapeDtypeStruct((8, cells), jnp.int32),
            jax.ShapeDtypeStruct((cells, 8), jnp.int32),
            jax.ShapeDtypeStruct((128, 8), F32),
            jax.ShapeDtypeStruct(cells_shape, BF16),
            jax.ShapeDtypeStruct(cells_shape, BF16),
            jax.ShapeDtypeStruct(cells_shape[1:], BF16),
        ),
        in_specs=[SM, SM, SM, SM, VM],
        out_specs=(SM, VM, VM, VM, VM, VM, VM),
        scratch_shapes=[pltpu.VMEM((clip_count, 8, width), F32)],
        compiler_params=params(20),
        cost_estimate=takes(3),
        name="setup",
    )(place, frames, rows, cols, clip_input.transpose(2, 1, 0, 3, 4))
    class_lines = class_weight.T

    part = swap(own, "sp", 1)
    across = [(i, i + 1 if i % 2 else i - 1) for i in range(sp_count)]
    outer = lax.ppermute(ahead, "sp", [(i, j) for i, j in across if 0 <= j < sp_count])
    outer_part = swap(outer, "sp", 1)

    weight = in_hbm(space_weight.reshape(9 * width, middle))
    stored_shape = pltpu.HBM((3 * most, 3 * width), BF16)
    pick_scratch = pltpu.VMEM((2, 384, cells), BF16)
    plane_scratch = pltpu.VMEM((most // 2 + 256, 3 * width), BF16)
    mid_pre, belong, residual, stored, pooled_grad, bias_grad = pl.pallas_call(
        space_kernel,
        out_shape=(
            pltpu.VMEM((most, middle), F32),
            pltpu.VMEM((most + 256, 128), BF16),
            pltpu.VMEM((most + 256, width), F32),
            stored_shape,
            pltpu.VMEM((128, width), F32),
            pltpu.VMEM((1, width), F32),
        ),
        in_specs=[SM, VM, VM, VM, HBM, VM, VM, VM],
        out_specs=(VM, VM, VM, HBM, VM, VM),
        scratch_shapes=[
            pltpu.VMEM((most + 256, 3 * width), BF16),
            pick_scratch,
            pltpu.VMEM((9 * width, middle), BF16),
            pltpu.SemaphoreType.DMA((most // 64,)),
            pltpu.SemaphoreType.DMA(()),
        ],
        compiler_params=params(24),
        cost_estimate=takes(14),
        name="space_conv",
    )(meta, row_info, own, own_low, weight, logit_grad, class_lines, clip_info)
    mid_pre, stored, stats = pl.pallas_call(
        space_edge_kernel,
        out_shape=(
            pltpu.VMEM((most, middle), F32),
            stored_shape,
            jax.ShapeDtypeStruct((3, middle), F32),
        ),
        in_specs=[SM, VM, VM, HBM, VM, VM, HBM, VM],
        out_specs=(VM, HBM, VM),
        scratch_shapes=[
            pick_scratch,
            pltpu.VMEM((2, most // 2 + 256, 3 * width), BF16),
            pltpu.VMEM((6 * width, middle), BF16),
            pltpu.SemaphoreType.DMA((2, most // 128)),
            pltpu.SemaphoreType.DMA((2,)),
        ],
        input_output_aliases={2: 0, 3: 1},
        compiler_params=params(21),
        cost_estimate=takes(9),
        name="space_edge",
    )(meta, row_info, mid_pre, in_hbm(stored), part, outer, weight, belong)
    gain_mid, shift_mid = gain_mid[None], shift_mid[None]
    gain_out, shift_out = gain_out[None], shift_out[None]
    mid_merged = merge_all(stats)
    mid_low, out_pre, stats = pl.pallas_call(
        functools.partial(time_kernel, frame_count),
        out_shape=(
            pltpu.VMEM((most, middle), BF16),
            pltpu.VMEM((most, width), F32),
            jax.ShapeDtypeStruct((3, width), F32),
        ),
        in_specs=[SM, VM, VM, VM, VM, VM, VM, ANY],
        out_specs=(VM, VM, VM),
        scratch_shapes=[pltpu.VMEM((most + 256, 3 * middle), BF16)],
        compiler_params=params(19),
        cost_estimate=takes(8),
        name="time_conv",
    )(meta, mid_pre, belong, mid_merged, gain_mid, shift_mid, time_weight.reshape(3 * middle, width), outer_part)

    out_merged = merge_all(stats)
    act_grad, stats, pooled = pl.pallas_call(
        act_kernel,
        out_shape=(
            pltpu.VMEM((most, width), F32),
            jax.ShapeDtypeStruct((3, width), F32),
            jax.ShapeDtypeStruct((128, width), F32),
        ),
        in_specs=[SM] + [VM] * 9,
        out_specs=(VM, VM, VM),
        compiler_params=params(4),
        cost_estimate=takes(3),
        name="act",
    )(meta, out_pre, belong, residual, out_merged, gain_out, shift_out, pooled_grad, bias_grad, clip_info)

    out_sums = sum_all(stats, bits("sp") + bits("dp"))
    shift_out_grad, gain_out_grad, class_bias_grad = out_sums[0], out_sums[1], out_sums[2, :classes]
    wide, mid_act_grad, stats = pl.pallas_call(
        functools.partial(back_kernel, frame_count),
        out_shape=(
            pltpu.VMEM((most + 256, 3 * width), BF16),
            pltpu.VMEM((most, middle), F32),
            jax.ShapeDtypeStruct((2, middle), F32),
        ),
        in_specs=[SM] + [VM] * 11,
        out_specs=(VM, VM, VM),
        compiler_params=params(7),
        cost_estimate=takes(6),
        name="time_back",
    )(
        meta, act_grad, out_pre, belong, out_merged, gain_out, out_sums, time_weight, mid_pre, mid_merged,
        gain_mid, shift_mid,
    )

    small_half = 2048
    *small, stats = pl.pallas_call(
        time_grad_kernel,
        out_shape=(
            jax.ShapeDtypeStruct((4, small_half, 128), F32),
            jax.ShapeDtypeStruct((4, small_half, 128), BF16),
            jax.ShapeDtypeStruct((4, middle), F32),
        ),
        in_specs=[SM] + [VM] * 8,
        out_specs=(VM, VM, VM),
        scratch_shapes=[pltpu.VMEM((2 * small_half, width), F32), pltpu.VMEM((128, 3 * width), F32)],
        compiler_params=params(13),
        cost_estimate=takes(8),
        name="time_grad",
    )(meta, mid_low, wide, belong, gain_mid, shift_mid, pooled, logit_grad, stats)

    got = trade(small[1], small_order, 0)
    axes = bits("sp") + bits("dp")
    mid_sums = sum_all(stats, axes[:2])
    *small, mid_sums = pl.pallas_call(
        functools.partial(halve_pass_kernel, SMALL_TURN + 1),
        out_shape=(
            jax.ShapeDtypeStruct((4, small_half // 2, 128), F32),
            jax.ShapeDtypeStruct((4, small_half // 2, 128), BF16),
            jax.ShapeDtypeStruct((4, middle), F32),
        ),
        in_specs=[SM, VM, VM, VM],
        out_specs=(VM, VM, VM),
        compiler_params=params(8),
        cost_estimate=takes(1),
        name="time_halve",
    )(meta, small[0], got, mid_sums)
    mid_sums = sum_all(mid_sums, axes[2:])

    class Chain:
        def __init__(self, name, state, order, at):
            self.name, self.state, self.order, self.at = name, state, order, at
            self.stage, self.down = 0, True

        def step(self, after):
            if self.down:
                self.state = halve_step(*self.state, self.order, meta, self.at, self.stage, after, self.name)
                self.stage += 1
                if self.state[1] is None:
                    self.state, self.down, self.stage = self.state[0], False, self.stage - 1
            else:
                self.state = double_step(self.state, self.order, meta, self.at, self.stage, after, self.name)
                self.stage -= 1
            return self.state[0] if self.down else self.state

    chains = {"t": Chain("time", small, small_order, SMALL_TURN)}
    chains["t"].stage = 1
    after = chains["t"].step((mid_sums, mid_sums))
    shift_mid_grad, gain_mid_grad = mid_sums[0], mid_sums[1]
    mid_grad, keep, send = pl.pallas_call(
        mid_grad_kernel,
        out_shape=(
            pltpu.VMEM((most, middle), BF16),
            pltpu.VMEM((most, 640), BF16),
            pltpu.VMEM((most, 640), BF16),
        ),
        in_specs=[SM] + [VM] * 6 + [ANY],
        out_specs=(VM, VM, VM),
        compiler_params=params(6),
        cost_estimate=takes(2),
        name="mid_grad",
    )(meta, mid_act_grad, mid_pre, belong, mid_merged, gain_mid, mid_sums, after)
    other = swap(send, "sp", 1)
    row_scratch = [pick_scratch, plane_scratch, pltpu.SemaphoreType.DMA((5 * most // 128,))]
    gathered = pl.pallas_call(
        space_rows_kernel,
        out_shape=pltpu.VMEM((3 * most, 3 * width), BF16),
        in_specs=[SM, VM, HBM, VM, VM, ANY],
        out_specs=VM,
        scratch_shapes=row_scratch,
        compiler_params=params(10),
        cost_estimate=takes(4),
        name="space_rows",
    )(meta, row_info, in_hbm(stored), part, outer_part, send)

    def space_grad_part(first_tap, taps, after):
        shapes = (
            jax.ShapeDtypeStruct((taps, 1152, 128), F32),
            jax.ShapeDtypeStruct((taps, 1152, 128), BF16),
        )
        if first_tap == 0:
            return pl.pallas_call(
                functools.partial(space_grad_first_kernel, first_tap),
                out_shape=shapes,
                in_specs=[SM, VM, VM, VM, ANY, ANY],
                out_specs=(VM, VM),
                scratch_shapes=[pltpu.VMEM((640, width), F32)],
                compiler_params=params(10),
                cost_estimate=takes(9),
                name="space_grad",
            )(meta, gathered, keep, other, *after)
        return pl.pallas_call(
            functools.partial(space_grad_kernel, first_tap),
            out_shape=shapes,
            in_specs=[SM, VM, HBM, VM, VM, VM, VM, ANY, ANY],
            out_specs=(VM, VM),
            scratch_shapes=[
                pltpu.VMEM((3 * most, 3 * width), BF16),
                pltpu.VMEM((640, width), F32),
                *row_scratch,
            ],
            compiler_params=params(30),
            cost_estimate=takes(11),
            name="space_grad",
        )(meta, row_info, in_hbm(stored), part, outer_part, keep, other, *after)

    chunks = {"b": (0, 4), "c": (4, 5)}
    dense, edges, logits = {}, {}, {}
    left = {"t": 2 * steps - 1, "b": 2 * steps - 1, "c": 2 * steps - 1}
    space_grad = None
    token_shape = jax.ShapeDtypeStruct((8, 128), F32)
    last = {}
    after = send, send

    def step(name):
        left[name] -= 1
        token = chains[name].step(after)
        return token, token

    for event in PLAN:
        if event in "tbc":
            if left[event]:
                after = step(event)
        elif event in "BC":
            name = event.lower()
            keep_part, send_part = space_grad_part(*chunks[name], after)
            chains[name] = Chain("taps" + name, (keep_part, send_part), order, TURN)
            after = send_part, send_part
        elif event in "01":
            side = int(event)
            dense[side], edges[side], logits[side] = pl.pallas_call(
                functools.partial(input_back_kernel, side, frame_count),
                out_shape=(
                    jax.ShapeDtypeStruct((frame_count, cells, width), F32),
                    jax.ShapeDtypeStruct((frame_count, cells, width), BF16),
                    jax.ShapeDtypeStruct((clip_count, classes), F32),
                ),
                in_specs=[SM, VM, VM, HBM, VM, VM, VM, ANY, ANY],
                out_specs=(VM, VM, VM),
                scratch_shapes=[
                    pltpu.VMEM((6 * width, middle), BF16),
                    pltpu.VMEM((2, most // 2 + 256, 3 * width), BF16),
                    pltpu.VMEM((cells, 3 * cells), BF16),
                    pltpu.VMEM((most // 2 + 256, width), BF16),
                    pltpu.VMEM((most // 2 + 256, width), BF16),
                    pltpu.SemaphoreType.DMA(()),
                ],
                compiler_params=params(26),
                cost_estimate=takes(17),
                name="input_back",
            )(meta, col_info, mid_grad, weight, act_grad, pooled, class_lines, *after)
            if side == 0:
                scores = logits[0]
                for axis, bit in bits("sp"):
                    scores = scores + swap(scores, axis, bit)
                up = lax.ppermute(edges[0], "sp", [(i, i - 1) for i in range(1, sp_count)])
            else:
                down = lax.ppermute(edges[1], "sp", [(i, i + 1) for i in range(sp_count - 1)])
            after = edges[side], edges[side]
        elif event == "i":
            input_grad, token = pl.pallas_call(
                input_join_kernel,
                out_shape=(
                    jax.ShapeDtypeStruct((row_count, frame_count, clip_count, col_count, width), F32),
                    token_shape,
                ),
                in_specs=[SM, VM, VM, VM, VM, VM, ANY, ANY],
                out_specs=(VM, VM),
                scratch_shapes=[pltpu.VMEM((clip_count, 8, width), F32)],
                compiler_params=params(18),
                cost_estimate=takes(2),
                name="input_join",
            )(meta, col_info, dense[0], dense[1], down, up, after[0], scores)
            after = token, token
        elif event == "T":
            while left["t"]:
                after = step("t")
            own_half = chains["t"].state
            time_grad, class_weight_grad, token = pl.pallas_call(
                time_join_kernel,
                out_shape=(
                    jax.ShapeDtypeStruct((3 * middle, width), F32),
                    jax.ShapeDtypeStruct((classes, width), F32),
                    token_shape,
                ),
                in_specs=[SM] + [VM] * 5 + [ANY, ANY],
                out_specs=(VM, VM, VM),
                compiler_params=params(16),
                cost_estimate=takes(5),
                name="time_join",
            )(meta, own_half, trade(own_half, small_order, 0), gain_mid, shift_mid, mid_sums, *after)
            after = token, token
        elif event in "pq":
            name = "b" if event == "p" else "c"
            while left[name]:
                after = step(name)
            own_half = chains[name].state
            got_half = trade(own_half, order, 0)
            relay = got_half
            if event == "q":
                relay = pl.pallas_call(
                    relay_kernel,
                    out_shape=jax.ShapeDtypeStruct(got_half.shape, BF16),
                    in_specs=[VM, ANY, ANY],
                    out_specs=VM,
                    compiler_params=params(4),
                    cost_estimate=takes(1),
                    name="relay",
                )(got_half, *after)
            last[name] = [own_half, got_half, swap(own_half, "sp", 1), swap(relay, "sp", 1)]
            after = after[0], got_half
        else:
            name = "b" if event == "P" else "c"
            first_tap, taps = chunks[name]
            piece = pl.BlockSpec((1, 1152, 128), lambda n, meta: (n, 0, 0))
            before = [] if space_grad is None else [space_grad]
            space_grad, token = pl.pallas_call(
                functools.partial(join_kernel, steps),
                grid_spec=pltpu.PrefetchScalarGridSpec(
                    num_scalar_prefetch=1,
                    grid=(taps,),
                    in_specs=[piece] * 4 + [ANY] * (2 + len(before)),
                    out_specs=(
                        pl.BlockSpec((1, width, middle), lambda n, meta, tap=first_tap: (n + tap, 0, 0)),
                        pl.BlockSpec((8, 128), lambda n, meta: (0, 0)),
                    ),
                ),
                out_shape=(jax.ShapeDtypeStruct((9, width, middle), F32), token_shape),
                input_output_aliases={7: 0} if before else {},
                compiler_params=params(12),
                cost_estimate=takes(6),
                name="join",
            )(meta, *last[name], *after, *before)
            after = token, token
    space_grad = space_grad.reshape(3, 3, width, middle)
    input_grad = input_grad.transpose(2, 1, 0, 3, 4)
    time_grad = time_grad.reshape(3, middle, width)
    class_weight_grad = class_weight_grad.T
    logits = scores + class_bias
    return (
        logits,
        input_grad,
        space_grad,
        time_grad,
        gain_mid_grad,
        shift_mid_grad,
        gain_out_grad,
        shift_out_grad,
        class_weight_grad,
        class_bias_grad,
    )


def solution(mesh):
    placed = (
        P("dp", None, "sp", None, None),
        P(),
        P(),
        P(),
        P(),
        P(),
        P(),
        P(),
        P(),
        P("dp"),
        P("dp"),
        P("dp"),
        P("dp", None),
    )
    return jax.shard_map(
        shards,
        mesh=mesh,
        in_specs=placed,
        out_specs=(
            P("dp", None),
            P("dp", None, "sp", None, None),
            P(),
            P(),
            P(),
            P(),
            P(),
            P(),
            P(),
            P(),
        ),
        check_vma=False,
    )
```

```python
import functools

import jax
import jax.numpy as jnp
from jax import lax
from jax.experimental import pallas as pl
from jax.experimental.pallas import tpu as pltpu
from jax.sharding import PartitionSpec as P

EPSILON = 1e-05
HIGH = lax.Precision.HIGHEST
F32 = jnp.float32
BF16 = jnp.bfloat16
S_AT, CORE_AT, ROW_AT, OFF, LEN, PAD, END_AT, FIRST_AT, TURN, SMALL_TURN = 0, 1, 2, 4, 8, 12, 16, 17, 18, 33
META = 48

PLAN = "Bt0btCbt1bctcbticbtcbctbccpTPqQ"

VM = pl.BlockSpec(memory_space=pltpu.VMEM)
SM = pl.BlockSpec(memory_space=pltpu.SMEM)
ANY = pl.BlockSpec(memory_space=pl.ANY)
HBM = pl.BlockSpec(memory_space=pltpu.HBM)


def in_hbm(value):
    return pltpu.with_memory_space_constraint(value, pltpu.HBM)


STEP = 6


def takes(us):
    return pl.CostEstimate(flops=us * 1_100_000_000, bytes_accessed=us * 3_300_000, transcendentals=0)


def params(mib):
    return pltpu.CompilerParams(vmem_limit_bytes=mib << 20)


def nt_dot(a, b):
    return lax.dot_general(a, b, (((1,), (1,)), ((), ())), preferred_element_type=F32)


def tn_dot(a, b):
    return lax.dot_general(a, b, (((0,), (0,)), ((), ())), preferred_element_type=F32)


def dot(a, b):
    return jnp.dot(a, b, preferred_element_type=F32)


def split(value):
    high = value.astype(BF16)
    return high, (value - high.astype(F32)).astype(BF16)


def sigmoid(v):
    return 1.0 / (1.0 + jnp.exp(-v))


def slope(v):
    s = sigmoid(v)
    return s * (1.0 + v * (1.0 - s))


def at16(index):
    return pl.multiple_of(index, 16)


def at64(index):
    return pl.multiple_of(index, 64)


def at128(index):
    return pl.multiple_of(index, 128)


def sweep(rows, size, body):
    count = lax.div(rows, size)

    def one(m, carry):
        body(pl.multiple_of(m * size, size), size)
        return carry

    lax.fori_loop(0, count, one, 0)

    @pl.when(rows > count * size)
    def _():
        body(pl.multiple_of(count * size, size), size // 2)


def pick_rows(row_info, shift):
    place, col, cols = row_info[0:1, :], row_info[1:2, :], row_info[2:3, :]
    home = col - shift
    ok = (col < cols) & (home >= 0) & (home < cols)
    spot = jnp.where(ok, place - shift, -1)
    size = row_info.shape[1]
    index = lax.broadcasted_iota(jnp.int32, (size, size), 0)
    return jnp.where(index == spot, 1.0, 0.0).astype(BF16)


def pick_cols(col_info, shift):
    place, col, cols = col_info[:, 0:1], col_info[:, 1:2], col_info[:, 2:3]
    home = col - shift
    ok = (col < cols) & (home >= 0) & (home < cols)
    spot = jnp.where(ok, place - shift, -1)
    size = col_info.shape[0]
    index = lax.broadcasted_iota(jnp.int32, (size, size), 1)
    return jnp.where(index == spot, 1.0, 0.0).astype(BF16)


def each_list(meta, base, frame_count, store):
    for t in range(frame_count):
        for half in range(2):

            @pl.when(half * 128 < meta[PAD + t])
            def _(t=t, half=half):
                store(t, half, at16(base + meta[OFF + t] + half * 128))


def setup_kernel(
    sp_count, orders, where, frames, rows, cols, values, meta, row_info, col_info, clip_info, own, own_low, ahead, pad
):
    row_count, frame_count, clip_count, col_count, width = values.shape
    size = clip_count * 8
    core = lax.rem(where[1], 2)
    first_row = where[1] * row_count
    total = jnp.int32(0)
    for t in range(frame_count):
        length = jnp.int32(0)
        for b in range(clip_count):
            length += jnp.where(frames[b] > t, cols[b], 0)
        padded = (length + 15) // 16 * 16
        meta[OFF + t], meta[LEN + t], meta[PAD + t] = total, length, padded
        total += padded
    meta[S_AT], meta[CORE_AT], meta[ROW_AT] = (total + 63) // 64 * 64, core, first_row
    meta[END_AT] = total
    meta[FIRST_AT] = jnp.where(where[1] == 0, 1, 0)
    place = where[0] * sp_count + where[1]
    for start, (order, other) in zip((TURN, SMALL_TURN), orders):
        for n, (zero, one) in enumerate(zip(*order)):
            meta[start + n] = jnp.where(place & jnp.where(core == 0, zero, one) != 0, 1, 0)
        meta[start + len(order[0])] = jnp.where(place & jnp.where(core == 0, other[0], other[1]) != 0, 1, 0)

    lane = lax.broadcasted_iota(jnp.int32, (1, size), 1)
    clip, col = lax.shift_right_logical(lane, 3), lane & 7
    zero = jnp.zeros((1, size), jnp.int32)
    of_cell, of_clip = [zero] * 3, [zero] * 3
    for b in range(clip_count):
        for n, source in enumerate((cols, frames, rows)):
            of_cell[n] = jnp.where(clip == b, source[b], of_cell[n])
            of_clip[n] = jnp.where(lane == b, source[b], of_clip[n])
    start = zero
    for b in range(clip_count):
        ahead_of = (frames[b] > of_cell[1]) | ((frames[b] == of_cell[1]) & (clip > b))
        start += jnp.where(ahead_of, cols[b], 0)
    info = [start + col, col, of_cell[0], of_cell[1], of_cell[2], zero, zero, zero]
    for n, line in enumerate(info[:3] + of_clip[1:] + [zero] * 3):
        row_info[n : n + 1, :] = line
    col_info[...] = jnp.concatenate(info, axis=0).astype(F32).T.astype(jnp.int32)
    per_clip = jnp.maximum(of_clip[0] * of_clip[1] * of_clip[2], 1).astype(F32)[:, 0:128]
    clip_info[...] = jnp.concatenate([per_clip] * 8, axis=0).T

    pad[:, col_count:, :] = jnp.zeros((clip_count, 8 - col_count, width), F32)
    cells = col_info[...]
    for h in range(row_count):
        for t in range(frame_count):
            pad[:, 0:col_count, :] = values[h, t]
            inside = (cells[:, 1:2] < cells[:, 2:3]) & (cells[:, 3:4] > t) & (cells[:, 4:5] > first_row + h)
            masked = pad[...].reshape(size, width) * jnp.where(inside, 1.0, 0.0)
            own[h, t], own_low[h, t] = split(masked)

            @pl.when(core == h)
            def _(t=t, masked=masked):
                ahead[t] = masked.astype(BF16)


def gather_setup(row_info, pick):
    info = row_info[...]
    for j in range(3):
        hot = pick_rows(info, j - 1)
        for half in range(2):
            pick[half, j * 128 : (j + 1) * 128, :] = hot[half * 128 : (half + 1) * 128, :]


def gather_plane(meta, pick, source, packed, base, frame_count):
    def store(t, half, row):
        got = dot(pick[half], source(t)).astype(BF16)
        for j in range(3):
            packed[pl.ds(row, 128), j * 512 : (j + 1) * 512] = got[j * 128 : (j + 1) * 128, :]

    each_list(meta, base, frame_count, store)
    packed[pl.ds(at16(base + meta[END_AT]), 128), :] = jnp.zeros((128, 1536), BF16)


def copy_out(rows, source, begin, target, start, sems, action):
    def one(m, carry):
        copy = pltpu.make_async_copy(
            source.at[pl.ds(at64(begin + m * 64), 64)], target.at[pl.ds(at64(start + m * 64), 64)], sems.at[m]
        )
        if action == "start":
            copy.start()
        else:
            copy.wait()
        return carry

    lax.fori_loop(0, lax.div(rows, 64), one, 0)


def space_kernel(
    meta, row_info, own, own_low, weight_in, logit_grad, class_weight, clip_info,
    mid_pre, belong, residual, stored, pooled_grad, bias_grad, packed, pick, weight, sems, load,
):
    frame_count = own.shape[1]
    core = meta[CORE_AT]
    s = meta[S_AT]
    fetch = pltpu.make_async_copy(weight_in, weight, load)
    fetch.start()
    gather_setup(row_info, pick)

    for h in range(2):
        gather_plane(meta, pick, lambda t, h=h: own[h, t], packed, h * s, frame_count)
    copy_out(2 * s, packed, 0, stored, (1 + 2 * core) * s, sems, "start")
    size = row_info.shape[1]
    clip_of = lax.broadcasted_iota(jnp.int32, (size, 128), 0) // 8
    lane = lax.broadcasted_iota(jnp.int32, (size, 128), 1)
    frames_of = jnp.broadcast_to(row_info[3:4, 0:128], (size, 128))
    rows_of = jnp.broadcast_to(row_info[4:5, 0:128], (size, 128))
    for h in range(2):

        def store(t, half, row, h=h):
            hot = pick[half, 128:256, :]
            inside = (clip_of == lane) & (frames_of > t) & (rows_of > meta[ROW_AT] + h)
            belong[pl.ds(row, 128), :] = dot(hot, jnp.where(inside, 1.0, 0.0).astype(BF16)).astype(BF16)
            residual[pl.ds(row, 128), :] = dot(hot, own[h, t]) + dot(hot, own_low[h, t])

        each_list(meta, h * s, frame_count, store)
        belong[pl.ds(at16(h * s + meta[END_AT]), 128), :] = jnp.zeros((128, 128), BF16)
        residual[pl.ds(at16(h * s + meta[END_AT]), 128), :] = jnp.zeros((128, 512), F32)
    clips, classes = logit_grad.shape
    pooled_grad[...] = jnp.zeros(pooled_grad.shape, F32)
    pooled_grad[0:clips, :] = (
        jnp.dot(logit_grad[...], class_weight[...], precision=HIGH, preferred_element_type=F32)
        / clip_info[0:clips, 0:1]
    )
    bias_grad[...] = jnp.zeros(bias_grad.shape, F32)
    bias_grad[:, 0:classes] = jnp.sum(logit_grad[...], axis=0, keepdims=True) * meta[FIRST_AT].astype(F32)
    fetch.wait()
    for h in range(2):

        def conv(row, size, h=h):
            rows = pl.ds(at64(h * s + row), size)

            acc = None
            for plane in range(2):
                i = plane - h + 1
                term = dot(packed[pl.ds(at64(plane * s + row), size), :], weight[i * 1536 : (i + 1) * 1536, :])
                acc = term if acc is None else acc + term
            mid_pre[rows, :] = acc

        sweep(s, 128, conv)
    copy_out(2 * s, packed, 0, stored, (1 + 2 * core) * s, sems, "wait")


def mask_of(belong, row, size):
    return jnp.sum(belong[pl.ds(row, size), :].astype(F32), axis=1, keepdims=True)


def norm_of(merged):
    count = merged[0:1, :]
    return merged[1:2, :] / count, lax.rsqrt(merged[2:3, :] / count + EPSILON)


def norm_sums(meta, values, belong, stats):
    mask = mask_of(belong, 0, 128)
    pivot = jnp.sum(values[0:128, :] * mask, axis=0, keepdims=True) / jnp.maximum(jnp.sum(mask), 1.0)
    stats[...] = jnp.zeros(stats.shape, F32)

    def sums(row, size):
        mask = mask_of(belong, row, size)
        off = (values[pl.ds(row, size), :] - pivot) * mask
        stats[0:1, :] += jnp.sum(mask, axis=0, keepdims=True)
        stats[1:2, :] += jnp.sum(off, axis=0, keepdims=True)
        stats[2:3, :] += jnp.sum(off * off, axis=0, keepdims=True)

    sweep(2 * meta[S_AT], 256, sums)
    count, total = stats[0:1, :], stats[1:2, :]
    stats[2:3, :] = jnp.maximum(stats[2:3, :] - total * total / count, 0.0)
    stats[1:2, :] = total + count * pivot


def space_edge_kernel(
    meta, row_info, mid_in, stored_in, part, outer, weight_in, belong, mid_pre, stored, stats,
    pick, planes, weight, sems, load,
):
    core = meta[CORE_AT]
    s = meta[S_AT]
    frame_count = outer.shape[0]
    fetches = [
        pltpu.make_async_copy(weight_in.at[pl.ds(n * 3072, 1536)], weight.at[pl.ds(n * 1536, 1536)], load.at[n])
        for n in range(2)
    ]
    for fetch in fetches:
        fetch.start()
    gather_setup(row_info, pick)
    gather_plane(meta, pick, lambda t: part[core, t], planes.at[0], 0, frame_count)
    gather_plane(meta, pick, lambda t: outer[t], planes.at[1], 0, frame_count)
    near, far = (3 - core) * s, 5 * core * s
    copy_out(s, planes.at[0], 0, stored, near, sems.at[0], "start")
    copy_out(s, planes.at[1], 0, stored, far, sems.at[1], "start")
    for fetch in fetches:
        fetch.wait()

    def conv(row, size):
        for n, row_of, lines in ((0, 1 - core, 1 - core), (1, core, core)):
            block = pl.ds(at64(row_of * s + row), size)
            taps = weight[pl.ds(pl.multiple_of(lines * 1536, 512), 1536), :]
            mid_pre[block, :] += dot(planes[n, pl.ds(row, size), :], taps)

    sweep(s, 128, conv)
    norm_sums(meta, mid_pre, belong, stats)
    copy_out(s, planes.at[0], 0, stored, near, sems.at[0], "wait")
    copy_out(s, planes.at[1], 0, stored, far, sems.at[1], "wait")


def shift_lists(meta, frame_count, source, target, width, move):
    s = meta[S_AT]
    for h in range(2):

        def store(t, half, row, h=h):
            other = t + move
            if 0 <= other < frame_count:
                block = source(at16(h * s + meta[OFF + other] + half * 128))
                place = half * 128 + lax.broadcasted_iota(jnp.int32, (128, 1), 0)
                keep = jnp.where(place < meta[LEN + other], 1.0, 0.0).astype(BF16)
                target(row, block * keep)
            else:
                target(row, jnp.zeros((128, width), BF16))

        each_list(meta, h * s, frame_count, store)
        target(at16(h * s + meta[END_AT]), jnp.zeros((128, width), BF16))


def time_kernel(
    frame_count, meta, mid_pre, belong, merged, gain, shift, weight, after, mid_low, out_pre, stats, wide
):
    rows = 2 * meta[S_AT]
    center, scale = norm_of(merged)

    def act(row, size):
        block = pl.ds(row, size)
        value = gain[...] * ((mid_pre[block, :] - center) * scale) + shift[...]
        low = (value * sigmoid(value) * mask_of(belong, row, size)).astype(BF16)
        wide[block, 1152:2304] = low
        mid_low[block, :] = low

    sweep(rows, 256, act)
    wide[pl.ds(at128(rows), 256), :] = jnp.zeros((256, 3456), BF16)
    for k in (0, 2):

        def source(row):
            return wide[pl.ds(row, 128), 1152:2304]

        def target(row, value, k=k):
            wide[pl.ds(row, 128), k * 1152 : (k + 1) * 1152] = value

        shift_lists(meta, frame_count, source, target, 1152, k - 1)

    def conv(row, size):
        out_pre[pl.ds(row, size), :] = dot(wide[pl.ds(row, size), :], weight[...])

    sweep(rows, 256, conv)
    norm_sums(meta, out_pre, belong, stats)


def act_kernel(
    meta, out_pre, belong, residual, merged, gain_ref, shift_ref, pooled_grad, bias_grad, clip_info,
    act_grad, stats, pooled,
):
    center, scale = norm_of(merged)
    high, rest = split(pooled_grad[...])
    pooled[...] = jnp.zeros(pooled.shape, F32)
    stats[...] = jnp.zeros(stats.shape, F32)

    def step(row, size):
        block = pl.ds(row, size)
        hot = belong[block, :]
        normed = (out_pre[block, :] - center) * scale
        value = gain_ref[...] * normed + shift_ref[...] + residual[block, :]
        s = sigmoid(value)
        first, second = split(value * s)
        pooled[...] += tn_dot(hot, first) + tn_dot(hot, second)
        grad = (dot(hot, high) + dot(hot, rest)) * (s * (1.0 + value * (1.0 - s)))
        act_grad[block, :] = grad
        stats[0:1, :] += jnp.sum(grad, axis=0, keepdims=True)
        stats[1:2, :] += jnp.sum(grad * normed, axis=0, keepdims=True)

    sweep(2 * meta[S_AT], 256, step)
    stats[2:3, :] = bias_grad[...]
    pooled[...] = pooled[...] / clip_info[:, 0:1]


def back_kernel(
    frame_count, meta, act_grad, out_pre, belong, out_merged, out_gain, out_sums, weight, mid_pre, mid_merged,
    mid_gain, mid_shift, wide, mid_act_grad, stats,
):
    rows = 2 * meta[S_AT]
    out_center, out_scale = norm_of(out_merged)
    mid_center, mid_scale = norm_of(mid_merged)
    out_shift_part = out_sums[0:1, :] / out_merged[0:1, :]
    out_gain_part = out_sums[1:2, :] / out_merged[0:1, :]
    stats[...] = jnp.zeros(stats.shape, F32)

    def grad(row, size):
        block = pl.ds(row, size)
        normed = (out_pre[block, :] - out_center) * out_scale
        inner = act_grad[block, :] - mask_of(belong, row, size) * (out_shift_part + normed * out_gain_part)
        wide[block, 512:1024] = (out_gain[...] * out_scale * inner).astype(BF16)

    sweep(rows, 256, grad)
    wide[pl.ds(at128(rows), 256), :] = jnp.zeros((256, 1536), BF16)
    for k in (0, 2):

        def source(row):
            return wide[pl.ds(row, 128), 512:1024]

        def target(row, value, k=k):
            wide[pl.ds(row, 128), k * 512 : (k + 1) * 512] = value

        shift_lists(meta, frame_count, source, target, 512, 1 - k)

    def conv(row, size):
        block = pl.ds(row, size)
        acc = nt_dot(wide[block, 0:512], weight[0])
        acc += nt_dot(wide[block, 512:1024], weight[1])
        acc += nt_dot(wide[block, 1024:1536], weight[2])
        normed = (mid_pre[block, :] - mid_center) * mid_scale
        acc = acc * mask_of(belong, row, size) * slope(mid_gain[...] * normed + mid_shift[...])
        mid_act_grad[block, :] = acc
        stats[0:1, :] += jnp.sum(acc, axis=0, keepdims=True)
        stats[1:2, :] += jnp.sum(acc * normed, axis=0, keepdims=True)

    sweep(rows, 256, conv)


def typical_act(gain, shift):
    spread = 3.0**0.5 * gain
    value = 0.0
    for share, at in ((1.0, shift - spread), (4.0, shift), (1.0, shift + spread)):
        value += share / 6.0 * at * sigmoid(at)
    return jnp.concatenate([value] * 8, axis=0).T[:, 0:1]


def time_grad_kernel(
    meta, mid_low, wide, belong, gain, shift, pooled, logit_grad, stats, keep, send, passed, total, by_clip
):
    rows = 2 * meta[S_AT]
    by_clip[...] = jnp.zeros(by_clip.shape, F32)

    def sums(row, size):
        by_clip[...] += tn_dot(belong[pl.ds(row, size), :], wide[pl.ds(row, size), :])

    sweep(rows, 256, sums)
    grad_sums = jnp.sum(by_clip[...], axis=0, keepdims=True)
    passed[0:2, :] = stats[...]
    passed[2:3, :] = grad_sums[:, 0:1152]
    passed[3:4, :] = jnp.zeros((1, 1152), F32)
    passed[3:4, 0:384] = grad_sums[:, 1152:1536]
    typical = typical_act(gain[...], shift[...])
    core = meta[CORE_AT]
    middle = mid_low.shape[1]
    classes = logit_grad.shape[1]
    half = keep.shape[1]
    for k in range(3):
        lines = slice(k * middle, (k + 1) * middle)
        total[lines, :] = -typical * grad_sums[:, k * 512 : (k + 1) * 512]

        def step(row, size, k=k, lines=lines):
            block = pl.ds(row, size)
            total[lines, :] += tn_dot(mid_low[block, :], wide[block, k * 512 : (k + 1) * 512])

        sweep(rows, 256, step)
    total[3 * middle : 3 * middle + classes, :] = lax.dot_general(
        logit_grad[...], pooled[0 : logit_grad.shape[0], :], (((0,), (0,)), ((), ())), precision=HIGH, preferred_element_type=F32
    )
    total[3 * middle + classes :, :] = jnp.zeros((2 * half - 3 * middle - classes, 512), F32)
    for lane in range(4):
        lanes = slice(lane * 128, (lane + 1) * 128)
        keep[lane] = total[pl.ds(at128(core * half), half), lanes]
        send[lane] = total[pl.ds(at128((1 - core) * half), half), lanes].astype(BF16)


def relay_kernel(got, *rest):
    rest[-1][...] = got[...]


def time_join_kernel(meta, own, got, gain, shift, sums, after, also, time_grad, class_grad, token):
    token[...] = jnp.zeros(token.shape, F32)
    half = own.shape[1]
    rest = time_grad.shape[0] - half

    def place(first, second):
        for lane in range(4):
            lanes = slice(lane * 128, (lane + 1) * 128)
            time_grad[0:half, lanes] = first[lane].astype(F32)
            time_grad[half:, lanes] = second[lane, 0:rest, :].astype(F32)
            class_grad[:, lanes] = second[lane, rest : rest + class_grad.shape[0], :].astype(F32)

    @pl.when(meta[CORE_AT] == 0)
    def _():
        place(own, got)

    @pl.when(meta[CORE_AT] != 0)
    def _():
        place(got, own)

    typical = typical_act(gain[...], shift[...])
    middle = gain.shape[1]
    grad_sums = jnp.concatenate([sums[2:3, :], sums[3:4, 0:384]], axis=1)
    for k in range(3):
        time_grad[k * middle : (k + 1) * middle, :] += typical * grad_sums[:, k * 512 : (k + 1) * 512]


def mid_grad_kernel(meta, mid_act_grad, mid_pre, belong, merged, gain, sums, after, whole, keep, send):
    core = meta[CORE_AT]
    center, scale = norm_of(merged)
    shift_part = sums[0:1, :] / merged[0:1, :]
    gain_part = sums[1:2, :] / merged[0:1, :]

    def step(row, size):
        block = pl.ds(row, size)
        normed = (mid_pre[block, :] - center) * scale
        inner = mid_act_grad[block, :] - mask_of(belong, row, size) * (shift_part + normed * gain_part)
        low = (gain[...] * scale * inner).astype(BF16)
        whole[block, :] = low

        @pl.when(core == 0)
        def _():
            keep[block, 0:512] = low[:, 0:512]
            send[block, 0:512] = low[:, 512:1024]

        @pl.when(core != 0)
        def _():
            keep[block, 0:512] = low[:, 512:1024]
            send[block, 0:512] = low[:, 0:512]

        keep[block, 512:640] = low[:, 1024:1152]
        send[block, 512:640] = low[:, 1024:1152]

    sweep(2 * meta[S_AT], 256, step)


def space_grad_taps(first_tap, meta, packed, own, part, keep, send, total):
    core = meta[CORE_AT]
    s = meta[S_AT]
    mine = meta[TURN]

    def one(tap, carry):
        i, j = lax.div(first_tap + tap, 3), lax.rem(first_tap + tap, 3)
        lanes = pl.ds(at128(j * 512), 512)

        total[...] = jnp.zeros(total.shape, F32)

        def step(row, size):
            first = packed[pl.ds(at64((2 * core + i) * s + row), size), lanes]
            second = packed[pl.ds(at64((2 - 2 * core + i) * s + row), size), lanes]
            total[...] += tn_dot(own[pl.ds(row, size), :], first) + tn_dot(part[pl.ds(row, size), :], second)

        sweep(2 * s, 256, step)
        for half, out, kind in ((mine, keep, F32), (1 - mine, send, BF16)):
            lane = half * 256
            out[tap, 0:512, :] = total[0:512, pl.ds(at128(lane), 128)].astype(kind)
            out[tap, 512:1024, :] = total[0:512, pl.ds(at128(lane + 128), 128)].astype(kind)
            out[tap, 1024:1152, :] = total[512:640, pl.ds(at128(core * 256 + half * 128), 128)].astype(kind)
        return carry

    lax.fori_loop(0, keep.shape[0], one, 0)


def space_rows(meta, row_info, stored, part, outer, packed, pick, plane, sems):
    core = meta[CORE_AT]
    s = meta[S_AT]
    copy_out(4 * s, stored, 2 * core * s, packed, 2 * core * s, sems, "start")
    gather_setup(row_info, pick)
    for source, place in ((lambda t: part[1 - core, t], 4 - 3 * core), (lambda t: outer[t], 5 - 5 * core)):
        gather_plane(meta, pick, source, plane, 0, outer.shape[0])

        def put(row, size, place=place):
            packed[pl.ds(at64(place * s + row), size), :] = plane[pl.ds(row, size), :]

        sweep(s, 128, put)
    copy_out(4 * s, stored, 2 * core * s, packed, 2 * core * s, sems, "wait")


def space_rows_kernel(meta, row_info, stored, part, outer, after, packed, pick, plane, sems):
    space_rows(meta, row_info, stored, part, outer, packed, pick, plane, sems)


def space_grad_kernel(
    first_tap, meta, row_info, stored, near, outer, own, part, after, also, keep, send, packed, total, pick, plane, sems
):
    space_rows(meta, row_info, stored, near, outer, packed, pick, plane, sems)
    space_grad_taps(first_tap, meta, packed, own, part, keep, send, total)


def space_grad_first_kernel(first_tap, meta, packed, own, part, after, also, keep, send, total):
    space_grad_taps(first_tap, meta, packed, own, part, keep, send, total)


def halve_kernel(at, meta, keep, got, after, also, next_keep, next_send):
    half = next_keep.shape[1]
    mine = meta[at]

    def one(tap, carry):
        low, high = pl.ds(at16(mine * half), half), pl.ds(at16((1 - mine) * half), half)
        next_keep[tap] = keep[tap, low, :] + got[tap, low, :].astype(F32)
        next_send[tap] = (keep[tap, high, :] + got[tap, high, :].astype(F32)).astype(BF16)
        return carry

    lax.fori_loop(0, keep.shape[0], one, 0)


def halve_pass_kernel(at, meta, keep, got, value, next_keep, next_send, passed):
    passed[...] = value[...]
    halve_kernel(at, meta, keep, got, None, None, next_keep, next_send)


def share_kernel(keep, got, after, also, out):
    def one(tap, carry):
        out[tap] = (keep[tap] + got[tap].astype(F32)).astype(BF16)
        return carry

    lax.fori_loop(0, keep.shape[0], one, 0)


def double_kernel(at, meta, own, got, after, also, out):
    half = own.shape[1]
    mine = meta[at]

    def one(tap, carry):
        out[tap, pl.ds(at16(mine * half), half), :] = own[tap]
        out[tap, pl.ds(at16((1 - mine) * half), half), :] = got[tap]
        return carry

    lax.fori_loop(0, own.shape[0], one, 0)


def input_back_kernel(
    side, frame_count, meta, col_info, grad, weight_in, act_grad, pooled, class_weight, after, also,
    dense, edge, logits, weight, wide, spread, high, rest, load,
):
    s = meta[S_AT]
    fetch = pltpu.make_async_copy(weight_in.at[pl.ds(side * 1536, 3072)], weight, load)
    fetch.start()
    if side == 0:
        logits[...] = lax.dot_general(
            pooled[0 : logits.shape[0], :],
            class_weight[...],
            (((1,), (1,)), ((), ())),
            precision=HIGH,
            preferred_element_type=F32,
        )
    else:
        logits[...] = jnp.zeros(logits.shape, F32)
    info = col_info[...]
    for j in range(3):
        spread[:, j * 256 : (j + 1) * 256] = pick_cols(info, j - 1)

    def cut(row, size):
        first, second = split(act_grad[pl.ds(at64(side * s + row), size), :])
        high[pl.ds(row, size), :] = first
        rest[pl.ds(row, size), :] = second

    sweep(s, 128, cut)
    for part in (high, rest):
        part[pl.ds(at64(s), 256), :] = jnp.zeros((256, 512), BF16)
    for plane in range(2):
        wide[plane, pl.ds(at64(s), 256), :] = jnp.zeros((256, 1536), BF16)
    fetch.wait()
    outer_weight, inner_weight = weight[0:1536, :], weight[1536:3072, :]
    if side:
        outer_weight, inner_weight = inner_weight, outer_weight

    def conv(row, size):
        near, far = grad[pl.ds(at64(side * s + row), size), :], grad[pl.ds(at64((1 - side) * s + row), size), :]
        both = nt_dot(jnp.concatenate([near, far], axis=0), outer_weight)
        wide[0, pl.ds(row, size), :] = both[0:size, :].astype(BF16)
        wide[1, pl.ds(row, size), :] = (both[size:, :] + nt_dot(near, inner_weight)).astype(BF16)

    sweep(s, 128, conv)
    for t in range(frame_count):

        def scatter(size, t=t):
            rows = pl.ds(at16(meta[OFF + t]), size)
            edge_acc = inner = None
            for j in range(3):
                hot = spread[:, j * 256 : j * 256 + size]
                first = dot(hot, wide[0, rows, j * 512 : (j + 1) * 512])
                second = dot(hot, wide[1, rows, j * 512 : (j + 1) * 512])
                edge_acc = first if j == 0 else edge_acc + first
                inner = second if j == 0 else inner + second
            hot = spread[:, 256 : 256 + size]
            edge[t] = edge_acc.astype(BF16)
            dense[t] = inner + dot(hot, high[rows, :]) + dot(hot, rest[rows, :])

        @pl.when(meta[LEN + t] > 128)
        def _(scatter=scatter):
            scatter(256)

        @pl.when(meta[LEN + t] <= 128)
        def _(scatter=scatter):
            scatter(128)


def input_join_kernel(meta, col_info, first, second, down, up, after, also, out, token, pad):
    frame_count, clip_count, col_count, width = out.shape[1:]
    token[...] = jnp.zeros(token.shape, F32)
    cells = col_info[...]
    for h, (own, got) in enumerate(((first, down), (second, up))):
        for t in range(frame_count):
            inside = (cells[:, 1:2] < cells[:, 2:3]) & (cells[:, 3:4] > t) & (cells[:, 4:5] > meta[ROW_AT] + h)
            value = jnp.where(inside, own[t] + got[t].astype(F32), 0.0)
            pad[...] = value.reshape(clip_count, 8, width)
            out[h, t] = pad[:, 0:col_count, :]


def join_kernel(steps, meta, own, got, part_own, part_got, after, also, *rest):
    out, token = rest[-2:]
    token[...] = jnp.zeros(token.shape, F32)
    core = meta[CORE_AT]
    mine, other = meta[TURN], meta[TURN + steps]
    for piece, half, owner in (
        (own, mine, core),
        (got, 1 - mine, core),
        (part_own, other, 1 - core),
        (part_got, 1 - other, 1 - core),
    ):
        row = half * 256
        middles = pl.ds(at128(owner * 512), 512)
        out[0, pl.ds(at128(row), 128), middles] = piece[0, 0:512, :].astype(F32).T
        out[0, pl.ds(at128(row + 128), 128), middles] = piece[0, 512:1024, :].astype(F32).T
        out[0, pl.ds(at128(owner * 256 + half * 128), 128), 1024:1152] = piece[0, 1024:1152, :].astype(F32).T


def swap(value, axis, bit):
    size = lax.axis_size(axis)
    if size <= bit:
        return None
    return lax.ppermute(value, axis, [(i, i ^ bit) for i in range(size)])


def bits(axis):
    return [(axis, 1 << n) for n in range((lax.axis_size(axis) - 1).bit_length())]


def sum_all(value, axes):
    for axis, bit in axes:
        value = value + swap(value, axis, bit)
    return value


def merge_all(stats):
    stats = stats[:3]
    row = lax.broadcasted_iota(jnp.int32, stats.shape, 0)
    for axis, bit in bits("sp") + bits("dp"):
        other = swap(stats, axis, bit)
        gap = stats[1] / stats[0] - other[1] / other[0]
        extra = gap * gap * (stats[0] * other[0] / (stats[0] + other[0]))
        stats = stats + other + jnp.where(row == 2, extra[None], 0.0)
    return stats


def trade(value, order, stage):
    size = lax.axis_size(("dp", "sp"))
    return lax.ppermute(value, ("dp", "sp"), [(i, i ^ order[i % 2][stage]) for i in range(size)])


def halve_step(keep, send, order, meta, at, stage, after, name):
    got = trade(send, order, stage)
    n, rows, lanes = keep.shape
    if stage + 1 == len(order[0]):
        share = pl.pallas_call(
            share_kernel,
            out_shape=jax.ShapeDtypeStruct(keep.shape, BF16),
            in_specs=[VM, VM, ANY, ANY],
            out_specs=VM,
            compiler_params=params(6),
            cost_estimate=takes(STEP),
            name=name + "_share",
        )(keep, got, *after)
        return share, None
    half = rows // 2
    if half % 16:
        pairs = (keep + got.astype(F32)).reshape(n, 2, half, lanes)
        mine = meta[at + stage + 1]
        keep = lax.dynamic_index_in_dim(pairs, mine, 1, keepdims=False)
        send = lax.dynamic_index_in_dim(pairs, 1 - mine, 1, keepdims=False).astype(BF16)
        return keep, send
    return pl.pallas_call(
        functools.partial(halve_kernel, at + stage + 1),
        out_shape=(
            jax.ShapeDtypeStruct((n, half, lanes), F32),
            jax.ShapeDtypeStruct((n, half, lanes), BF16),
        ),
        in_specs=[SM, VM, VM, ANY, ANY],
        out_specs=(VM, VM),
        compiler_params=params(10),
        cost_estimate=takes(STEP),
        name=name + "_halve%d" % stage,
    )(meta, keep, got, *after)


def double_step(own, order, meta, at, stage, after, name):
    got = trade(own, order, stage)
    n, rows, lanes = own.shape
    if rows % 16:
        mine = meta[at + stage]
        return jnp.concatenate([jnp.where(mine == 0, own, got), jnp.where(mine == 0, got, own)], axis=1)
    return pl.pallas_call(
        functools.partial(double_kernel, at + stage),
        out_shape=jax.ShapeDtypeStruct((n, 2 * rows, lanes), BF16),
        in_specs=[SM, VM, VM, ANY, ANY],
        out_specs=VM,
        compiler_params=params(8),
        cost_estimate=takes(STEP),
        name=name + "_double%d" % stage,
    )(meta, own, got, *after)


def shards(
    clip_input,
    space_weight,
    time_weight,
    gain_mid,
    shift_mid,
    gain_out,
    shift_out,
    class_weight,
    class_bias,
    frames,
    rows,
    cols,
    logit_grad,
):
    clip_count, frame_count, row_count, col_count, width = clip_input.shape
    middle = space_weight.shape[-1]
    classes = class_weight.shape[1]
    cells = clip_count * 8
    most = row_count * frame_count * clip_count * col_count
    sp_count = lax.axis_size("sp")
    x = [bit for _, bit in bits("sp")[1:]]
    y, z = [[bit * sp_count for _, bit in part] for part in (bits("dp")[:1], bits("dp")[1:])]
    order = x + y + z, y + x + z
    small_order = [1] + order[0], [1] + order[1]
    steps = len(order[0])
    orders = (order, (order[1][0], order[0][0])), (small_order, (1, 1))
    place = jnp.stack([lax.axis_index("dp"), lax.axis_index("sp")]).astype(jnp.int32)
    cells_shape = (row_count, frame_count, cells, width)
    meta, row_info, col_info, clip_info, own, own_low, ahead = pl.pallas_call(
        functools.partial(setup_kernel, sp_count, orders),
        out_shape=(
            jax.ShapeDtypeStruct((META,), jnp.int32),
            jax.ShapeDtypeStruct((8, cells), jnp.int32),
            jax.ShapeDtypeStruct((cells, 8), jnp.int32),
            jax.ShapeDtypeStruct((128, 8), F32),
            jax.ShapeDtypeStruct(cells_shape, BF16),
            jax.ShapeDtypeStruct(cells_shape, BF16),
            jax.ShapeDtypeStruct(cells_shape[1:], BF16),
        ),
        in_specs=[SM, SM, SM, SM, VM],
        out_specs=(SM, VM, VM, VM, VM, VM, VM),
        scratch_shapes=[pltpu.VMEM((clip_count, 8, width), F32)],
        compiler_params=params(20),
        cost_estimate=takes(3),
        name="setup",
    )(place, frames, rows, cols, clip_input.transpose(2, 1, 0, 3, 4))
    class_lines = class_weight.T

    part = swap(own, "sp", 1)
    across = [(i, i + 1 if i % 2 else i - 1) for i in range(sp_count)]
    outer = lax.ppermute(ahead, "sp", [(i, j) for i, j in across if 0 <= j < sp_count])
    outer_part = swap(outer, "sp", 1)

    weight = in_hbm(space_weight.reshape(9 * width, middle))
    stored_shape = pltpu.HBM((3 * most, 3 * width), BF16)
    pick_scratch = pltpu.VMEM((2, 384, cells), BF16)
    plane_scratch = pltpu.VMEM((most // 2 + 256, 3 * width), BF16)
    mid_pre, belong, residual, stored, pooled_grad, bias_grad = pl.pallas_call(
        space_kernel,
        out_shape=(
            pltpu.VMEM((most, middle), F32),
            pltpu.VMEM((most + 256, 128), BF16),
            pltpu.VMEM((most + 256, width), F32),
            stored_shape,
            pltpu.VMEM((128, width), F32),
            pltpu.VMEM((1, width), F32),
        ),
        in_specs=[SM, VM, VM, VM, HBM, VM, VM, VM],
        out_specs=(VM, VM, VM, HBM, VM, VM),
        scratch_shapes=[
            pltpu.VMEM((most + 256, 3 * width), BF16),
            pick_scratch,
            pltpu.VMEM((9 * width, middle), BF16),
            pltpu.SemaphoreType.DMA((most // 64,)),
            pltpu.SemaphoreType.DMA(()),
        ],
        compiler_params=params(24),
        cost_estimate=takes(14),
        name="space_conv",
    )(meta, row_info, own, own_low, weight, logit_grad, class_lines, clip_info)
    mid_pre, stored, stats = pl.pallas_call(
        space_edge_kernel,
        out_shape=(
            pltpu.VMEM((most, middle), F32),
            stored_shape,
            jax.ShapeDtypeStruct((3, middle), F32),
        ),
        in_specs=[SM, VM, VM, HBM, VM, VM, HBM, VM],
        out_specs=(VM, HBM, VM),
        scratch_shapes=[
            pick_scratch,
            pltpu.VMEM((2, most // 2 + 256, 3 * width), BF16),
            pltpu.VMEM((6 * width, middle), BF16),
            pltpu.SemaphoreType.DMA((2, most // 128)),
            pltpu.SemaphoreType.DMA((2,)),
        ],
        input_output_aliases={2: 0, 3: 1},
        compiler_params=params(21),
        cost_estimate=takes(9),
        name="space_edge",
    )(meta, row_info, mid_pre, in_hbm(stored), part, outer, weight, belong)
    gain_mid, shift_mid = gain_mid[None], shift_mid[None]
    gain_out, shift_out = gain_out[None], shift_out[None]
    mid_merged = merge_all(stats)
    mid_low, out_pre, stats = pl.pallas_call(
        functools.partial(time_kernel, frame_count),
        out_shape=(
            pltpu.VMEM((most, middle), BF16),
            pltpu.VMEM((most, width), F32),
            jax.ShapeDtypeStruct((3, width), F32),
        ),
        in_specs=[SM, VM, VM, VM, VM, VM, VM, ANY],
        out_specs=(VM, VM, VM),
        scratch_shapes=[pltpu.VMEM((most + 256, 3 * middle), BF16)],
        compiler_params=params(19),
        cost_estimate=takes(8),
        name="time_conv",
    )(meta, mid_pre, belong, mid_merged, gain_mid, shift_mid, time_weight.reshape(3 * middle, width), outer_part)

    out_merged = merge_all(stats)
    act_grad, stats, pooled = pl.pallas_call(
        act_kernel,
        out_shape=(
            pltpu.VMEM((most, width), F32),
            jax.ShapeDtypeStruct((3, width), F32),
            jax.ShapeDtypeStruct((128, width), F32),
        ),
        in_specs=[SM] + [VM] * 9,
        out_specs=(VM, VM, VM),
        compiler_params=params(4),
        cost_estimate=takes(3),
        name="act",
    )(meta, out_pre, belong, residual, out_merged, gain_out, shift_out, pooled_grad, bias_grad, clip_info)

    out_sums = sum_all(stats, bits("sp") + bits("dp"))
    shift_out_grad, gain_out_grad, class_bias_grad = out_sums[0], out_sums[1], out_sums[2, :classes]
    wide, mid_act_grad, stats = pl.pallas_call(
        functools.partial(back_kernel, frame_count),
        out_shape=(
            pltpu.VMEM((most + 256, 3 * width), BF16),
            pltpu.VMEM((most, middle), F32),
            jax.ShapeDtypeStruct((2, middle), F32),
        ),
        in_specs=[SM] + [VM] * 11,
        out_specs=(VM, VM, VM),
        compiler_params=params(7),
        cost_estimate=takes(6),
        name="time_back",
    )(
        meta, act_grad, out_pre, belong, out_merged, gain_out, out_sums, time_weight, mid_pre, mid_merged,
        gain_mid, shift_mid,
    )

    small_half = 2048
    *small, stats = pl.pallas_call(
        time_grad_kernel,
        out_shape=(
            jax.ShapeDtypeStruct((4, small_half, 128), F32),
            jax.ShapeDtypeStruct((4, small_half, 128), BF16),
            jax.ShapeDtypeStruct((4, middle), F32),
        ),
        in_specs=[SM] + [VM] * 8,
        out_specs=(VM, VM, VM),
        scratch_shapes=[pltpu.VMEM((2 * small_half, width), F32), pltpu.VMEM((128, 3 * width), F32)],
        compiler_params=params(13),
        cost_estimate=takes(8),
        name="time_grad",
    )(meta, mid_low, wide, belong, gain_mid, shift_mid, pooled, logit_grad, stats)

    got = trade(small[1], small_order, 0)
    axes = bits("sp")[1:] + bits("dp") + bits("sp")[:1]
    mid_sums = sum_all(stats, axes[:2])
    *small, mid_sums = pl.pallas_call(
        functools.partial(halve_pass_kernel, SMALL_TURN + 1),
        out_shape=(
            jax.ShapeDtypeStruct((4, small_half // 2, 128), F32),
            jax.ShapeDtypeStruct((4, small_half // 2, 128), BF16),
            jax.ShapeDtypeStruct((4, middle), F32),
        ),
        in_specs=[SM, VM, VM, VM],
        out_specs=(VM, VM, VM),
        compiler_params=params(8),
        cost_estimate=takes(1),
        name="time_halve",
    )(meta, small[0], got, mid_sums)
    mid_sums = sum_all(mid_sums, axes[2:])

    class Chain:
        def __init__(self, name, state, order, at):
            self.name, self.state, self.order, self.at = name, state, order, at
            self.stage, self.down = 0, True

        def step(self, after):
            if self.down:
                self.state = halve_step(*self.state, self.order, meta, self.at, self.stage, after, self.name)
                self.stage += 1
                if self.state[1] is None:
                    self.state, self.down, self.stage = self.state[0], False, self.stage - 1
            else:
                self.state = double_step(self.state, self.order, meta, self.at, self.stage, after, self.name)
                self.stage -= 1
            return self.state[0] if self.down else self.state

    chains = {"t": Chain("time", small, small_order, SMALL_TURN)}
    chains["t"].stage = 1
    after = chains["t"].step((mid_sums, mid_sums))
    shift_mid_grad, gain_mid_grad = mid_sums[0], mid_sums[1]
    mid_grad, keep, send = pl.pallas_call(
        mid_grad_kernel,
        out_shape=(
            pltpu.VMEM((most, middle), BF16),
            pltpu.VMEM((most, 640), BF16),
            pltpu.VMEM((most, 640), BF16),
        ),
        in_specs=[SM] + [VM] * 6 + [ANY],
        out_specs=(VM, VM, VM),
        compiler_params=params(6),
        cost_estimate=takes(2),
        name="mid_grad",
    )(meta, mid_act_grad, mid_pre, belong, mid_merged, gain_mid, mid_sums, after)
    other = swap(send, "sp", 1)
    row_scratch = [pick_scratch, plane_scratch, pltpu.SemaphoreType.DMA((5 * most // 128,))]
    gathered = pl.pallas_call(
        space_rows_kernel,
        out_shape=pltpu.VMEM((3 * most, 3 * width), BF16),
        in_specs=[SM, VM, HBM, VM, VM, ANY],
        out_specs=VM,
        scratch_shapes=row_scratch,
        compiler_params=params(10),
        cost_estimate=takes(4),
        name="space_rows",
    )(meta, row_info, in_hbm(stored), part, outer_part, send)

    def space_grad_part(first_tap, taps, after):
        shapes = (
            jax.ShapeDtypeStruct((taps, 1152, 128), F32),
            jax.ShapeDtypeStruct((taps, 1152, 128), BF16),
        )
        if first_tap == 0:
            return pl.pallas_call(
                functools.partial(space_grad_first_kernel, first_tap),
                out_shape=shapes,
                in_specs=[SM, VM, VM, VM, ANY, ANY],
                out_specs=(VM, VM),
                scratch_shapes=[pltpu.VMEM((640, width), F32)],
                compiler_params=params(10),
                cost_estimate=takes(9),
                name="space_grad",
            )(meta, gathered, keep, other, *after)
        return pl.pallas_call(
            functools.partial(space_grad_kernel, first_tap),
            out_shape=shapes,
            in_specs=[SM, VM, HBM, VM, VM, VM, VM, ANY, ANY],
            out_specs=(VM, VM),
            scratch_shapes=[
                pltpu.VMEM((3 * most, 3 * width), BF16),
                pltpu.VMEM((640, width), F32),
                *row_scratch,
            ],
            compiler_params=params(30),
            cost_estimate=takes(11),
            name="space_grad",
        )(meta, row_info, in_hbm(stored), part, outer_part, keep, other, *after)

    chunks = {"b": (0, 4), "c": (4, 5)}
    dense, edges, logits = {}, {}, {}
    left = {"t": 2 * steps - 1, "b": 2 * steps - 1, "c": 2 * steps - 1}
    space_grad = None
    token_shape = jax.ShapeDtypeStruct((8, 128), F32)
    last = {}
    after = send, send

    def step(name):
        left[name] -= 1
        token = chains[name].step(after)
        return token, token

    for event in PLAN:
        if event in "tbc":
            if left[event]:
                after = step(event)
        elif event in "BC":
            name = event.lower()
            keep_part, send_part = space_grad_part(*chunks[name], after)
            chains[name] = Chain("taps" + name, (keep_part, send_part), order, TURN)
            after = send_part, send_part
        elif event in "01":
            side = int(event)
            dense[side], edges[side], logits[side] = pl.pallas_call(
                functools.partial(input_back_kernel, side, frame_count),
                out_shape=(
                    jax.ShapeDtypeStruct((frame_count, cells, width), F32),
                    jax.ShapeDtypeStruct((frame_count, cells, width), BF16),
                    jax.ShapeDtypeStruct((clip_count, classes), F32),
                ),
                in_specs=[SM, VM, VM, HBM, VM, VM, VM, ANY, ANY],
                out_specs=(VM, VM, VM),
                scratch_shapes=[
                    pltpu.VMEM((6 * width, middle), BF16),
                    pltpu.VMEM((2, most // 2 + 256, 3 * width), BF16),
                    pltpu.VMEM((cells, 3 * cells), BF16),
                    pltpu.VMEM((most // 2 + 256, width), BF16),
                    pltpu.VMEM((most // 2 + 256, width), BF16),
                    pltpu.SemaphoreType.DMA(()),
                ],
                compiler_params=params(26),
                cost_estimate=takes(17),
                name="input_back",
            )(meta, col_info, mid_grad, weight, act_grad, pooled, class_lines, *after)
            if side == 0:
                scores = logits[0]
                for axis, bit in bits("sp"):
                    scores = scores + swap(scores, axis, bit)
                up = lax.ppermute(edges[0], "sp", [(i, i - 1) for i in range(1, sp_count)])
            else:
                down = lax.ppermute(edges[1], "sp", [(i, i + 1) for i in range(sp_count - 1)])
            after = edges[side], edges[side]
        elif event == "i":
            input_grad, token = pl.pallas_call(
                input_join_kernel,
                out_shape=(
                    jax.ShapeDtypeStruct((row_count, frame_count, clip_count, col_count, width), F32),
                    token_shape,
                ),
                in_specs=[SM, VM, VM, VM, VM, VM, ANY, ANY],
                out_specs=(VM, VM),
                scratch_shapes=[pltpu.VMEM((clip_count, 8, width), F32)],
                compiler_params=params(18),
                cost_estimate=takes(2),
                name="input_join",
            )(meta, col_info, dense[0], dense[1], down, up, after[0], scores)
            after = token, token
        elif event == "T":
            while left["t"]:
                after = step("t")
            own_half = chains["t"].state
            time_grad, class_weight_grad, token = pl.pallas_call(
                time_join_kernel,
                out_shape=(
                    jax.ShapeDtypeStruct((3 * middle, width), F32),
                    jax.ShapeDtypeStruct((classes, width), F32),
                    token_shape,
                ),
                in_specs=[SM] + [VM] * 5 + [ANY, ANY],
                out_specs=(VM, VM, VM),
                compiler_params=params(16),
                cost_estimate=takes(5),
                name="time_join",
            )(meta, own_half, trade(own_half, small_order, 0), gain_mid, shift_mid, mid_sums, *after)
            after = token, token
        elif event in "pq":
            name = "b" if event == "p" else "c"
            while left[name]:
                after = step(name)
            own_half = chains[name].state
            got_half = trade(own_half, order, 0)
            relay = got_half
            if event == "q":
                relay = pl.pallas_call(
                    relay_kernel,
                    out_shape=jax.ShapeDtypeStruct(got_half.shape, BF16),
                    in_specs=[VM, ANY, ANY],
                    out_specs=VM,
                    compiler_params=params(4),
                    cost_estimate=takes(1),
                    name="relay",
                )(got_half, *after)
            last[name] = [own_half, got_half, swap(own_half, "sp", 1), swap(relay, "sp", 1)]
            after = after[0], got_half
        else:
            name = "b" if event == "P" else "c"
            first_tap, taps = chunks[name]
            piece = pl.BlockSpec((1, 1152, 128), lambda n, meta: (n, 0, 0))
            before = [] if space_grad is None else [space_grad]
            space_grad, token = pl.pallas_call(
                functools.partial(join_kernel, steps),
                grid_spec=pltpu.PrefetchScalarGridSpec(
                    num_scalar_prefetch=1,
                    grid=(taps,),
                    in_specs=[piece] * 4 + [ANY] * (2 + len(before)),
                    out_specs=(
                        pl.BlockSpec((1, width, middle), lambda n, meta, tap=first_tap: (n + tap, 0, 0)),
                        pl.BlockSpec((8, 128), lambda n, meta: (0, 0)),
                    ),
                ),
                out_shape=(jax.ShapeDtypeStruct((9, width, middle), F32), token_shape),
                input_output_aliases={7: 0} if before else {},
                compiler_params=params(12),
                cost_estimate=takes(6),
                name="join",
            )(meta, *last[name], *after, *before)
            after = token, token
    space_grad = space_grad.reshape(3, 3, width, middle)
    input_grad = input_grad.transpose(2, 1, 0, 3, 4)
    time_grad = time_grad.reshape(3, middle, width)
    class_weight_grad = class_weight_grad.T
    logits = scores + class_bias
    return (
        logits,
        input_grad,
        space_grad,
        time_grad,
        gain_mid_grad,
        shift_mid_grad,
        gain_out_grad,
        shift_out_grad,
        class_weight_grad,
        class_bias_grad,
    )


def solution(mesh):
    placed = (
        P("dp", None, "sp", None, None),
        P(),
        P(),
        P(),
        P(),
        P(),
        P(),
        P(),
        P(),
        P("dp"),
        P("dp"),
        P("dp"),
        P("dp", None),
    )
    return jax.shard_map(
        shards,
        mesh=mesh,
        in_specs=placed,
        out_specs=(
            P("dp", None),
            P("dp", None, "sp", None, None),
            P(),
            P(),
            P(),
            P(),
            P(),
            P(),
            P(),
            P(),
        ),
        check_vma=False,
    )
```
